128 devices in a mesh: dp: 32 (over x, y, core), mp: 4 (over z).
Axes of the slice: x: 4, y: 4, z: 4, core: 2. Of those that a mesh axis runs over, the one named last changes fastest.
Arguments:
- columns: bfloat16 [4, 4096, 15360], P(None, 'dp', 'mp'), may hold values from -6 to 6
- lefts: bfloat16 [4, 4096, 1792], P(None, 'dp', 'mp'), may hold values from -6 to 6
- projs: bfloat16 [4, 1792, 256], P(None, 'mp'), may hold values from -0.125 to 0.125
- slot_table: int32 [4, 20], P('mp'), may hold values from 0 to 31, as said below
- refresh_group: int32 [4, 20], P('mp'), may hold values from 0 to 3
- left_stats: float32 [4, 32, 256, 256], P('mp', 'dp'), as said below
- right_stats: float32 [4, 32, 768, 768], P('mp', 'dp'), as said below
- left_roots: bfloat16 [4, 32, 256, 256], P('mp', 'dp')
- right_roots: bfloat16 [4, 32, 768, 768], P('mp', 'dp')
Outputs:
- new_left_stats: float32 [4, 32, 256, 256], P('mp', 'dp')
- new_right_stats: float32 [4, 32, 768, 768], P('mp', 'dp')
- new_left_roots: bfloat16 [4, 32, 256, 256], P('mp', 'dp')
- new_right_roots: bfloat16 [4, 32, 768, 768], P('mp', 'dp')
- update: bfloat16 [4, 256, 15360], P(None, None, 'mp')
The draws below stay inside these ranges and needn't reach their ends.
Inputs may be any that keep to these rules, and one draw needn't show every extreme that they name: `slot_table`: each row holds 20 distinct slots; slot s belongs to owner s // 1 of dp; slot 31 is named in every row, and in every row some owner holds 1 block. `left_stats`: symmetric positive definite. `right_stats`: symmetric positive definite.
All inputs are finite; a program needn't handle non-finite values.
Results may differ from the reference program's by a relative error of at most 0.0068.
Values may be sent and summed in bfloat16 or wider, within the bound.
A program may use at most 192 MiB of HBM per device.

```python
import math
import jax
import jax.numpy as jnp
from jax import lax

D = 1792
FF = 15360
RANK = 256
BW = 768
ADAPTERS = 4
ITERS = 3
NGROUP = 4
TOKENS = 4096
BPA = 5
BPC = 20
SLOTS = 32
N_MP = 4


def log_spread(key, full_shape, lower, upper):
    return jnp.exp(jax.random.uniform(key, full_shape, jnp.float32, jnp.log(lower), jnp.log(upper)))


def assemble(diagonal, noise_draw, spread):
    dimension = diagonal.shape[-1]
    identity = jnp.eye(dimension, dtype=jnp.float32)
    symmetric = (noise_draw + jnp.swapaxes(noise_draw, -1, -2)) * 0.70710678
    coupling = jnp.sqrt(diagonal[..., :, None] * diagonal[..., None, :]) * (spread / jnp.sqrt(dimension * 1.0))
    return diagonal[..., :, None] * identity + symmetric * coupling * (1.0 - identity)


def draw_slot_table(key, part):
    key = jax.random.fold_in(key, 11)
    row_keys = jax.random.split(key, N_MP)

    def draw_row(row_key):
        first_key, second_key = jax.random.split(row_key)
        others = jax.random.permutation(first_key, SLOTS - 1)[:BPC - 1]
        named = jnp.concatenate([others, jnp.array([SLOTS - 1], dtype=others.dtype)])
        return named[jax.random.permutation(second_key, BPC)]
    return jax.vmap(draw_row)(row_keys).astype(jnp.int32)


def draw_left_stats(key, part):
    key = jax.random.fold_in(key, 21)
    first_key, second_key = jax.random.split(key)
    full_shape = (N_MP, SLOTS, RANK, RANK)
    diagonal = log_spread(first_key, full_shape[:3], 200.0, 2000.0)
    noise_draw = jax.random.normal(second_key, full_shape, jnp.float32)
    return assemble(diagonal, noise_draw, 0.25)


def draw_right_stats(key, part):
    key = jax.random.fold_in(key, 22)
    first_key, second_key = jax.random.split(key)
    full_shape = (N_MP, SLOTS, BW, BW)
    diagonal = log_spread(first_key, full_shape[:3], 100.0, 1000.0)
    noise_draw = jax.random.normal(second_key, full_shape, jnp.float32)
    return assemble(diagonal, noise_draw, 0.25)


def draw_left_roots(key, part):
    key = jax.random.fold_in(key, 23)
    first_key, second_key = jax.random.split(key)
    full_shape = (N_MP, SLOTS, RANK, RANK)
    diagonal = log_spread(first_key, full_shape[:3], 0.1, 0.4)
    noise_draw = jax.random.normal(second_key, full_shape, jnp.float32)
    return assemble(diagonal, noise_draw, 0.25).astype(jnp.bfloat16)


def draw_right_roots(key, part):
    key = jax.random.fold_in(key, 24)
    first_key, second_key = jax.random.split(key)
    full_shape = (N_MP, SLOTS, BW, BW)
    diagonal = log_spread(first_key, full_shape[:3], 0.1, 0.4)
    noise_draw = jax.random.normal(second_key, full_shape, jnp.float32)
    return assemble(diagonal, noise_draw, 0.25).astype(jnp.bfloat16)


def set_ends(result, rng, low, top_value):
    longest = result.shape.index(max(result.shape))
    spots = []
    for shift in (0, 1):
        where = [jax.random.randint(jax.random.fold_in(rng, axis), (), 0, length) for axis, length in enumerate(result.shape)]
        where[longest] = (where[longest] + shift) % result.shape[longest]
        spots.append(tuple(where))
    return result.at[spots[0]].set(low).at[spots[1]].set(top_value)


def level_of(stream_key, shape, pieces, least, high):
    loudness = 1.0
    for position, shards_of in pieces:
        draws = jax.random.uniform(jax.random.fold_in(jax.random.fold_in(stream_key, 6), position), (shards_of,), jnp.float32, least / len(pieces), high / len(pieces))
        loudness = loudness * jnp.repeat(jnp.exp(draws), shape[position] // shards_of).reshape((-1,) + (1,) * (len(shape) - 1 - position))
    return loudness


def gaussian(own_key, extent, scale, bound, cuts=(), kind=jnp.bfloat16):
    result = scale * jax.random.normal(own_key, extent, jnp.float32)
    if cuts:
        result = result * level_of(own_key, extent, cuts, -0.22, 0.18)
    return jnp.clip(result, -bound, bound).astype(kind)


def setup_inputs(seed: int = 0) -> dict:
    seeds = jax.random.split(jax.random.key(seed), 10)
    return {
        "columns": gaussian(seeds[0], (ADAPTERS, TOKENS, FF), 1.0, 6.0, ((1, 32), (2, 4))),
        "lefts": gaussian(seeds[1], (ADAPTERS, TOKENS, D), 1.0, 6.0, ((1, 32), (2, 4))),
        "projs": gaussian(seeds[2], (ADAPTERS, D, RANK), D ** -0.5, 0.125, ((1, 4),)),
        "slot_table": draw_slot_table(jax.random.fold_in(seeds[9], 71), 0),
        "refresh_group": set_ends(jax.random.randint(seeds[4], (N_MP, BPC), 0, NGROUP), jax.random.fold_in(seeds[4], 1), 0, NGROUP - 1).astype(jnp.int32),
        "left_stats": draw_left_stats(jax.random.fold_in(seeds[9], 71), 0),
        "right_stats": draw_right_stats(jax.random.fold_in(seeds[9], 71), 0),
        "left_roots": draw_left_roots(jax.random.fold_in(seeds[9], 71), 0),
        "right_roots": draw_right_roots(jax.random.fold_in(seeds[9], 71), 0),
    }


EPSILON = 1e-06

def newton_root(matrix):
    highest = lax.Precision.HIGHEST
    dimension = matrix.shape[-1]
    identity = jnp.eye(dimension, dtype=matrix.dtype)
    frob_norm = jnp.sqrt(jnp.sum(matrix * matrix) + EPSILON)
    current = identity * frob_norm ** (-0.25)
    scaled = matrix / frob_norm
    for _ in range(ITERS):
        factor = (5.0 * identity - scaled) * 0.25
        current = jnp.dot(current, factor, precision=highest)
        square = jnp.dot(factor, factor, precision=highest)
        scaled = jnp.dot(jnp.dot(square, square, precision=highest), scaled, precision=highest)
    return current

def reference(columns, lefts, projs, slot_table, refresh_group, left_stats, right_stats, left_roots, right_roots):
    highest = lax.Precision.HIGHEST
    factors = jnp.einsum('atd,adr->atr', lefts.astype(jnp.float32), projs.astype(jnp.float32)).astype(jnp.bfloat16)
    gradients = jnp.einsum('atr,atf->arf', factors.astype(jnp.float32), columns.astype(jnp.float32)) / math.sqrt(TOKENS)
    blocks = gradients.reshape(ADAPTERS, RANK, N_MP, BPA, BW).transpose(2, 0, 3, 1, 4).reshape(N_MP, BPC, RANK, BW)
    slot_ids = jnp.arange(SLOTS, dtype=jnp.int32)
    naming = slot_table[:, None, :] == slot_ids[None, :, None]
    occupied = jnp.any(naming, axis=2)
    block_ids = jnp.arange(BPC, dtype=jnp.int32)
    block_of = lax.optimization_barrier(jnp.sum(jnp.where(naming, block_ids[None, None, :], 0), axis=2)).astype(jnp.int32)
    picked = jax.vmap(lambda source, index: jnp.take(source, index, axis=0))(blocks, block_of)
    slot_grad = picked * occupied[:, :, None, None].astype(gradients.dtype)
    group_of = jax.vmap(lambda source, index: jnp.take(source, index, axis=0))(refresh_group, block_of)
    renew = jnp.logical_and(occupied, group_of == 0)
    new_left = 0.9 * left_stats + 0.1 * jnp.einsum('msrw,msqw->msrq', slot_grad, slot_grad, precision=highest)
    new_right = 0.9 * right_stats + 0.1 * jnp.einsum('msrw,msrv->mswv', slot_grad, slot_grad, precision=highest)

    def refresh_one(slot_items):
        renew_flag, left_stat, right_stat, left_root, right_root = slot_items
        return lax.cond(renew_flag, lambda: (newton_root(left_stat).astype(jnp.bfloat16), newton_root(right_stat).astype(jnp.bfloat16)), lambda: (left_root, right_root))
    flat_items = (renew.reshape(-1), new_left.reshape(-1, RANK, RANK), new_right.reshape(-1, BW, BW), left_roots.reshape(-1, RANK, RANK), right_roots.reshape(-1, BW, BW))
    root_left, root_right = lax.map(refresh_one, flat_items)
    root_left = root_left.reshape(N_MP, SLOTS, RANK, RANK)
    root_right = root_right.reshape(N_MP, SLOTS, BW, BW)
    grad_half = slot_grad.astype(jnp.bfloat16)
    half_product = jnp.einsum('msrq,msqw->msrw', root_left.astype(jnp.float32), grad_half.astype(jnp.float32)).astype(jnp.bfloat16)
    direction = jnp.einsum('msrw,mswv->msrv', half_product.astype(jnp.float32), root_right.astype(jnp.float32))
    graft_ratio = jnp.sqrt((lax.optimization_barrier(jnp.mean(slot_grad * slot_grad, axis=(2, 3))) + EPSILON) / (lax.optimization_barrier(jnp.mean(direction * direction, axis=(2, 3))) + EPSILON))
    slot_update = (direction * graft_ratio[:, :, None, None]).astype(jnp.bfloat16)
    placed_back = jax.vmap(lambda source, index: jnp.take(source, index, axis=0))(slot_update, slot_table)
    update = placed_back.reshape(N_MP, ADAPTERS, BPA, RANK, BW).transpose(1, 3, 0, 2, 4).reshape(ADAPTERS, RANK, FF)
    return (new_left, new_right, root_left, root_right, update)
```

```python
import functools
import math

import jax
import jax.numpy as jnp
from jax import lax
from jax.experimental import pallas as pl
from jax.experimental.pallas import tpu as pltpu
from jax.sharding import PartitionSpec as P

BW = 768
EPSILON = 1e-06
NX, NY, NC, NZ = 4, 4, 2, 4
SIDE = 4
ORDER = (0, 1, 3, 2)
MESH = pl.DeviceIdType.MESH
F32, BF16 = jnp.float32, jnp.bfloat16


def coords():
    dp = lax.axis_index("dp")
    return dp // (NY * NC), (dp // NC) % NY, dp % NC, lax.axis_index("mp")


def at(x, y, c):
    return {"dp": (x * NY + y) * NC + c}


def along(axis, step, x, y, c):
    return at((x + step) % NX, y, c) if axis == 0 else at(x, (y + step) % NY, c)


def remote(src, dst, send, recv, device):
    return pltpu.make_async_remote_copy(
        src_ref=src, dst_ref=dst, send_sem=send, recv_sem=recv, device_id=device, device_id_type=MESH
    )


def plane_partners(x, y, c):
    partners = [at(x, y, 1 - c)]
    for step in range(1, SIDE):
        for core in range(NC):
            partners.append(at((x + step) % NX, y, (c + core) % NC))
            partners.append(at(x, (y + step) % NY, (c + core) % NC))
    return partners


def greet(partners):
    barrier = pltpu.get_barrier_semaphore()
    for partner in partners:
        pl.semaphore_signal(barrier, inc=1, device_id=partner, device_id_type=MESH)
    pl.semaphore_wait(barrier, len(partners))


class RingSum:
    def __init__(self, axis, pos, place, src, far, near, send, recv, rows):
        self.axis, self.pos, self.place = axis, pos, place
        self.src, self.far, self.near, self.send, self.recv = src, far, near, send, recv
        self.half = rows // 2
        self.started = []

    def q(self, step):
        return (self.pos + step) % SIDE

    def halves(self, part):
        return pl.ds(part * self.half, self.half)

    def copy(self, message, items):
        right, left = along(self.axis, 1, *self.place), along(self.axis, SIDE - 1, *self.place)
        first, second = self.halves(0), self.halves(1)
        src, dst, device = (
            (self.src.at[self.q(2), items, first], self.far.at[0, items], right),
            (self.src.at[self.q(2), items, second], self.far.at[1, items], left),
            (self.src.at[self.q(1), items, second], self.near.at[0, items, second], right),
            (self.src.at[self.q(3), items, first], self.near.at[1, items, first], left),
            (self.src.at[self.q(1), items, first], self.near.at[0, items, first], right),
            (self.src.at[self.q(3), items, second], self.near.at[1, items, second], left),
        )[message]
        return src, dst, device

    def start(self, message, items, index):
        src, dst, device = self.copy(message, items)
        descriptor = remote(src, dst, self.send.at[index, message], self.recv.at[index, message], device)
        descriptor.start()
        self.started.append(descriptor)

    def wait(self, message, items, index):
        _, dst, device = self.copy(message, items)
        remote(dst, dst, self.send.at[index, message], self.recv.at[index, message], device).wait_recv()

    def first(self, items, index):
        for message in (0, 1, 2, 3):
            self.start(message, items, index)

    def second(self, items, index):
        for message, step, part in ((0, 1, 0), (1, 3, 1)):
            self.wait(message, items, index)
            rows = self.halves(part)
            total = self.src[self.q(step), items, rows].astype(F32) + self.far[message, items].astype(F32)
            self.src[self.q(step), items, rows] = total.astype(BF16)
            self.start(message + 4, items, index)

    def total(self, items, index):
        for message in (2, 3, 4, 5):
            self.wait(message, items, index)
        own = self.src[self.pos, items].astype(F32)
        return own + self.near[0, items].astype(F32) + self.near[1, items].astype(F32)

    def finish(self):
        for descriptor in self.started:
            descriptor.wait_send()


class RingGather:
    def __init__(self, axis, pos, place, buf, send, recv, rows):
        self.axis, self.pos, self.place = axis, pos, place
        self.buf, self.send, self.recv = buf, send, recv
        self.half = rows // 2
        self.started = []

    def q(self, step):
        return (self.pos + step) % SIDE

    def view(self, step, items, part):
        return self.buf.at[self.q(step), items, pl.ds(part * self.half, self.half)]

    PLAN = ((0, 0, 3, 1), (1, 0, 1, 3), (1, 0, 3, 1), (0, 0, 1, 3), (0, 3, 2, 1), (1, 1, 2, 3))

    def start(self, message, items, index):
        part, here, _, direction = self.PLAN[message]
        view = self.view(here, items, part)
        device = along(self.axis, direction, *self.place)
        descriptor = remote(view, view, self.send.at[index, message], self.recv.at[index, message], device)
        descriptor.start()
        self.started.append(descriptor)

    def wait(self, message, items, index):
        part, _, there, direction = self.PLAN[message]
        view = self.view(there, items, part)
        device = along(self.axis, direction, *self.place)
        remote(view, view, self.send.at[index, message], self.recv.at[index, message], device).wait_recv()

    def first(self, items, index):
        for message in (0, 1, 2, 3):
            self.start(message, items, index)

    def second(self, items, index):
        for message in (0, 1):
            self.wait(message, items, index)
            self.start(message + 4, items, index)

    def finish(self):
        for descriptor in self.started:
            descriptor.wait_send()


def reduce_kernel(
    scale, columns, lefts, projs, table, grad_out,
    cols, part, part_in, factors, blocks, far1, near1, summed, slots, far2, near2, pieces, grad, block_of,
    col_sem, sib_send, sib_recv, part_send, part_recv, fac_send, fac_recv, swap_send, swap_recv,
    send1, recv1, send2, recv2, send3, recv3, own_sem,
):
    adapters, tokens, width = columns.shape
    rank = projs.shape[2]
    per_adapter = width // BW
    half = BW // NC
    group = rank // (2 * SIDE)
    slot_count = NX * NY * NC
    x, y, c, z = coords()
    sibling = at(x, y, 1 - c)
    mine, theirs = pl.ds(pl.multiple_of(c * tokens, tokens), tokens), pl.ds(pl.multiple_of((1 - c) * tokens, tokens), tokens)
    greet(plane_partners(x, y, c) + [{"mp": (z + step) % NZ} for step in range(1, NZ)])
    sends = []

    local, swapped = [], []
    for j in range(per_adapter):
        lanes = pl.ds(pl.multiple_of(j * BW + (1 - c) * half, half), half)
        swap = remote(columns.at[:, :, lanes], cols.at[j, :, mine], sib_send.at[j], sib_recv.at[j], sibling)
        swap.start()
        sends.append(swap)
        swapped.append(remote(cols.at[j, :, theirs], cols.at[j, :, theirs], sib_send.at[j], sib_recv.at[j], sibling))
    for j in range(per_adapter):
        lanes = pl.ds(pl.multiple_of(j * BW + c * half, half), half)
        keep = pltpu.make_async_copy(columns.at[:, :, lanes], cols.at[j, :, mine], col_sem.at[j])
        keep.start()
        local.append(keep)

    def partial(a):
        return jnp.dot(lefts[a], projs[a], preferred_element_type=F32)

    for step in (2, 1, 3):
        part[step - 1] = partial((z + step) % NZ)
        copy = remote(
            part.at[step - 1], part_in.at[step - 1], part_send.at[step - 1], part_recv.at[step - 1],
            {"mp": (z + step) % NZ},
        )
        copy.start()
        sends.append(copy)
    total = partial(z)
    for step in (1, 3, 2):
        remote(
            part_in.at[step - 1], part_in.at[step - 1], part_send.at[step - 1], part_recv.at[step - 1], sibling
        ).wait_recv()
        total += part_in[step - 1]
    factors[z, mine] = total.astype(BF16)
    for step in (2, 1, 3):
        view = factors.at[z, mine]
        copy = remote(view, view, fac_send.at[step - 1], fac_recv.at[step - 1], {"mp": (z + step) % NZ})
        copy.start()
        sends.append(copy)

    place = (x, y, c)
    ring1 = [
        RingSum(o, place[o], place, blocks.at[o], far1.at[o], near1.at[o], send1.at[o], recv1.at[o], group)
        for o in range(2)
    ]
    items = []
    for t, step in enumerate(ORDER):
        a = (z + step) % NZ
        view = factors.at[a, mine]
        if step:
            back = NZ - step
            remote(view, view, fac_send.at[back - 1], fac_recv.at[back - 1], sibling).wait_recv()
        swap = remote(view, view, swap_send.at[t], swap_recv.at[t], sibling)
        swap.start()
        sends.append(swap)
        other = factors.at[a, theirs]
        remote(other, other, swap_send.at[t], swap_recv.at[t], sibling).wait_recv()
        if t == 0:
            for j in range(per_adapter):
                local[j].wait()
                swapped[j].wait_recv()
        factor = factors[a]

        def block(j, carry):
            product = lax.dot_general(
                factor, cols[j, a], (((0,), (0,)), ((), ())), preferred_element_type=F32
            ).astype(BF16)
            for o in range(2):
                for q in range(SIDE):
                    low = (o * SIDE + q) * group
                    blocks[o, q, a * per_adapter + j] = product[low : low + group]
            return carry

        lax.fori_loop(0, per_adapter, block, 0)
        items.append(pl.ds(a * per_adapter, per_adapter))
        for o in range(2):
            ring1[o].first(items[t], t)

    empty = adapters * per_adapter

    def find(s, carry):
        found = jnp.int32(empty)
        for k in range(adapters * per_adapter):
            found = jnp.where(table[0, k] == s, jnp.int32(k), found)
        block_of[s] = found
        return carry

    lax.fori_loop(0, slot_count, find, 0)

    for t in range(adapters):
        for o in range(2):
            ring1[o].second(items[t], t)
    for o in range(2):
        summed[o, empty] = jnp.zeros(summed.shape[2:], BF16)
    for t in range(adapters):
        for o in range(2):
            summed[o, items[t]] = ring1[o].total(items[t], t).astype(BF16)

    every = pl.ds(0, SIDE * NC)
    ring2 = [
        RingSum(1 - o, place[1 - o], place, slots.at[o], far2.at[o], near2.at[o], send2.at[o], recv2.at[o], group)
        for o in range(2)
    ]
    for step in (2, 1, 3, 0):
        for o in range(2):
            dest = ring2[o].q(step)

            def fill(j, carry, o=o, dest=dest):
                s = (j // NC) * (NY * NC) + dest * NC + j % NC if o == 0 else dest * (NY * NC) + j
                slots[o, dest, j] = summed[o, block_of[s]]
                return carry

            lax.fori_loop(0, SIDE * NC, fill, 0)
            if step == 2:
                ring2[o].start(0, every, 0)
                ring2[o].start(1, every, 0)
            if step == 1:
                ring2[o].start(2, every, 0)
            if step == 3:
                ring2[o].start(3, every, 0)
    for o in range(2):
        ring2[o].second(every, 0)

    def target(o, step, core):
        return at((x + step) % NX, y, (c + core) % NC) if o == 0 else at(x, (y + step) % NY, (c + core) % NC)

    def spot(o, step, core):
        q, lane = (place[o] + step) % SIDE, (c + core) % NC
        return grad.at[
            pl.ds(pl.multiple_of((o * SIDE + q) * group, group), group), pl.ds(pl.multiple_of(lane * half, half), half)
        ]

    owned = []
    for o in range(2):
        pieces[o] = (ring2[o].total(every, 0) * scale).astype(BF16)
        for step in (2, 1, 3, 0):
            for core in range(NC):
                source = pieces.at[o, ((place[o] + step) % SIDE) * NC + (c + core) % NC]
                if step == 0 and core == 0:
                    copy = pltpu.make_async_copy(source, spot(o, 0, 0), own_sem.at[o])
                    copy.start()
                    owned.append(copy)
                else:
                    index = step * NC + core
                    copy = remote(source, spot(o, 0, 0), send3.at[o, index], recv3.at[o, index], target(o, step, core))
                    copy.start()
                    sends.append(copy)
    for o in range(2):
        for step in range(SIDE):
            for core in range(NC):
                if step or core:
                    index = step * NC + core
                    view = spot(o, SIDE - step, NC - core)
                    remote(view, view, send3.at[o, index], recv3.at[o, index], sibling).wait_recv()
    for copy in owned:
        copy.wait()
    grad_out[...] = grad[...]
    for copy in sends:
        copy.wait_send()
    for ring in ring1 + ring2:
        ring.finish()


def summed_gradient(columns, lefts, projs, table, scale):
    adapters, tokens, width = columns.shape
    rank = projs.shape[2]
    per_adapter = width // BW
    count = adapters * per_adapter
    half, group, pair = BW // NC, rank // (2 * SIDE), SIDE * NC
    dma = pltpu.SemaphoreType.DMA
    return pl.pallas_call(
        functools.partial(reduce_kernel, scale),
        out_shape=jax.ShapeDtypeStruct((rank, BW), BF16),
        in_specs=[
            pl.BlockSpec(memory_space=pl.ANY),
            pl.BlockSpec(memory_space=pltpu.VMEM),
            pl.BlockSpec(memory_space=pltpu.VMEM),
            pl.BlockSpec(memory_space=pltpu.SMEM),
        ],
        out_specs=pl.BlockSpec(memory_space=pltpu.VMEM),
        scratch_shapes=[
            pltpu.VMEM((per_adapter, adapters, NC * tokens, half), BF16),
            pltpu.VMEM((NZ - 1, tokens, rank), F32),
            pltpu.VMEM((NZ - 1, tokens, rank), F32),
            pltpu.VMEM((adapters, NC * tokens, rank), BF16),
            pltpu.VMEM((2, SIDE, count, group, half), BF16),
            pltpu.VMEM((2, 2, count, group // 2, half), BF16),
            pltpu.VMEM((2, 2, count, group, half), BF16),
            pltpu.VMEM((2, count + 1, group, half), BF16),
            pltpu.VMEM((2, SIDE, pair, group, half), BF16),
            pltpu.VMEM((2, 2, pair, group // 2, half), BF16),
            pltpu.VMEM((2, 2, pair, group, half), BF16),
            pltpu.VMEM((2, pair, group, half), BF16),
            pltpu.VMEM((rank, BW), BF16),
            pltpu.SMEM((NX * NY * NC,), jnp.int32),
            dma((per_adapter,)),
            dma((per_adapter,)),
            dma((per_adapter,)),
            dma((NZ - 1,)),
            dma((NZ - 1,)),
            dma((NZ - 1,)),
            dma((NZ - 1,)),
            dma((adapters,)),
            dma((adapters,)),
            dma((2, adapters, 6)),
            dma((2, adapters, 6)),
            dma((2, 1, 6)),
            dma((2, 1, 6)),
            dma((2, pair)),
            dma((2, pair)),
            dma((2,)),
        ],
        compiler_params=pltpu.CompilerParams(
            collective_id=0, has_side_effects=True, vmem_limit_bytes=48 * 2**20
        ),
        name="summed_gradient",
    )(columns, lefts, projs, table)


def newton_polynomial():
    terms = [0.25 * math.comb(5, i) * 1.25 ** (5 - i) * (-0.25) ** i for i in range(6)]
    terms[0] += 1.25 * 0.25
    return terms


def dot16(a, b):
    return jnp.dot(a, b, preferred_element_type=F32)


def root_into(stat, out, n1, n2, n3, u, v, w):
    size = stat.shape[0]
    width = min(size, 256)
    tiles = [pl.ds(low, width) for low in range(0, size, width)]
    square = jnp.zeros((1, width), F32)
    for tile in tiles:
        value = stat[:, tile]
        square += jnp.sum(value * value, axis=0, keepdims=True)
    norm = jnp.sqrt(jnp.sum(square) + EPSILON)
    inverse = 1.0 / norm
    u1, u2, u3, u4, u5, u6 = newton_polynomial()
    for tile in tiles:
        n1[:, tile] = (stat[:, tile] * inverse).astype(BF16)
    for tile in tiles:
        n2[:, tile] = dot16(n1[...], n1[:, tile]).astype(BF16)
    for tile in tiles:
        value = dot16(n1[...], n2[:, tile])
        n3[:, tile] = value.astype(BF16)
        second, first = n2[:, tile].astype(F32), n1[:, tile].astype(F32)
        v[:, tile] = (u4 * first + u5 * second + u6 * value).astype(BF16)
        u[:, tile] = (u1 * first + u2 * second + u3 * value).astype(BF16)
    for tile in tiles:
        w[:, tile] = (u[:, tile].astype(F32) + dot16(n3[...], v[:, tile])).astype(BF16)
    for tile in tiles:
        value = w[:, tile]
        n2[:, tile] = (dot16(w[...], value) - 3.125 * value.astype(F32)).astype(BF16)
        n3[:, tile] = (1.5625 * n1[:, tile].astype(F32) - dot16(w[...], n1[:, tile])).astype(BF16)
    for tile in tiles:
        value = n2[:, tile]
        v[:, tile] = (dot16(n2[...], value) + (2 * 1.5625**2) * value.astype(F32)).astype(BF16)
    scale = jnp.sqrt(jnp.sqrt(inverse))
    for low, tile in zip(range(0, size, width), tiles):
        value = n3[:, tile]
        last = 1.25 * w[:, tile].astype(F32) + (0.25 * 1.5625**4) * value.astype(F32) + 0.25 * dot16(v[...], value)
        row = lax.broadcasted_iota(jnp.int32, (size, width), 0)
        column = lax.broadcasted_iota(jnp.int32, (size, width), 1)
        eye = jnp.where(row == column + low, jnp.float32(1.25 * 1.5625), jnp.float32(0.0))
        out[:, tile] = ((eye - last) * scale).astype(BF16)


def root_kernel(
    table, groups, grad, left_stat, right_stat, left_root, right_root,
    new_left, new_right, root_left, root_right, update,
    *scratch,
):
    rank, width = grad.shape
    value = grad[...]
    transposed = (((0,), (0,)), ((), ()))
    across = (((1,), (1,)), ((), ()))
    new_left[0, 0] = 0.9 * left_stat[0, 0] + 0.1 * lax.dot_general(value, value, across, preferred_element_type=F32)
    tile_width = min(width, 256)
    for low in range(0, width, tile_width):
        tile = pl.ds(low, tile_width)
        new_right[0, 0, :, tile] = 0.9 * right_stat[0, 0, :, tile] + 0.1 * lax.dot_general(
            value, grad[:, tile], transposed, preferred_element_type=F32
        )
    owner = lax.axis_index("dp")
    renew = jnp.bool_(False)
    for k in range(table.shape[1]):
        renew = jnp.logical_or(renew, jnp.logical_and(table[0, k] == owner, groups[0, k] == 0))

    @pl.when(renew)
    def _():
        root_into(new_left.at[0, 0], root_left.at[0, 0], *scratch[:6])
        root_into(new_right.at[0, 0], root_right.at[0, 0], *scratch[6:])

    @pl.when(jnp.logical_not(renew))
    def _():
        root_left[...] = left_root[...]
        root_right[...] = right_root[...]

    half_product = dot16(root_left[0, 0], value).astype(BF16)
    direction = dot16(half_product, root_right[0, 0])
    wide = value.astype(F32)
    count = 1.0 / (rank * width)
    ratio = (jnp.sum(wide * wide) * count + EPSILON) / (jnp.sum(direction * direction) * count + EPSILON)
    update[...] = (direction * jnp.sqrt(ratio)).astype(BF16)


def preconditioned(table, groups, grad, left_stats, right_stats, left_roots, right_roots):
    rank, width = grad.shape
    vmem, smem = pl.BlockSpec(memory_space=pltpu.VMEM), pl.BlockSpec(memory_space=pltpu.SMEM)
    like = lambda a, kind: jax.ShapeDtypeStruct(a.shape, kind)
    return pl.pallas_call(
        root_kernel,
        out_shape=(
            like(left_stats, F32), like(right_stats, F32), like(left_roots, BF16), like(right_roots, BF16),
            jax.ShapeDtypeStruct((rank, width), BF16),
        ),
        in_specs=[smem] * 2 + [vmem] * 5,
        out_specs=(vmem,) * 5,
        scratch_shapes=[pltpu.VMEM((rank, rank), BF16)] * 6 + [pltpu.VMEM((width, width), BF16)] * 6,
        compiler_params=pltpu.CompilerParams(vmem_limit_bytes=48 * 2**20),
        name="preconditioned",
    )(table, groups, grad, left_stats, right_stats, left_roots, right_roots)


def gather_kernel(table, update, out, by_slot, by_block, send1, recv1, send2, recv2, send3, recv3, swap_send, swap_recv, own_sem, out_sem):
    rank, width = update.shape
    half, group, pair = width // NC, rank // (2 * SIDE), SIDE * NC
    rows_of, adapters = out.shape[3], out.shape[4]
    x, y, c, _ = coords()
    place = (x, y, c)
    sibling = at(x, y, 1 - c)
    greet(plane_partners(x, y, c))
    sends = []

    def spot(o, step, core):
        return by_slot.at[o, place[1 - o], ((place[o] + step) % SIDE) * NC + (c + core) % NC]

    owned = []
    for step in (2, 1, 3, 0):
        for o in range(2):
            for core in range(NC):
                q, lane = (place[o] + step) % SIDE, (c + core) % NC
                source = update.at[
                    pl.ds(pl.multiple_of((o * SIDE + q) * group, group), group),
                    pl.ds(pl.multiple_of(lane * half, half), half),
                ]
                if step == 0 and core == 0:
                    copy = pltpu.make_async_copy(source, spot(o, 0, 0), own_sem.at[o])
                    copy.start()
                    owned.append(copy)
                else:
                    index = step * NC + core
                    device = at(q, y, lane) if o == 0 else at(x, q, lane)
                    copy = remote(source, spot(o, 0, 0), send1.at[o, index], recv1.at[o, index], device)
                    copy.start()
                    sends.append(copy)

    every = pl.ds(0, pair)
    ring2 = [
        RingGather(1 - o, place[1 - o], place, by_slot.at[o], send2.at[o], recv2.at[o], group) for o in range(2)
    ]
    for o in range(2):
        owned[o].wait()
        for step in range(SIDE):
            for core in range(NC):
                if step or core:
                    index = step * NC + core
                    view = spot(o, SIDE - step, NC - core)
                    remote(view, view, send1.at[o, index], recv1.at[o, index], sibling).wait_recv()
        ring2[o].first(every, 0)
    for o in range(2):
        ring2[o].second(every, 0)
    for o in range(2):
        for message in (2, 3, 4, 5):
            ring2[o].wait(message, every, 0)

    ring1 = [
        RingGather(o, place[o], place, by_block.at[o, :, c], send1_, recv1_, group)
        for o, (send1_, recv1_) in enumerate(((send3.at[0], recv3.at[0]), (send3.at[1], recv3.at[1])))
    ]
    everyone = pl.ds(0, adapters)

    def pass_on(o, step, j):
        view = by_block.at[o, (place[o] + step) % SIDE, c, j]
        copy = remote(view, view, swap_send.at[o, step, j], swap_recv.at[o, step, j], sibling)
        copy.start()
        sends.append(copy)

    return_items = []
    for j in range(rows_of):
        for o in range(2):

            def fill(a, carry, o=o, j=j):
                s = table[0, a * rows_of + j]
                if o == 0:
                    row, item = (s // NC) % NY, (s // (NY * NC)) * NC + s % NC
                else:
                    row, item = s // (NY * NC), s % (NY * NC)
                by_block[o, place[o], c, j, a] = by_slot[o, row, item]
                return carry

            lax.fori_loop(0, adapters, fill, 0)
            ring1[o].buf = by_block.at[o, :, c, j]
            ring1[o].first(everyone, j)
            pass_on(o, 0, j)
    for j in range(rows_of):
        for o in range(2):
            ring1[o].buf = by_block.at[o, :, c, j]
            ring1[o].second(everyone, j)
    for j in range(rows_of):
        for o in range(2):
            ring1[o].buf = by_block.at[o, :, c, j]
            ring1[o].wait(2, everyone, j)
            pass_on(o, 3, j)
            ring1[o].wait(3, everyone, j)
            pass_on(o, 1, j)
    for j in range(rows_of):
        for o in range(2):
            ring1[o].buf = by_block.at[o, :, c, j]
            ring1[o].wait(4, everyone, j)
            ring1[o].wait(5, everyone, j)
            pass_on(o, 2, j)
    for o in range(2):
        for step in range(SIDE):
            for j in range(rows_of):
                view = by_block.at[o, (place[o] + step) % SIDE, 1 - c, j]
                remote(view, view, swap_send.at[o, step, j], swap_recv.at[o, step, j], sibling).wait_recv()
    for copy in sends:
        copy.wait_send()
    for ring in ring1 + ring2:
        ring.finish()
    copy = pltpu.make_async_copy(by_block, out, out_sem.at[0])
    copy.start()
    copy.wait()


def gathered(table, update, adapters):
    rank, width = update.shape
    half, group, pair = width // NC, rank // (2 * SIDE), SIDE * NC
    per_adapter = table.shape[1] // adapters
    shape = (2, SIDE, NC, per_adapter, adapters, group, half)
    dma = pltpu.SemaphoreType.DMA
    return pl.pallas_call(
        gather_kernel,
        out_shape=jax.ShapeDtypeStruct(shape, BF16),
        in_specs=[pl.BlockSpec(memory_space=pltpu.SMEM), pl.BlockSpec(memory_space=pltpu.VMEM)],
        out_specs=pl.BlockSpec(memory_space=pl.ANY),
        scratch_shapes=[
            pltpu.VMEM((2, SIDE, pair, group, half), BF16),
            pltpu.VMEM(shape, BF16),
            dma((2, pair)),
            dma((2, pair)),
            dma((2, 1, 6)),
            dma((2, 1, 6)),
            dma((2, per_adapter, 6)),
            dma((2, per_adapter, 6)),
            dma((2, SIDE, per_adapter)),
            dma((2, SIDE, per_adapter)),
            dma((2,)),
            dma((1,)),
        ],
        compiler_params=pltpu.CompilerParams(
            collective_id=1, has_side_effects=True, vmem_limit_bytes=48 * 2**20
        ),
        name="gathered",
    )(table, update)


def place_kernel(parts, out, sem):
    group, half = parts.shape[5:]
    copies = []
    for o in range(2):
        for q in range(SIDE):
            for c in range(NC):
                for j in range(parts.shape[3]):
                    copies.append(
                        pltpu.make_async_copy(
                            parts.at[o, q, c, j],
                            out.at[:, pl.ds((o * SIDE + q) * group, group), pl.ds(j * BW + c * half, half)],
                            sem.at[len(copies)],
                        )
                    )
    for copy in copies:
        copy.start()
    for copy in copies:
        copy.wait()


def placed_blocks(parts):
    _, _, _, per_adapter, adapters, group, _ = parts.shape
    return pl.pallas_call(
        place_kernel,
        out_shape=jax.ShapeDtypeStruct((adapters, 2 * SIDE * group, per_adapter * BW), BF16),
        in_specs=[pl.BlockSpec(memory_space=pl.ANY)],
        out_specs=pl.BlockSpec(memory_space=pl.ANY),
        scratch_shapes=[pltpu.SemaphoreType.DMA((2 * SIDE * NC * per_adapter,))],
        name="placed_blocks",
    )(parts)


def body(
    columns,
    lefts,
    projs,
    slot_table,
    refresh_group,
    left_stats,
    right_stats,
    left_roots,
    right_roots,
):
    total_tokens = lax.axis_size("dp") * columns.shape[1]
    grad = summed_gradient(columns, lefts, projs, slot_table, 1.0 / math.sqrt(total_tokens))
    new_left, new_right, root_left, root_right, update = preconditioned(
        slot_table, refresh_group, grad, left_stats, right_stats, left_roots, right_roots
    )
    parts = gathered(slot_table, update, columns.shape[0])
    return new_left, new_right, root_left, root_right, placed_blocks(parts)


def solution(mesh):
    placed = (
        P(None, "dp", "mp"),
        P(None, "dp", "mp"),
        P(None, "mp", None),
        P("mp", None),
        P("mp", None),
        P("mp", "dp", None, None),
        P("mp", "dp", None, None),
        P("mp", "dp", None, None),
        P("mp", "dp", None, None),
    )
    return jax.shard_map(
        body,
        mesh=mesh,
        in_specs=placed,
        out_specs=(
            P("mp", "dp", None, None),
            P("mp", "dp", None, None),
            P("mp", "dp", None, None),
            P("mp", "dp", None, None),
            P(None, None, "mp"),
        ),
        check_vma=False,
    )
```

```python
import functools
import math

import jax
import jax.numpy as jnp
from jax import lax
from jax.experimental import pallas as pl
from jax.experimental.pallas import tpu as pltpu
from jax.sharding import PartitionSpec as P

BW = 768
EPSILON = 1e-06
NX, NY, NC, NZ = 4, 4, 2, 4
SIDE = 4
ORDER = (0, 1, 3, 2)
MESH = pl.DeviceIdType.MESH
F32, BF16 = jnp.float32, jnp.bfloat16


def coords():
    dp = lax.axis_index("dp")
    return dp // (NY * NC), (dp // NC) % NY, dp % NC, lax.axis_index("mp")


def at(x, y, c):
    return {"dp": (x * NY + y) * NC + c}


def along(axis, step, x, y, c):
    return at((x + step) % NX, y, c) if axis == 0 else at(x, (y + step) % NY, c)


def remote(src, dst, send, recv, device):
    return pltpu.make_async_remote_copy(
        src_ref=src, dst_ref=dst, send_sem=send, recv_sem=recv, device_id=device, device_id_type=MESH
    )


def plane_partners(x, y, c):
    partners = [at(x, y, 1 - c)]
    for step in range(1, SIDE):
        for core in range(NC):
            partners.append(at((x + step) % NX, y, (c + core) % NC))
            partners.append(at(x, (y + step) % NY, (c + core) % NC))
    return partners


def greet(partners):
    barrier = pltpu.get_barrier_semaphore()
    for partner in partners:
        pl.semaphore_signal(barrier, inc=1, device_id=partner, device_id_type=MESH)


def await_partners(partners):
    pl.semaphore_wait(pltpu.get_barrier_semaphore(), len(partners))


class RingSum:
    def __init__(self, axis, pos, place, src, far, near, send, recv, rows):
        self.axis, self.pos, self.place = axis, pos, place
        self.src, self.far, self.near, self.send, self.recv = src, far, near, send, recv
        self.half = rows // 2
        self.started = []

    def q(self, step):
        return (self.pos + step) % SIDE

    def halves(self, part):
        return pl.ds(part * self.half, self.half)

    def copy(self, message, items):
        right, left = along(self.axis, 1, *self.place), along(self.axis, SIDE - 1, *self.place)
        first, second = self.halves(0), self.halves(1)
        src, dst, device = (
            (self.src.at[self.q(2), items, first], self.far.at[0, items], right),
            (self.src.at[self.q(2), items, second], self.far.at[1, items], left),
            (self.src.at[self.q(1), items, second], self.near.at[0, items, second], right),
            (self.src.at[self.q(3), items, first], self.near.at[1, items, first], left),
            (self.src.at[self.q(1), items, first], self.near.at[0, items, first], right),
            (self.src.at[self.q(3), items, second], self.near.at[1, items, second], left),
        )[message]
        return src, dst, device

    def start(self, message, items, index):
        src, dst, device = self.copy(message, items)
        descriptor = remote(src, dst, self.send.at[index, message], self.recv.at[index, message], device)
        descriptor.start()
        self.started.append(descriptor)

    def wait(self, message, items, index):
        _, dst, device = self.copy(message, items)
        remote(dst, dst, self.send.at[index, message], self.recv.at[index, message], device).wait_recv()

    def first(self, items, index):
        for message in (0, 1, 2, 3):
            self.start(message, items, index)

    def second(self, items, index):
        for message, step, part in ((0, 1, 0), (1, 3, 1)):
            self.wait(message, items, index)
            rows = self.halves(part)
            total = self.src[self.q(step), items, rows].astype(F32) + self.far[message, items].astype(F32)
            self.src[self.q(step), items, rows] = total.astype(BF16)
            self.start(message + 4, items, index)

    def total(self, items, index):
        for message in (2, 3, 4, 5):
            self.wait(message, items, index)
        own = self.src[self.pos, items].astype(F32)
        return own + self.near[0, items].astype(F32) + self.near[1, items].astype(F32)

    def finish(self):
        for descriptor in self.started:
            descriptor.wait_send()


class RingGather:
    def __init__(self, axis, pos, place, buf, send, recv, rows):
        self.axis, self.pos, self.place = axis, pos, place
        self.buf, self.send, self.recv = buf, send, recv
        self.half = rows // 2
        self.started = []

    def q(self, step):
        return (self.pos + step) % SIDE

    def view(self, step, items, part):
        return self.buf.at[self.q(step), items, pl.ds(part * self.half, self.half)]

    PLAN = ((0, 0, 3, 1), (1, 0, 1, 3), (1, 0, 3, 1), (0, 0, 1, 3), (0, 3, 2, 1), (1, 1, 2, 3))

    def start(self, message, items, index):
        part, here, _, direction = self.PLAN[message]
        view = self.view(here, items, part)
        device = along(self.axis, direction, *self.place)
        descriptor = remote(view, view, self.send.at[index, message], self.recv.at[index, message], device)
        descriptor.start()
        self.started.append(descriptor)

    def wait(self, message, items, index):
        part, _, there, direction = self.PLAN[message]
        view = self.view(there, items, part)
        device = along(self.axis, direction, *self.place)
        remote(view, view, self.send.at[index, message], self.recv.at[index, message], device).wait_recv()

    def first(self, items, index):
        for message in (0, 1, 2, 3):
            self.start(message, items, index)

    def second(self, items, index):
        for message in (0, 1):
            self.wait(message, items, index)
            self.start(message + 4, items, index)

    def finish(self):
        for descriptor in self.started:
            descriptor.wait_send()


def reduce_kernel(
    scale, columns, lefts, projs, table, grad_out,
    lefts_in, projs_in, table_in, cols, part, part_in, factors, blocks, far1, near1, summed, slots, far2, near2, pieces, grad, block_of,
    in_sem, col_sem, sib_send, sib_recv, part_send, part_recv, fac_send, fac_recv, swap_send, swap_recv,
    send1, recv1, send2, recv2, send3, recv3, own_sem,
):
    adapters, tokens, width = columns.shape
    rank = projs.shape[2]
    per_adapter = width // BW
    half = BW // NC
    group = rank // (2 * SIDE)
    slot_count = NX * NY * NC
    x, y, c, z = coords()
    sibling = at(x, y, 1 - c)
    mine = pl.ds(pl.multiple_of(c * tokens, tokens), tokens)
    theirs = pl.ds(pl.multiple_of((1 - c) * tokens, tokens), tokens)
    partners = plane_partners(x, y, c) + [{"mp": (z + step) % NZ} for step in range(1, NZ)]
    greet(partners)
    inputs = []
    for source, dest in ((projs, projs_in), (lefts, lefts_in), (table, table_in)):
        copy = pltpu.make_async_copy(source, dest, in_sem.at[len(inputs)])
        copy.start()
        inputs.append(copy)
    local, swapped, sends = [], [], []
    for j in range(per_adapter):
        lanes = pl.ds(pl.multiple_of(j * BW + c * half, half), half)
        keep = pltpu.make_async_copy(columns.at[:, :, lanes], cols.at[j, :, mine], col_sem.at[j])
        keep.start()
        local.append(keep)

    def partial(a):
        return lax.dot_general(projs_in[a], lefts_in[a], (((0,), (0,)), ((), ())), preferred_element_type=F32)

    inputs[0].wait()
    inputs[1].wait()
    for step in (2, 1, 3):
        part[step - 1] = partial((z + step) % NZ).astype(BF16)
    own = partial(z)
    await_partners(partners)

    for step in (2, 1, 3):
        copy = remote(
            part.at[step - 1], part_in.at[step - 1], part_send.at[step - 1], part_recv.at[step - 1],
            {"mp": (z + step) % NZ},
        )
        copy.start()
        sends.append(copy)

    for j in range(per_adapter):
        lanes = pl.ds(pl.multiple_of(j * BW + (1 - c) * half, half), half)
        swap = remote(columns.at[:, :, lanes], cols.at[j, :, mine], sib_send.at[j], sib_recv.at[j], sibling)
        swap.start()
        sends.append(swap)
        swapped.append(remote(cols.at[j, :, theirs], cols.at[j, :, theirs], sib_send.at[j], sib_recv.at[j], sibling))

    total = own
    for step in (1, 3, 2):
        remote(
            part_in.at[step - 1], part_in.at[step - 1], part_send.at[step - 1], part_recv.at[step - 1], sibling
        ).wait_recv()
        total += part_in[step - 1].astype(F32)
    factors[z, c] = total.astype(BF16)
    for step in (2, 1, 3):
        view = factors.at[z, c]
        copy = remote(view, view, fac_send.at[step - 1], fac_recv.at[step - 1], {"mp": (z + step) % NZ})
        copy.start()
        sends.append(copy)

    place = (x, y, c)
    ring1 = [
        RingSum(o, place[o], place, blocks.at[o], far1.at[o], near1.at[o], send1.at[o], recv1.at[o], group)
        for o in range(2)
    ]
    items = []
    for t, step in enumerate(ORDER):
        a = (z + step) % NZ
        view = factors.at[a, c]
        if step:
            back = NZ - step
            remote(view, view, fac_send.at[back - 1], fac_recv.at[back - 1], sibling).wait_recv()
        swap = remote(view, view, swap_send.at[t], swap_recv.at[t], sibling)
        swap.start()
        sends.append(swap)
        other = factors.at[a, 1 - c]
        remote(other, other, swap_send.at[t], swap_recv.at[t], sibling).wait_recv()
        if t == 0:
            for j in range(per_adapter):
                local[j].wait()
                swapped[j].wait_recv()
        factor = jnp.concatenate([factors[a, 0], factors[a, 1]], axis=1)

        def block(j, carry):
            product = lax.dot_general(
                factor, cols[j, a], (((1,), (0,)), ((), ())), preferred_element_type=F32
            ).astype(BF16)
            for o in range(2):
                for q in range(SIDE):
                    low = (o * SIDE + q) * group
                    blocks[o, q, a * per_adapter + j] = product[low : low + group]
            return carry

        lax.fori_loop(0, per_adapter, block, 0)
        items.append(pl.ds(a * per_adapter, per_adapter))
        for o in range(2):
            ring1[o].first(items[t], t)

    empty = adapters * per_adapter

    def find(s, carry):
        found = jnp.int32(empty)
        for k in range(adapters * per_adapter):
            found = jnp.where(table_in[0, k] == s, jnp.int32(k), found)
        block_of[s] = found
        return carry

    inputs[2].wait()
    lax.fori_loop(0, slot_count, find, 0)

    for t in range(adapters):
        for o in range(2):
            ring1[o].second(items[t], t)
    for o in range(2):
        summed[o, empty] = jnp.zeros(summed.shape[2:], BF16)
    for t in range(adapters):
        for o in range(2):
            summed[o, items[t]] = ring1[o].total(items[t], t).astype(BF16)

    every = pl.ds(0, SIDE * NC)
    ring2 = [
        RingSum(1 - o, place[1 - o], place, slots.at[o], far2.at[o], near2.at[o], send2.at[o], recv2.at[o], group)
        for o in range(2)
    ]
    for step in (2, 1, 3, 0):
        for o in range(2):
            dest = ring2[o].q(step)

            def fill(j, carry, o=o, dest=dest):
                s = (j // NC) * (NY * NC) + dest * NC + j % NC if o == 0 else dest * (NY * NC) + j
                slots[o, dest, j] = summed[o, block_of[s]]
                return carry

            lax.fori_loop(0, SIDE * NC, fill, 0)
            if step == 2:
                ring2[o].start(0, every, 0)
                ring2[o].start(1, every, 0)
            if step == 1:
                ring2[o].start(2, every, 0)
            if step == 3:
                ring2[o].start(3, every, 0)
    for o in range(2):
        ring2[o].second(every, 0)

    def target(o, step, core):
        return at((x + step) % NX, y, (c + core) % NC) if o == 0 else at(x, (y + step) % NY, (c + core) % NC)

    def spot(o, step, core):
        q, lane = (place[o] + step) % SIDE, (c + core) % NC
        return grad.at[
            pl.ds(pl.multiple_of((o * SIDE + q) * group, group), group), pl.ds(pl.multiple_of(lane * half, half), half)
        ]

    owned = []
    for o in range(2):
        pieces[o] = (ring2[o].total(every, 0) * scale).astype(BF16)
        for step in (2, 1, 3, 0):
            for core in range(NC):
                source = pieces.at[o, ((place[o] + step) % SIDE) * NC + (c + core) % NC]
                if step == 0 and core == 0:
                    copy = pltpu.make_async_copy(source, spot(o, 0, 0), own_sem.at[o])
                    copy.start()
                    owned.append(copy)
                else:
                    index = step * NC + core
                    copy = remote(source, spot(o, 0, 0), send3.at[o, index], recv3.at[o, index], target(o, step, core))
                    copy.start()
                    sends.append(copy)
    for o in range(2):
        for step in range(SIDE):
            for core in range(NC):
                if step or core:
                    index = step * NC + core
                    view = spot(o, SIDE - step, NC - core)
                    remote(view, view, send3.at[o, index], recv3.at[o, index], sibling).wait_recv()
    for copy in owned:
        copy.wait()
    grad_out[...] = grad[...]
    for copy in sends:
        copy.wait_send()
    for ring in ring1 + ring2:
        ring.finish()


def summed_gradient(columns, lefts, projs, table, scale):
    adapters, tokens, width = columns.shape
    rank = projs.shape[2]
    per_adapter = width // BW
    count = adapters * per_adapter
    half, group, pair = BW // NC, rank // (2 * SIDE), SIDE * NC
    dma = pltpu.SemaphoreType.DMA
    return pl.pallas_call(
        functools.partial(reduce_kernel, scale),
        out_shape=jax.ShapeDtypeStruct((rank, BW), BF16),
        in_specs=[
            pl.BlockSpec(memory_space=pltpu.HBM),
            pl.BlockSpec(memory_space=pltpu.HBM),
            pl.BlockSpec(memory_space=pltpu.HBM),
            pl.BlockSpec(memory_space=pltpu.HBM),
        ],
        out_specs=pl.BlockSpec(memory_space=pltpu.VMEM),
        scratch_shapes=[
            pltpu.VMEM(lefts.shape, BF16),
            pltpu.VMEM(projs.shape, BF16),
            pltpu.SMEM(table.shape, jnp.int32),
            pltpu.VMEM((per_adapter, adapters, NC * tokens, half), BF16),
            pltpu.VMEM((NZ - 1, rank, tokens), BF16),
            pltpu.VMEM((NZ - 1, rank, tokens), BF16),
            pltpu.VMEM((adapters, NC, rank, tokens), BF16),
            pltpu.VMEM((2, SIDE, count, group, half), BF16),
            pltpu.VMEM((2, 2, count, group // 2, half), BF16),
            pltpu.VMEM((2, 2, count, group, half), BF16),
            pltpu.VMEM((2, count + 1, group, half), BF16),
            pltpu.VMEM((2, SIDE, pair, group, half), BF16),
            pltpu.VMEM((2, 2, pair, group // 2, half), BF16),
            pltpu.VMEM((2, 2, pair, group, half), BF16),
            pltpu.VMEM((2, pair, group, half), BF16),
            pltpu.VMEM((rank, BW), BF16),
            pltpu.SMEM((NX * NY * NC,), jnp.int32),
            dma((3,)),
            dma((per_adapter,)),
            dma((per_adapter,)),
            dma((per_adapter,)),
            dma((NZ - 1,)),
            dma((NZ - 1,)),
            dma((NZ - 1,)),
            dma((NZ - 1,)),
            dma((adapters,)),
            dma((adapters,)),
            dma((2, adapters, 6)),
            dma((2, adapters, 6)),
            dma((2, 1, 6)),
            dma((2, 1, 6)),
            dma((2, pair)),
            dma((2, pair)),
            dma((2,)),
        ],
        compiler_params=pltpu.CompilerParams(
            collective_id=0, has_side_effects=True, vmem_limit_bytes=121 * 2**19
        ),
        name="summed_gradient",
    )(columns, lefts, projs, table)


def newton_polynomial():
    terms = [0.25 * math.comb(5, i) * 1.25 ** (5 - i) * (-0.25) ** i for i in range(6)]
    terms[0] += 1.25 * 0.25
    return terms


def dot16(a, b):
    return jnp.dot(a, b, preferred_element_type=F32)


def root_into(stat, out, n1, n2, n3, u, v, w):
    size = stat.shape[0]
    width = min(size, 256)
    tiles = [pl.ds(low, width) for low in range(0, size, width)]
    square = jnp.zeros((1, width), F32)
    for tile in tiles:
        value = stat[:, tile]
        square += jnp.sum(value * value, axis=0, keepdims=True)
    norm = jnp.sqrt(jnp.sum(square) + EPSILON)
    inverse = 1.0 / norm
    u1, u2, u3, u4, u5, u6 = newton_polynomial()
    for tile in tiles:
        n1[:, tile] = (stat[:, tile] * inverse).astype(BF16)
    for tile in tiles:
        n2[:, tile] = dot16(n1[...], n1[:, tile]).astype(BF16)
    for tile in tiles:
        value = dot16(n1[...], n2[:, tile])
        n3[:, tile] = value.astype(BF16)
        second, first = n2[:, tile].astype(F32), n1[:, tile].astype(F32)
        v[:, tile] = (u4 * first + u5 * second + u6 * value).astype(BF16)
        u[:, tile] = (u1 * first + u2 * second + u3 * value).astype(BF16)
    for tile in tiles:
        w[:, tile] = (u[:, tile].astype(F32) + dot16(n3[...], v[:, tile])).astype(BF16)
    for tile in tiles:
        value = w[:, tile]
        n2[:, tile] = (dot16(w[...], value) - 3.125 * value.astype(F32)).astype(BF16)
        n3[:, tile] = (1.5625 * n1[:, tile].astype(F32) - dot16(w[...], n1[:, tile])).astype(BF16)
    for tile in tiles:
        value = n2[:, tile]
        v[:, tile] = (dot16(n2[...], value) + (2 * 1.5625**2) * value.astype(F32)).astype(BF16)
    scale = jnp.sqrt(jnp.sqrt(inverse))
    for low, tile in zip(range(0, size, width), tiles):
        value = n3[:, tile]
        last = 1.25 * w[:, tile].astype(F32) + (0.25 * 1.5625**4) * value.astype(F32) + 0.25 * dot16(v[...], value)
        row = lax.broadcasted_iota(jnp.int32, (size, width), 0)
        column = lax.broadcasted_iota(jnp.int32, (size, width), 1)
        eye = jnp.where(row == column + low, jnp.float32(1.25 * 1.5625), jnp.float32(0.0))
        out[:, tile] = ((eye - last) * scale).astype(BF16)


def root_kernel(
    table, groups, grad, left_stat, right_stat, left_root, right_root,
    new_left, new_right, root_left, root_right, update,
    *scratch,
):
    rank, width = grad.shape
    value = grad[...]
    transposed = (((0,), (0,)), ((), ()))
    across = (((1,), (1,)), ((), ()))
    new_left[0, 0] = 0.9 * left_stat[0, 0] + 0.1 * lax.dot_general(value, value, across, preferred_element_type=F32)
    tile_width = min(width, 256)
    for low in range(0, width, tile_width):
        tile = pl.ds(low, tile_width)
        new_right[0, 0, :, tile] = 0.9 * right_stat[0, 0, :, tile] + 0.1 * lax.dot_general(
            value, grad[:, tile], transposed, preferred_element_type=F32
        )
    owner = lax.axis_index("dp")
    renew = jnp.bool_(False)
    for k in range(table.shape[1]):
        renew = jnp.logical_or(renew, jnp.logical_and(table[0, k] == owner, groups[0, k] == 0))

    @pl.when(renew)
    def _():
        root_into(new_left.at[0, 0], root_left.at[0, 0], *scratch[:6])
        root_into(new_right.at[0, 0], root_right.at[0, 0], *scratch[6:])

    @pl.when(jnp.logical_not(renew))
    def _():
        root_left[...] = left_root[...]
        root_right[...] = right_root[...]

    half_product = dot16(root_left[0, 0], value).astype(BF16)
    direction = dot16(half_product, root_right[0, 0])
    wide = value.astype(F32)
    count = 1.0 / (rank * width)
    ratio = (jnp.sum(wide * wide) * count + EPSILON) / (jnp.sum(direction * direction) * count + EPSILON)
    update[...] = (direction * jnp.sqrt(ratio)).astype(BF16)


def preconditioned(table, groups, grad, left_stats, right_stats, left_roots, right_roots):
    rank, width = grad.shape
    vmem, smem = pl.BlockSpec(memory_space=pltpu.VMEM), pl.BlockSpec(memory_space=pltpu.SMEM)
    like = lambda a, kind: jax.ShapeDtypeStruct(a.shape, kind)
    return pl.pallas_call(
        root_kernel,
        out_shape=(
            like(left_stats, F32), like(right_stats, F32), like(left_roots, BF16), like(right_roots, BF16),
            jax.ShapeDtypeStruct((rank, width), BF16),
        ),
        in_specs=[smem] * 2 + [vmem] * 5,
        out_specs=(vmem,) * 5,
        scratch_shapes=[pltpu.VMEM((rank, rank), BF16)] * 6 + [pltpu.VMEM((width, width), BF16)] * 6,
        compiler_params=pltpu.CompilerParams(vmem_limit_bytes=48 * 2**20),
        name="preconditioned",
    )(table, groups, grad, left_stats, right_stats, left_roots, right_roots)


def gather_kernel(
    table_hbm, update, by_block, table, by_slot, table_sem, send1, recv1, send2, recv2, send3, recv3, swap_send, swap_recv, own_sem
):
    rank, width = update.shape
    half, group, pair = width // NC, rank // (2 * SIDE), SIDE * NC
    rows_of, adapters = by_block.shape[3], by_block.shape[4]
    x, y, c, _ = coords()
    place = (x, y, c)
    sibling = at(x, y, 1 - c)
    partners = plane_partners(x, y, c)
    greet(partners)
    table_copy = pltpu.make_async_copy(table_hbm, table, table_sem.at[0])
    table_copy.start()
    await_partners(partners)
    sends = []

    def spot(o, step, core):
        return by_slot.at[o, place[1 - o], ((place[o] + step) % SIDE) * NC + (c + core) % NC]

    owned = []
    for step in (2, 1, 3, 0):
        for o in range(2):
            for core in range(NC):
                q, lane = (place[o] + step) % SIDE, (c + core) % NC
                source = update.at[
                    pl.ds(pl.multiple_of((o * SIDE + q) * group, group), group),
                    pl.ds(pl.multiple_of(lane * half, half), half),
                ]
                if step == 0 and core == 0:
                    copy = pltpu.make_async_copy(source, spot(o, 0, 0), own_sem.at[o])
                    copy.start()
                    owned.append(copy)
                else:
                    index = step * NC + core
                    device = at(q, y, lane) if o == 0 else at(x, q, lane)
                    copy = remote(source, spot(o, 0, 0), send1.at[o, index], recv1.at[o, index], device)
                    copy.start()
                    sends.append(copy)

    every = pl.ds(0, pair)
    ring2 = [
        RingGather(1 - o, place[1 - o], place, by_slot.at[o], send2.at[o], recv2.at[o], group) for o in range(2)
    ]
    for o in range(2):
        owned[o].wait()
        for step in range(SIDE):
            for core in range(NC):
                if step or core:
                    index = step * NC + core
                    view = spot(o, SIDE - step, NC - core)
                    remote(view, view, send1.at[o, index], recv1.at[o, index], sibling).wait_recv()
        ring2[o].first(every, 0)
    for o in range(2):
        ring2[o].second(every, 0)
    for o in range(2):
        for message in (2, 3, 4, 5):
            ring2[o].wait(message, every, 0)

    ring1 = [
        RingGather(o, place[o], place, by_block.at[o, :, c], send1_, recv1_, group)
        for o, (send1_, recv1_) in enumerate(((send3.at[0], recv3.at[0]), (send3.at[1], recv3.at[1])))
    ]
    everyone = pl.ds(0, adapters)

    def pass_on(o, step, j):
        view = by_block.at[o, (place[o] + step) % SIDE, c, j]
        copy = remote(view, view, swap_send.at[o, step, j], swap_recv.at[o, step, j], sibling)
        copy.start()
        sends.append(copy)

    table_copy.wait()
    for j in range(rows_of):
        for o in range(2):

            def fill(a, carry, o=o, j=j):
                s = table[0, a * rows_of + j]
                if o == 0:
                    row, item = (s // NC) % NY, (s // (NY * NC)) * NC + s % NC
                else:
                    row, item = s // (NY * NC), s % (NY * NC)
                by_block[o, place[o], c, j, a] = by_slot[o, row, item]
                return carry

            lax.fori_loop(0, adapters, fill, 0)
            ring1[o].buf = by_block.at[o, :, c, j]
            ring1[o].first(everyone, j)
            pass_on(o, 0, j)
    for j in range(rows_of):
        for o in range(2):
            ring1[o].buf = by_block.at[o, :, c, j]
            ring1[o].second(everyone, j)
    for j in range(rows_of):
        for o in range(2):
            ring1[o].buf = by_block.at[o, :, c, j]
            ring1[o].wait(2, everyone, j)
            pass_on(o, 3, j)
            ring1[o].wait(3, everyone, j)
            pass_on(o, 1, j)
    for j in range(rows_of):
        for o in range(2):
            ring1[o].buf = by_block.at[o, :, c, j]
            ring1[o].wait(4, everyone, j)
            ring1[o].wait(5, everyone, j)
            pass_on(o, 2, j)
    for o in range(2):
        for step in range(SIDE):
            for j in range(rows_of):
                view = by_block.at[o, (place[o] + step) % SIDE, 1 - c, j]
                remote(view, view, swap_send.at[o, step, j], swap_recv.at[o, step, j], sibling).wait_recv()
    for copy in sends:
        copy.wait_send()
    for ring in ring1 + ring2:
        ring.finish()


def gathered(table, update, adapters):
    rank, width = update.shape
    half, group, pair = width // NC, rank // (2 * SIDE), SIDE * NC
    per_adapter = table.shape[1] // adapters
    shape = (2, SIDE, NC, per_adapter, adapters, group, half)
    dma = pltpu.SemaphoreType.DMA
    return pl.pallas_call(
        gather_kernel,
        out_shape=jax.ShapeDtypeStruct(shape, BF16),
        in_specs=[pl.BlockSpec(memory_space=pl.ANY), pl.BlockSpec(memory_space=pltpu.VMEM)],
        out_specs=pl.BlockSpec(memory_space=pltpu.VMEM),
        scratch_shapes=[
            pltpu.SMEM(table.shape, jnp.int32),
            pltpu.VMEM((2, SIDE, pair, group, half), BF16),
            dma((1,)),
            dma((2, pair)),
            dma((2, pair)),
            dma((2, 1, 6)),
            dma((2, 1, 6)),
            dma((2, per_adapter, 6)),
            dma((2, per_adapter, 6)),
            dma((2, SIDE, per_adapter)),
            dma((2, SIDE, per_adapter)),
            dma((2,)),
        ],
        compiler_params=pltpu.CompilerParams(
            collective_id=1, has_side_effects=True, vmem_limit_bytes=24 * 2**20
        ),
        name="gathered",
    )(table, update)


def place_kernel(parts, out, sem):
    group, half = parts.shape[5:]
    copies = []
    for o in range(2):
        for q in range(SIDE):
            for c in range(NC):
                for j in range(parts.shape[3]):
                    copies.append(
                        pltpu.make_async_copy(
                            parts.at[o, q, c, j],
                            out.at[:, pl.ds((o * SIDE + q) * group, group), pl.ds(j * BW + c * half, half)],
                            sem.at[len(copies)],
                        )
                    )
    for copy in copies:
        copy.start()
    for copy in copies:
        copy.wait()


def placed_blocks(parts):
    _, _, _, per_adapter, adapters, group, _ = parts.shape
    return pl.pallas_call(
        place_kernel,
        out_shape=jax.ShapeDtypeStruct((adapters, 2 * SIDE * group, per_adapter * BW), BF16),
        in_specs=[pl.BlockSpec(memory_space=pltpu.VMEM)],
        out_specs=pl.BlockSpec(memory_space=pltpu.HBM),
        scratch_shapes=[pltpu.SemaphoreType.DMA((2 * SIDE * NC * per_adapter,))],
        compiler_params=pltpu.CompilerParams(vmem_limit_bytes=16 * 2**20),
        name="placed_blocks",
    )(parts)


def body(
    columns,
    lefts,
    projs,
    slot_table,
    refresh_group,
    left_stats,
    right_stats,
    left_roots,
    right_roots,
):
    total_tokens = lax.axis_size("dp") * columns.shape[1]
    grad = summed_gradient(columns, jnp.swapaxes(lefts, 1, 2), projs, slot_table, 1.0 / math.sqrt(total_tokens))
    new_left, new_right, root_left, root_right, update = preconditioned(
        slot_table, refresh_group, grad, left_stats, right_stats, left_roots, right_roots
    )
    parts = gathered(slot_table, update, columns.shape[0])
    return new_left, new_right, root_left, root_right, placed_blocks(parts)


def solution(mesh):
    placed = (
        P(None, "dp", "mp"),
        P(None, "dp", "mp"),
        P(None, "mp", None),
        P("mp", None),
        P("mp", None),
        P("mp", "dp", None, None),
        P("mp", "dp", None, None),
        P("mp", "dp", None, None),
        P("mp", "dp", None, None),
    )
    return jax.shard_map(
        body,
        mesh=mesh,
        in_specs=placed,
        out_specs=(
            P("mp", "dp", None, None),
            P("mp", "dp", None, None),
            P("mp", "dp", None, None),
            P("mp", "dp", None, None),
            P(None, None, "mp"),
        ),
        check_vma=False,
    )
```

```python
import functools
import itertools
import math

import jax
import jax.numpy as jnp
from jax import lax
from jax.experimental import pallas as pl
from jax.experimental.pallas import tpu as pltpu
from jax.sharding import PartitionSpec as P

BW = 768
EPSILON = 1e-06
NX, NY, NC, NZ = 4, 4, 2, 4
SIDE = 4
ORDER = (0, 1, 3, 2)
MESH = pl.DeviceIdType.MESH
F32, BF16 = jnp.float32, jnp.bfloat16


def coords():
    dp = lax.axis_index("dp")
    return dp // (NY * NC), (dp // NC) % NY, dp % NC, lax.axis_index("mp")


def at(x, y, c):
    return {"dp": (x * NY + y) * NC + c}


def along(axis, step, x, y, c):
    return at((x + step) % NX, y, c) if axis == 0 else at(x, (y + step) % NY, c)


def remote(src, dst, send, recv, device):
    return pltpu.make_async_remote_copy(
        src_ref=src, dst_ref=dst, send_sem=send, recv_sem=recv, device_id=device, device_id_type=MESH
    )


def plane_partners(x, y, c):
    partners = [at(x, y, 1 - c)]
    for step in range(1, SIDE):
        for core in range(NC):
            partners.append(at((x + step) % NX, y, (c + core) % NC))
            partners.append(at(x, (y + step) % NY, (c + core) % NC))
    return partners


def greet(partners):
    barrier = pltpu.get_barrier_semaphore()
    for partner in partners:
        pl.semaphore_signal(barrier, inc=1, device_id=partner, device_id_type=MESH)


def await_partners(partners):
    pl.semaphore_wait(pltpu.get_barrier_semaphore(), len(partners))


class Ring:
    def __init__(self, axis, pos, place, send, recv):
        self.axis, self.pos, self.place, self.send, self.recv = axis, pos, place, send, recv
        self.started = []

    def q(self, step):
        return (self.pos + step) % SIDE

    def put(self, src, dst, step, index):
        descriptor = remote(src, dst, self.send.at[index], self.recv.at[index], along(self.axis, step, *self.place))
        descriptor.start()
        self.started.append(descriptor)

    def wait(self, dst, index):
        device = along(self.axis, 1, *self.place)
        remote(dst, dst, self.send.at[index], self.recv.at[index], device).wait_recv()

    def finish(self):
        for descriptor in self.started:
            descriptor.wait_send()


class RingSum(Ring):
    def __init__(self, axis, pos, place, src, far, near, send, recv):
        super().__init__(axis, pos, place, send, recv)
        self.src, self.far, self.near = src, far, near

    def first(self, d, view, index):
        self.put(self.src.at[(self.q(2),) + view], self.far.at[view], d, (index, 0))
        self.put(self.src.at[(self.q(SIDE - d),) + view], self.near.at[(d // 2,) + view], SIDE - d, (index, 1))

    def wait_far(self, view, index):
        self.wait(self.far.at[view], (index, 0))

    def second(self, d, view, index):
        total = self.src[(self.q(d),) + view].astype(F32) + self.far[view].astype(F32)
        self.src[(self.q(d),) + view] = total.astype(BF16)
        self.put(self.src.at[(self.q(d),) + view], self.near.at[(1 - d // 2,) + view], d, (index, 2))

    def wait_near(self, d, view, index):
        self.wait(self.near.at[(d // 2,) + view], (index, 1))

    def wait_sum(self, d, view, index):
        self.wait(self.near.at[(1 - d // 2,) + view], (index, 2))

    def total(self, view):
        own = self.src[(self.pos,) + view].astype(F32)
        return own + self.near[(0,) + view].astype(F32) + self.near[(1,) + view].astype(F32)


class RingGather(Ring):
    def __init__(self, axis, pos, place, buf, send, recv):
        super().__init__(axis, pos, place, send, recv)
        self.buf = buf

    def at(self, step, view):
        return self.buf.at[(self.q(step),) + view]

    def first(self, d, view, index):
        self.put(self.at(0, view), self.at(0, view), d, (index, 0))
        self.put(self.at(0, view), self.at(0, view), SIDE - d, (index, 1))

    def second(self, d, view, index):
        self.wait(self.at(SIDE - d, view), (index, 0))
        self.put(self.at(SIDE - d, view), self.at(SIDE - d, view), d, (index, 2))

    def wait_near(self, d, view, index):
        self.wait(self.at(d, view), (index, 1))

    def wait_opposite(self, view, index):
        self.wait(self.at(2, view), (index, 2))


def reduce_kernel(
    scale, columns, lefts, projs, table, grad_out,
    lefts_in, projs_in, table_in, cols, part, part_in, factors, blocks, far1, near1, summed, slots, far2, near2,
    pieces, grad, block_of,
    in_sem, col_sem, sib_send, sib_recv, part_send, part_recv, fac_send, fac_recv, swap_send, swap_recv,
    send1, recv1, send2, recv2, send3, recv3, own_sem,
):
    adapters, tokens, width = columns.shape
    rank = projs.shape[2]
    per_adapter = width // BW
    half = BW // NC
    group = rank // (2 * SIDE)
    slot_count = NX * NY * NC
    x, y, c, z = coords()
    sibling = at(x, y, 1 - c)
    mine = pl.ds(pl.multiple_of(c * tokens, tokens), tokens)
    theirs = pl.ds(pl.multiple_of((1 - c) * tokens, tokens), tokens)
    partners = plane_partners(x, y, c) + [{"mp": (z + step) % NZ} for step in range(1, NZ)]
    greet(partners)
    inputs = []
    for source, dest in ((projs, projs_in), (lefts, lefts_in), (table, table_in)):
        copy = pltpu.make_async_copy(source, dest, in_sem.at[len(inputs)])
        copy.start()
        inputs.append(copy)
    local, swapped, sends = [], [], []
    for j in range(per_adapter):
        lanes = pl.ds(pl.multiple_of(j * BW + c * half, half), half)
        keep = pltpu.make_async_copy(columns.at[:, :, lanes], cols.at[j, :, mine], col_sem.at[j])
        keep.start()
        local.append(keep)

    def partial(a):
        return lax.dot_general(projs_in[a], lefts_in[a], (((0,), (0,)), ((), ())), preferred_element_type=F32)

    inputs[0].wait()
    inputs[1].wait()
    for step in (2, 1, 3):
        part[step - 1] = partial((z + step) % NZ).astype(BF16)
    own = partial(z)
    await_partners(partners)

    for step in (2, 1, 3):
        copy = remote(
            part.at[step - 1], part_in.at[step - 1], part_send.at[step - 1], part_recv.at[step - 1],
            {"mp": (z + step) % NZ},
        )
        copy.start()
        sends.append(copy)

    for j in range(per_adapter):
        lanes = pl.ds(pl.multiple_of(j * BW + (1 - c) * half, half), half)
        swap = remote(columns.at[:, :, lanes], cols.at[j, :, mine], sib_send.at[j], sib_recv.at[j], sibling)
        swap.start()
        sends.append(swap)
        swapped.append(remote(cols.at[j, :, theirs], cols.at[j, :, theirs], sib_send.at[j], sib_recv.at[j], sibling))

    total = own
    for step in (1, 3, 2):
        remote(
            part_in.at[step - 1], part_in.at[step - 1], part_send.at[step - 1], part_recv.at[step - 1], sibling
        ).wait_recv()
        total += part_in[step - 1].astype(F32)
    factors[z, c] = total.astype(BF16)
    for step in (2, 1, 3):
        view = factors.at[z, c]
        copy = remote(view, view, fac_send.at[step - 1], fac_recv.at[step - 1], {"mp": (z + step) % NZ})
        copy.start()
        sends.append(copy)

    place = (x, y, c)
    ring1 = [
        RingSum(o, place[o], place, blocks.at[o], far1.at[o], near1.at[o], send1.at[o], recv1.at[o]) for o in range(2)
    ]
    parts = range(2)
    tall = group // 2
    items, way = [], (1, 3, 1, 3)
    for t, step in enumerate(ORDER):
        a = (z + step) % NZ
        view = factors.at[a, c]
        if step:
            back = NZ - step
            remote(view, view, fac_send.at[back - 1], fac_recv.at[back - 1], sibling).wait_recv()
        swap = remote(view, view, swap_send.at[t], swap_recv.at[t], sibling)
        swap.start()
        sends.append(swap)
        other = factors.at[a, 1 - c]
        remote(other, other, swap_send.at[t], swap_recv.at[t], sibling).wait_recv()
        if t == 0:
            for j in range(per_adapter):
                local[j].wait()
                swapped[j].wait_recv()
        factor = jnp.concatenate([factors[a, 0], factors[a, 1]], axis=1)

        def block(j, carry):
            product = lax.dot_general(
                factor, cols[j, a], (((1,), (0,)), ((), ())), preferred_element_type=F32
            ).astype(BF16)
            for o in range(2):
                for q in range(SIDE):
                    for h in parts:
                        low = (o * SIDE + q) * group + h * tall
                        blocks[o, q, h, a * per_adapter + j] = product[low : low + tall]
            return carry

        lax.fori_loop(0, per_adapter, block, 0)
        items.append(pl.ds(a * per_adapter, per_adapter))
        for o in range(2):
            ring1[o].first(way[t], (slice(None), items[t]), 4 * t)

    empty = adapters * per_adapter

    def find(s, carry):
        found = jnp.int32(empty)
        for k in range(adapters * per_adapter):
            found = jnp.where(table_in[0, k] == s, jnp.int32(k), found)
        block_of[s] = found
        return carry

    inputs[2].wait()
    lax.fori_loop(0, slot_count, find, 0)

    for o in range(2):
        for h in parts:
            summed[o, empty, h] = jnp.zeros(summed.shape[3:], BF16)
    for h in parts:
        for t in range(adapters):
            for o in range(2):
                if h == 0:
                    ring1[o].wait_far((slice(None), items[t]), 4 * t)
                ring1[o].second(way[t], (h, items[t]), 4 * t + h)

    ring2 = [
        RingSum(1 - o, place[1 - o], place, slots.at[o], far2.at[o], near2.at[o], send2.at[o], recv2.at[o])
        for o in range(2)
    ]
    sets = ((1, pl.ds(0, SIDE)), (3, pl.ds(SIDE, SIDE)))
    for h in parts:
        for t in range(adapters):
            for o in range(2):
                if h == 0:
                    ring1[o].wait_near(way[t], (slice(None), items[t]), 4 * t)
                ring1[o].wait_sum(way[t], (h, items[t]), 4 * t + h)
                summed[o, items[t], h] = ring1[o].total((h, items[t])).astype(BF16)
        for step in (2, 1, 3, 0):
            for o in range(2):
                dest = ring2[o].q(step)

                def fill(j, carry, o=o, dest=dest, h=h):
                    s = (j // NC) * (NY * NC) + dest * NC + j % NC if o == 0 else dest * (NY * NC) + j
                    slots[o, dest, h, j] = summed[o, block_of[s], h]
                    return carry

                lax.fori_loop(0, SIDE * NC, fill, 0)
        for o in range(2):
            for n, (d, some) in enumerate(sets):
                ring2[o].first(d, (h, some), 2 * h + n)
    for h in parts:
        for o in range(2):
            for n, (d, some) in enumerate(sets):
                ring2[o].wait_far((h, some), 2 * h + n)
                ring2[o].second(d, (h, some), 2 * h + n)

    def target(o, step, core):
        return at((x + step) % NX, y, (c + core) % NC) if o == 0 else at(x, (y + step) % NY, (c + core) % NC)

    def spot(o, step, core):
        q, lane = (place[o] + step) % SIDE, (c + core) % NC
        return grad.at[
            pl.ds(pl.multiple_of((o * SIDE + q) * group, group), group), pl.ds(pl.multiple_of(lane * half, half), half)
        ]

    owned = []
    for o in range(2):
        for h in parts:
            for n, (d, some) in enumerate(sets):
                ring2[o].wait_near(d, (h, some), 2 * h + n)
                ring2[o].wait_sum(d, (h, some), 2 * h + n)
            pieces[o, :, pl.ds(h * tall, tall)] = (ring2[o].total((h,)) * scale).astype(BF16)
        for step in (2, 1, 3, 0):
            for core in range(NC):
                source = pieces.at[o, ((place[o] + step) % SIDE) * NC + (c + core) % NC]
                if step == 0 and core == 0:
                    copy = pltpu.make_async_copy(source, spot(o, 0, 0), own_sem.at[o])
                    copy.start()
                    owned.append(copy)
                else:
                    index = step * NC + core
                    copy = remote(source, spot(o, 0, 0), send3.at[o, index], recv3.at[o, index], target(o, step, core))
                    copy.start()
                    sends.append(copy)
    for o in range(2):
        for step in range(SIDE):
            for core in range(NC):
                if step or core:
                    index = step * NC + core
                    view = spot(o, SIDE - step, NC - core)
                    remote(view, view, send3.at[o, index], recv3.at[o, index], sibling).wait_recv()
    for copy in owned:
        copy.wait()
    grad_out[...] = grad[...]
    for copy in sends:
        copy.wait_send()
    for ring in ring1 + ring2:
        ring.finish()


def summed_gradient(columns, lefts, projs, table, scale):
    adapters, tokens, width = columns.shape
    rank = projs.shape[2]
    per_adapter = width // BW
    count = adapters * per_adapter
    half, group, pair = BW // NC, rank // (2 * SIDE), SIDE * NC
    dma = pltpu.SemaphoreType.DMA
    return pl.pallas_call(
        functools.partial(reduce_kernel, scale),
        out_shape=jax.ShapeDtypeStruct((rank, BW), BF16),
        in_specs=[
            pl.BlockSpec(memory_space=pltpu.HBM),
            pl.BlockSpec(memory_space=pltpu.HBM),
            pl.BlockSpec(memory_space=pltpu.HBM),
            pl.BlockSpec(memory_space=pltpu.HBM),
        ],
        out_specs=pl.BlockSpec(memory_space=pltpu.VMEM),
        scratch_shapes=[
            pltpu.VMEM(lefts.shape, BF16),
            pltpu.VMEM(projs.shape, BF16),
            pltpu.SMEM(table.shape, jnp.int32),
            pltpu.VMEM((per_adapter, adapters, NC * tokens, half), BF16),
            pltpu.VMEM((NZ - 1, rank, tokens), BF16),
            pltpu.VMEM((NZ - 1, rank, tokens), BF16),
            pltpu.VMEM((adapters, NC, rank, tokens), BF16),
            pltpu.VMEM((2, SIDE, 2, count, group // 2, half), BF16),
            pltpu.VMEM((2, 2, count, group // 2, half), BF16),
            pltpu.VMEM((2, 2, 2, count, group // 2, half), BF16),
            pltpu.VMEM((2, count + 1, 2, group // 2, half), BF16),
            pltpu.VMEM((2, SIDE, 2, pair, group // 2, half), BF16),
            pltpu.VMEM((2, 2, pair, group // 2, half), BF16),
            pltpu.VMEM((2, 2, 2, pair, group // 2, half), BF16),
            pltpu.VMEM((2, pair, group, half), BF16),
            pltpu.VMEM((rank, BW), BF16),
            pltpu.SMEM((NX * NY * NC,), jnp.int32),
            dma((3,)),
            dma((per_adapter,)),
            dma((per_adapter,)),
            dma((per_adapter,)),
            dma((NZ - 1,)),
            dma((NZ - 1,)),
            dma((NZ - 1,)),
            dma((NZ - 1,)),
            dma((adapters,)),
            dma((adapters,)),
            dma((2, 4 * adapters, 3)),
            dma((2, 4 * adapters, 3)),
            dma((2, 4, 3)),
            dma((2, 4, 3)),
            dma((2, pair)),
            dma((2, pair)),
            dma((2,)),
        ],
        compiler_params=pltpu.CompilerParams(
            collective_id=0, has_side_effects=True, vmem_limit_bytes=63 * 2**20
        ),
        name="summed_gradient",
    )(columns, lefts, projs, table)


def newton_polynomial():
    terms = [0.25 * math.comb(5, i) * 1.25 ** (5 - i) * (-0.25) ** i for i in range(6)]
    terms[0] += 1.25 * 0.25
    return terms


def dot16(a, b):
    return jnp.dot(a, b, preferred_element_type=F32)


def root_steps(stat, square, out, n1, n2, n3, u, v, w):
    size = stat.shape[0]
    width = min(size, 256)
    tiles = [pl.ds(low, width) for low in range(0, size, width)]
    inverse = lax.rsqrt(square + EPSILON)
    u1, u2, u3, u4, u5, u6 = newton_polynomial()
    for tile in tiles:
        n1[:, tile] = (stat[:, tile] * inverse).astype(BF16)
    yield
    for tile in tiles:
        n2[:, tile] = dot16(n1[...], n1[:, tile]).astype(BF16)
        yield
    for tile in tiles:
        value = dot16(n1[...], n2[:, tile])
        n3[:, tile] = value.astype(BF16)
        second, first = n2[:, tile].astype(F32), n1[:, tile].astype(F32)
        v[:, tile] = (u4 * first + u5 * second + u6 * value).astype(BF16)
        u[:, tile] = (u1 * first + u2 * second + u3 * value).astype(BF16)
        yield
    for tile in tiles:
        w[:, tile] = (u[:, tile].astype(F32) + dot16(n3[...], v[:, tile])).astype(BF16)
        yield
    for tile in tiles:
        value = w[:, tile]
        n2[:, tile] = (dot16(w[...], value) - 3.125 * value.astype(F32)).astype(BF16)
        yield
    for tile in tiles:
        value = n2[:, tile]
        v[:, tile] = (dot16(n2[...], value) + (2 * 1.5625**2) * value.astype(F32)).astype(BF16)
        n3[:, tile] = (1.5625 * n1[:, tile].astype(F32) - dot16(w[...], n1[:, tile])).astype(BF16)
        yield
    scale = jnp.sqrt(jnp.sqrt(inverse))
    for low, tile in zip(range(0, size, width), tiles):
        value = n3[:, tile]
        last = 1.25 * w[:, tile].astype(F32) + (0.25 * 1.5625**4) * value.astype(F32) + 0.25 * dot16(v[...], value)
        row = lax.broadcasted_iota(jnp.int32, (size, width), 0)
        column = lax.broadcasted_iota(jnp.int32, (size, width), 1)
        eye = jnp.where(row == column + low, jnp.float32(1.25 * 1.5625), jnp.float32(0.0))
        out[:, tile] = ((eye - last) * scale).astype(BF16)
        yield


def root_kernel(
    table, groups, grad_in, left_stat, right_stat, left_root, right_root,
    new_left_out, new_right_out, root_left_out, root_right_out, update,
    grad, old_left, old_right, new_left, new_right, root_left, root_right, in_sem, out_sem, *scratch,
):
    rank, width = grad.shape
    loads = [
        pltpu.make_async_copy(source, dest, in_sem.at[n])
        for n, (source, dest) in enumerate(
            ((grad_in, grad), (left_stat.at[0, 0], old_left), (right_stat.at[0, 0], old_right))
        )
    ]
    for load in loads:
        load.start()
    stores = []

    def store(source, dest):
        copy = pltpu.make_async_copy(source, dest.at[0, 0], out_sem.at[len(stores)])
        copy.start()
        stores.append(copy)

    owner = lax.axis_index("dp")
    renew = jnp.bool_(False)
    for k in range(table.shape[1]):
        renew = jnp.logical_or(renew, jnp.logical_and(table[0, k] == owner, groups[0, k] == 0))
    loads[0].wait()
    transposed = (((0,), (0,)), ((), ()))
    across = (((1,), (1,)), ((), ()))
    value = grad[...]
    product = lax.dot_general(value, value, across, preferred_element_type=F32)
    loads[1].wait()
    fresh = 0.9 * old_left[...] + 0.1 * product
    new_left[...] = fresh
    store(new_left, new_left_out)
    left_square = jnp.sum(fresh * fresh)
    loads[2].wait()
    tile_width = min(width, 256)
    squares = jnp.zeros((1, tile_width), F32)
    for low in range(0, width, tile_width):
        tile = pl.ds(low, tile_width)
        product = lax.dot_general(value, grad[:, tile], transposed, preferred_element_type=F32)
        fresh = 0.9 * old_right[:, tile] + 0.1 * product
        new_right[:, tile] = fresh
        squares += jnp.sum(fresh * fresh, axis=0, keepdims=True)
    store(new_right, new_right_out)
    right_square = jnp.sum(squares)

    @pl.when(renew)
    def _():
        steps = [
            root_steps(new_right, right_square, root_right, *scratch[6:]),
            root_steps(new_left, left_square, root_left, *scratch[:6]),
        ]
        for _ in itertools.zip_longest(*steps):
            pass

    @pl.when(jnp.logical_not(renew))
    def _():
        first = pltpu.make_async_copy(left_root.at[0, 0], root_left, in_sem.at[3])
        second = pltpu.make_async_copy(right_root.at[0, 0], root_right, in_sem.at[4])
        first.start()
        second.start()
        first.wait()
        second.wait()

    store(root_left, root_left_out)
    store(root_right, root_right_out)
    half_product = dot16(root_left[...], grad[...]).astype(BF16)
    direction = dot16(half_product, root_right[...])
    wide = grad[...].astype(F32)
    count = 1.0 / (rank * width)
    ratio = (jnp.sum(wide * wide) * count + EPSILON) / (jnp.sum(direction * direction) * count + EPSILON)
    update[...] = (direction * jnp.sqrt(ratio)).astype(BF16)
    for copy in stores:
        copy.wait()


def preconditioned(table, groups, grad, left_stats, right_stats, left_roots, right_roots):
    rank, width = grad.shape
    vmem, smem, hbm = (pl.BlockSpec(memory_space=space) for space in (pltpu.VMEM, pltpu.SMEM, pl.ANY))
    like = lambda a, kind: jax.ShapeDtypeStruct(a.shape, kind)
    return pl.pallas_call(
        root_kernel,
        out_shape=(
            like(left_stats, F32), like(right_stats, F32), like(left_roots, BF16), like(right_roots, BF16),
            jax.ShapeDtypeStruct((rank, width), BF16),
        ),
        in_specs=[smem] * 2 + [hbm] * 5,
        out_specs=(hbm,) * 4 + (vmem,),
        scratch_shapes=[
            pltpu.VMEM((rank, width), BF16),
            pltpu.VMEM((rank, rank), F32),
            pltpu.VMEM((width, width), F32),
            pltpu.VMEM((rank, rank), F32),
            pltpu.VMEM((width, width), F32),
            pltpu.VMEM((rank, rank), BF16),
            pltpu.VMEM((width, width), BF16),
            pltpu.SemaphoreType.DMA((5,)),
            pltpu.SemaphoreType.DMA((4,)),
        ]
        + [pltpu.VMEM((rank, rank), BF16)] * 6
        + [pltpu.VMEM((width, width), BF16)] * 6,
        compiler_params=pltpu.CompilerParams(vmem_limit_bytes=63 * 2**20),
        name="preconditioned",
    )(table, groups, grad, left_stats, right_stats, left_roots, right_roots)


def gather_kernel(
    table_hbm, update, by_block, table, slots00, slots01, slots10, slots11, table_sem,
    send1, recv1, send2, recv2, send3, recv3, swap_send, swap_recv, own_sem,
):
    rank, width = update.shape
    half, group = width // NC, rank // (2 * SIDE)
    adapters, per_adapter = by_block.shape[4:6]
    tall = group // 2
    parts = range(2)
    by_slot = ((slots00, slots01), (slots10, slots11))
    x, y, c, _ = coords()
    place = (x, y, c)
    sibling = at(x, y, 1 - c)
    partners = plane_partners(x, y, c)
    greet(partners)
    table_copy = pltpu.make_async_copy(table_hbm, table, table_sem.at[0])
    table_copy.start()
    await_partners(partners)
    sends = []

    def spot(o, h, step, core):
        return by_slot[o][h].at[place[1 - o], ((place[o] + step) % SIDE) * NC + (c + core) % NC]

    owned = []
    for h in parts:
        for step in (2, 1, 3, 0):
            for o in range(2):
                for core in range(NC):
                    q, lane = (place[o] + step) % SIDE, (c + core) % NC
                    source = update.at[
                        pl.ds(pl.multiple_of((o * SIDE + q) * group + h * tall, tall), tall),
                        pl.ds(pl.multiple_of(lane * half, half), half),
                    ]
                    if step == 0 and core == 0:
                        copy = pltpu.make_async_copy(source, spot(o, h, 0, 0), own_sem.at[o, h])
                        copy.start()
                        owned.append(copy)
                    else:
                        index = (o, h, step * NC + core)
                        device = at(q, y, lane) if o == 0 else at(x, q, lane)
                        copy = remote(source, spot(o, h, 0, 0), send1.at[index], recv1.at[index], device)
                        copy.start()
                        sends.append(copy)

    slot_sets = ((1, pl.ds(0, SIDE)), (3, pl.ds(SIDE, SIDE)))
    ring2 = [
        [RingGather(1 - o, place[1 - o], place, by_slot[o][h], send2.at[o, h], recv2.at[o, h]) for h in parts]
        for o in range(2)
    ]
    for h in parts:
        for o in range(2):
            owned[2 * h + o].wait()
            for step in range(SIDE):
                for core in range(NC):
                    if step or core:
                        index = (o, h, step * NC + core)
                        view = spot(o, h, SIDE - step, NC - core)
                        remote(view, view, send1.at[index], recv1.at[index], sibling).wait_recv()
            for n, (d, some) in enumerate(slot_sets):
                ring2[o][h].first(d, (some,), n)
    for h in parts:
        for o in range(2):
            for n, (d, some) in enumerate(slot_sets):
                ring2[o][h].second(d, (some,), n)

    ring1 = [RingGather(o, place[o], place, by_block.at[o, :, c], send3.at[o], recv3.at[o]) for o in range(2)]
    sets = ((1, pl.ds(0, adapters // 2)), (3, pl.ds(adapters // 2, adapters // 2)))

    def pass_on(o, step, h, n):
        view = by_block.at[o, (place[o] + step) % SIDE, c, h, sets[n][1]]
        index = (o, step, 2 * h + n)
        copy = remote(view, view, swap_send.at[index], swap_recv.at[index], sibling)
        copy.start()
        sends.append(copy)

    table_copy.wait()
    for h in parts:
        for o in range(2):
            for n, (d, some) in enumerate(slot_sets):
                ring2[o][h].wait_near(d, (some,), n)
                ring2[o][h].wait_opposite((some,), n)

            def fill(a, carry, o=o, h=h):
                for j in range(per_adapter):
                    s = table[0, a * per_adapter + j]
                    if o == 0:
                        row, item = (s // NC) % NY, (s // (NY * NC)) * NC + s % NC
                    else:
                        row, item = s // (NY * NC), s % (NY * NC)
                    by_block[o, place[o], c, h, a, j] = by_slot[o][h][row, item]
                return carry

            lax.fori_loop(0, adapters, fill, 0)
            for n, (d, some) in enumerate(sets):
                ring1[o].first(d, (h, some), 2 * h + n)
        for o in range(2):
            for n in range(2):
                pass_on(o, 0, h, n)
    for h in parts:
        for o in range(2):
            for n, (d, some) in enumerate(sets):
                ring1[o].second(d, (h, some), 2 * h + n)
                pass_on(o, SIDE - d, h, n)
        for o in range(2):
            for n, (d, some) in enumerate(sets):
                ring1[o].wait_near(d, (h, some), 2 * h + n)
                pass_on(o, d, h, n)
    for h in parts:
        for o in range(2):
            for n, (d, some) in enumerate(sets):
                ring1[o].wait_opposite((h, some), 2 * h + n)
                pass_on(o, 2, h, n)
    for o in range(2):
        for step in range(SIDE):
            for h in parts:
                for n in range(2):
                    view = by_block.at[o, (place[o] + step) % SIDE, 1 - c, h, sets[n][1]]
                    index = (o, step, 2 * h + n)
                    remote(view, view, swap_send.at[index], swap_recv.at[index], sibling).wait_recv()
    for copy in sends:
        copy.wait_send()
    for ring in ring1 + ring2[0] + ring2[1]:
        ring.finish()


def gathered(table, update, adapters):
    rank, width = update.shape
    half, group, pair = width // NC, rank // (2 * SIDE), SIDE * NC
    per_adapter = table.shape[1] // adapters
    shape = (2, SIDE, NC, 2, adapters, per_adapter, group // 2, half)
    dma = pltpu.SemaphoreType.DMA
    return pl.pallas_call(
        gather_kernel,
        out_shape=jax.ShapeDtypeStruct(shape, BF16),
        in_specs=[pl.BlockSpec(memory_space=pl.ANY), pl.BlockSpec(memory_space=pltpu.VMEM)],
        out_specs=pl.BlockSpec(memory_space=pltpu.VMEM),
        scratch_shapes=[
            pltpu.SMEM(table.shape, jnp.int32),
            pltpu.VMEM((SIDE, pair, group // 2, half), BF16),
            pltpu.VMEM((SIDE, pair, group // 2, half), BF16),
            pltpu.VMEM((SIDE, pair, group // 2, half), BF16),
            pltpu.VMEM((SIDE, pair, group // 2, half), BF16),
            dma((1,)),
            dma((2, 2, pair)),
            dma((2, 2, pair)),
            dma((2, 2, 2, 3)),
            dma((2, 2, 2, 3)),
            dma((2, 4, 3)),
            dma((2, 4, 3)),
            dma((2, SIDE, 4)),
            dma((2, SIDE, 4)),
            dma((2, 2)),
        ],
        compiler_params=pltpu.CompilerParams(
            collective_id=1, has_side_effects=True, vmem_limit_bytes=24 * 2**20
        ),
        name="gathered",
    )(table, update)


def place_kernel(parts, out, sem):
    per_adapter, tall, half = parts.shape[5:]
    copies = []
    for o in range(2):
        for q in range(SIDE):
            for h in range(2):
                for c in range(NC):
                    for j in range(per_adapter):
                        rows = pl.ds((o * SIDE + q) * 2 * tall + h * tall, tall)
                        lanes = pl.ds(j * BW + c * half, half)
                        copies.append(
                            pltpu.make_async_copy(parts.at[o, q, c, h, :, j], out.at[:, rows, lanes], sem.at[len(copies)])
                        )
    for copy in copies:
        copy.start()
    for copy in copies:
        copy.wait()


def placed_blocks(parts):
    _, _, _, _, adapters, per_adapter, tall, _ = parts.shape
    return pl.pallas_call(
        place_kernel,
        out_shape=jax.ShapeDtypeStruct((adapters, 4 * SIDE * tall, per_adapter * BW), BF16),
        in_specs=[pl.BlockSpec(memory_space=pltpu.VMEM)],
        out_specs=pl.BlockSpec(memory_space=pltpu.HBM),
        scratch_shapes=[pltpu.SemaphoreType.DMA((4 * SIDE * NC * per_adapter,))],
        compiler_params=pltpu.CompilerParams(vmem_limit_bytes=16 * 2**20),
        name="placed_blocks",
    )(parts)


def body(
    columns,
    lefts,
    projs,
    slot_table,
    refresh_group,
    left_stats,
    right_stats,
    left_roots,
    right_roots,
):
    total_tokens = lax.axis_size("dp") * columns.shape[1]
    grad = summed_gradient(columns, jnp.swapaxes(lefts, 1, 2), projs, slot_table, 1.0 / math.sqrt(total_tokens))
    new_left, new_right, root_left, root_right, update = preconditioned(
        slot_table, refresh_group, grad, left_stats, right_stats, left_roots, right_roots
    )
    parts = gathered(slot_table, update, columns.shape[0])
    return new_left, new_right, root_left, root_right, placed_blocks(parts)


def solution(mesh):
    placed = (
        P(None, "dp", "mp"),
        P(None, "dp", "mp"),
        P(None, "mp", None),
        P("mp", None),
        P("mp", None),
        P("mp", "dp", None, None),
        P("mp", "dp", None, None),
        P("mp", "dp", None, None),
        P("mp", "dp", None, None),
    )
    return jax.shard_map(
        body,
        mesh=mesh,
        in_specs=placed,
        out_specs=(
            P("mp", "dp", None, None),
            P("mp", "dp", None, None),
            P("mp", "dp", None, None),
            P("mp", "dp", None, None),
            P(None, None, "mp"),
        ),
        check_vma=False,
    )
```

```python
import functools
import itertools
import math

import jax
import jax.numpy as jnp
from jax import lax
from jax.experimental import pallas as pl
from jax.experimental.pallas import tpu as pltpu
from jax.sharding import PartitionSpec as P

BW = 768
EPSILON = 1e-06
NX, NY, NC, NZ = 4, 4, 2, 4
SIDE = 4
ORDER = (0, 1, 3, 2)
MESH = pl.DeviceIdType.MESH
F32, BF16 = jnp.float32, jnp.bfloat16


def coords():
    dp = lax.axis_index("dp")
    return dp // (NY * NC), (dp // NC) % NY, dp % NC, lax.axis_index("mp")


def at(x, y, c):
    return {"dp": (x * NY + y) * NC + c}


def along(axis, step, x, y, c):
    return at((x + step) % NX, y, c) if axis == 0 else at(x, (y + step) % NY, c)


def remote(src, dst, send, recv, device):
    return pltpu.make_async_remote_copy(
        src_ref=src, dst_ref=dst, send_sem=send, recv_sem=recv, device_id=device, device_id_type=MESH
    )


def plane_partners(x, y, c):
    partners = [at(x, y, 1 - c)]
    for step in range(1, SIDE):
        for core in range(NC):
            partners.append(at((x + step) % NX, y, (c + core) % NC))
            partners.append(at(x, (y + step) % NY, (c + core) % NC))
    return partners


def greet(partners):
    barrier = pltpu.get_barrier_semaphore()
    for partner in partners:
        pl.semaphore_signal(barrier, inc=1, device_id=partner, device_id_type=MESH)


def await_partners(partners):
    pl.semaphore_wait(pltpu.get_barrier_semaphore(), len(partners))


class Ring:
    def __init__(self, axis, pos, place, send, recv):
        self.axis, self.pos, self.place, self.send, self.recv = axis, pos, place, send, recv
        self.started = []

    def q(self, step):
        return (self.pos + step) % SIDE

    def put(self, src, dst, step, index):
        descriptor = remote(src, dst, self.send.at[index], self.recv.at[index], along(self.axis, step, *self.place))
        descriptor.start()
        self.started.append(descriptor)

    def wait(self, dst, index):
        device = along(self.axis, 1, *self.place)
        remote(dst, dst, self.send.at[index], self.recv.at[index], device).wait_recv()

    def finish(self):
        for descriptor in self.started:
            descriptor.wait_send()


class RingSum(Ring):
    def __init__(self, axis, pos, place, src, far, near, send, recv):
        super().__init__(axis, pos, place, send, recv)
        self.src, self.far, self.near = src, far, near

    def first(self, d, view, index):
        self.put(self.src.at[(self.q(2),) + view], self.far.at[view], d, (index, 0))
        self.put(self.src.at[(self.q(SIDE - d),) + view], self.near.at[(d // 2,) + view], SIDE - d, (index, 1))

    def wait_far(self, view, index):
        self.wait(self.far.at[view], (index, 0))

    def second(self, d, view, index):
        total = self.src[(self.q(d),) + view].astype(F32) + self.far[view].astype(F32)
        self.src[(self.q(d),) + view] = total.astype(BF16)
        self.put(self.src.at[(self.q(d),) + view], self.near.at[(1 - d // 2,) + view], d, (index, 2))

    def wait_near(self, d, view, index):
        self.wait(self.near.at[(d // 2,) + view], (index, 1))

    def wait_sum(self, d, view, index):
        self.wait(self.near.at[(1 - d // 2,) + view], (index, 2))

    def total(self, view):
        own = self.src[(self.pos,) + view].astype(F32)
        return own + self.near[(0,) + view].astype(F32) + self.near[(1,) + view].astype(F32)


class RingGather(Ring):
    def __init__(self, axis, pos, place, buf, send, recv):
        super().__init__(axis, pos, place, send, recv)
        self.buf = buf

    def at(self, step, view):
        return self.buf.at[(self.q(step),) + view]

    def first(self, d, view, index):
        self.put(self.at(0, view), self.at(0, view), d, (index, 0))
        self.put(self.at(0, view), self.at(0, view), SIDE - d, (index, 1))

    def second(self, d, view, index):
        self.wait(self.at(SIDE - d, view), (index, 0))
        self.put(self.at(SIDE - d, view), self.at(SIDE - d, view), d, (index, 2))

    def wait_near(self, d, view, index):
        self.wait(self.at(d, view), (index, 1))

    def wait_opposite(self, view, index):
        self.wait(self.at(2, view), (index, 2))


def reduce(
    scale, columns, lefts, projs, table, later,
    lefts_in, projs_in, table_in, cols, part, part_in, factors, blocks, far1, near1, summed, slots, far2, near2,
    pieces, grad, block_of,
    in_sem, col_sem, sib_send, sib_recv, part_send, part_recv, fac_send, fac_recv, swap_send, swap_recv,
    send1, recv1, send2, recv2, send3, recv3, own_sem,
):
    adapters, tokens, width = columns.shape
    rank = projs.shape[2]
    per_adapter = width // BW
    half = BW // NC
    group = rank // (2 * SIDE)
    slot_count = NX * NY * NC
    x, y, c, z = coords()
    sibling = at(x, y, 1 - c)
    mine = pl.ds(pl.multiple_of(c * tokens, tokens), tokens)
    theirs = pl.ds(pl.multiple_of((1 - c) * tokens, tokens), tokens)
    partners = plane_partners(x, y, c) + [{"mp": (z + step) % NZ} for step in range(1, NZ)]
    greet(partners)
    inputs = []
    for source, dest in ((projs, projs_in), (lefts, lefts_in), (table, table_in)):
        copy = pltpu.make_async_copy(source, dest, in_sem.at[len(inputs)])
        copy.start()
        inputs.append(copy)
    local, swapped, sends = [], [], []
    for j in range(per_adapter):
        lanes = pl.ds(pl.multiple_of(j * BW + c * half, half), half)
        keep = pltpu.make_async_copy(columns.at[:, :, lanes], cols.at[j, :, mine], col_sem.at[j])
        keep.start()
        local.append(keep)

    def partial(a):
        return lax.dot_general(projs_in[a], lefts_in[a], (((0,), (0,)), ((), ())), preferred_element_type=F32)

    inputs[0].wait()
    inputs[1].wait()
    for step in (2, 1, 3):
        part[step - 1] = partial((z + step) % NZ).astype(BF16)
    own = partial(z)
    await_partners(partners)

    for step in (2, 1, 3):
        copy = remote(
            part.at[step - 1], part_in.at[step - 1], part_send.at[step - 1], part_recv.at[step - 1],
            {"mp": (z + step) % NZ},
        )
        copy.start()
        sends.append(copy)

    for j in range(per_adapter):
        lanes = pl.ds(pl.multiple_of(j * BW + (1 - c) * half, half), half)
        swap = remote(columns.at[:, :, lanes], cols.at[j, :, mine], sib_send.at[j], sib_recv.at[j], sibling)
        swap.start()
        sends.append(swap)
        swapped.append(remote(cols.at[j, :, theirs], cols.at[j, :, theirs], sib_send.at[j], sib_recv.at[j], sibling))

    for copy in later:
        copy.start()
    total = own
    for step in (1, 3, 2):
        remote(
            part_in.at[step - 1], part_in.at[step - 1], part_send.at[step - 1], part_recv.at[step - 1], sibling
        ).wait_recv()
        total += part_in[step - 1].astype(F32)
    factors[z, c] = total.astype(BF16)
    for step in (2, 1, 3):
        view = factors.at[z, c]
        copy = remote(view, view, fac_send.at[step - 1], fac_recv.at[step - 1], {"mp": (z + step) % NZ})
        copy.start()
        sends.append(copy)

    place = (x, y, c)
    ring1 = [
        RingSum(o, place[o], place, blocks.at[o], far1.at[o], near1.at[o], send1.at[o], recv1.at[o]) for o in range(2)
    ]
    parts = range(2)
    tall = group // 2
    items, way = [], (1, 3, 1, 3)
    for t, step in enumerate(ORDER):
        a = (z + step) % NZ
        view = factors.at[a, c]
        if step:
            back = NZ - step
            remote(view, view, fac_send.at[back - 1], fac_recv.at[back - 1], sibling).wait_recv()
        swap = remote(view, view, swap_send.at[t], swap_recv.at[t], sibling)
        swap.start()
        sends.append(swap)
        other = factors.at[a, 1 - c]
        remote(other, other, swap_send.at[t], swap_recv.at[t], sibling).wait_recv()
        if t == 0:
            for j in range(per_adapter):
                local[j].wait()
                swapped[j].wait_recv()
        factor = jnp.concatenate([factors[a, 0], factors[a, 1]], axis=1)

        def block(j, carry):
            product = lax.dot_general(
                factor, cols[j, a], (((1,), (0,)), ((), ())), preferred_element_type=F32
            ).astype(BF16)
            for o in range(2):
                for q in range(SIDE):
                    for h in parts:
                        low = (o * SIDE + q) * group + h * tall
                        blocks[o, q, h, a * per_adapter + j] = product[low : low + tall]
            return carry

        lax.fori_loop(0, per_adapter, block, 0)
        items.append(pl.ds(a * per_adapter, per_adapter))
        for o in range(2):
            ring1[o].first(way[t], (slice(None), items[t]), 4 * t)

    empty = adapters * per_adapter

    def find(s, carry):
        found = jnp.int32(empty)
        for k in range(adapters * per_adapter):
            found = jnp.where(table_in[0, k] == s, jnp.int32(k), found)
        block_of[s] = found
        return carry

    inputs[2].wait()
    lax.fori_loop(0, slot_count, find, 0)

    for o in range(2):
        for h in parts:
            summed[o, empty, h] = jnp.zeros(summed.shape[3:], BF16)
    for h in parts:
        for t in range(adapters):
            for o in range(2):
                if h == 0:
                    ring1[o].wait_far((slice(None), items[t]), 4 * t)
                ring1[o].second(way[t], (h, items[t]), 4 * t + h)

    ring2 = [
        RingSum(1 - o, place[1 - o], place, slots.at[o], far2.at[o], near2.at[o], send2.at[o], recv2.at[o])
        for o in range(2)
    ]
    sets = ((1, pl.ds(0, SIDE)), (3, pl.ds(SIDE, SIDE)))
    for h in parts:
        for t in range(adapters):
            for o in range(2):
                if h == 0:
                    ring1[o].wait_near(way[t], (slice(None), items[t]), 4 * t)
                ring1[o].wait_sum(way[t], (h, items[t]), 4 * t + h)
                summed[o, items[t], h] = ring1[o].total((h, items[t])).astype(BF16)
        for step in (2, 1, 3, 0):
            for o in range(2):
                dest = ring2[o].q(step)

                def fill(j, carry, o=o, dest=dest, h=h):
                    s = (j // NC) * (NY * NC) + dest * NC + j % NC if o == 0 else dest * (NY * NC) + j
                    slots[o, dest, h, j] = summed[o, block_of[s], h]
                    return carry

                lax.fori_loop(0, SIDE * NC, fill, 0)
        for o in range(2):
            for n, (d, some) in enumerate(sets):
                ring2[o].first(d, (h, some), 2 * h + n)
    for h in parts:
        for o in range(2):
            for n, (d, some) in enumerate(sets):
                ring2[o].wait_far((h, some), 2 * h + n)
                ring2[o].second(d, (h, some), 2 * h + n)

    def target(o, step, core):
        return at((x + step) % NX, y, (c + core) % NC) if o == 0 else at(x, (y + step) % NY, (c + core) % NC)

    def spot(o, step, core):
        q, lane = (place[o] + step) % SIDE, (c + core) % NC
        return grad.at[
            pl.ds(pl.multiple_of((o * SIDE + q) * group, group), group), pl.ds(pl.multiple_of(lane * half, half), half)
        ]

    owned = []
    for o in range(2):
        for h in parts:
            for n, (d, some) in enumerate(sets):
                ring2[o].wait_near(d, (h, some), 2 * h + n)
                ring2[o].wait_sum(d, (h, some), 2 * h + n)
            pieces[o, :, pl.ds(h * tall, tall)] = (ring2[o].total((h,)) * scale).astype(BF16)
        for step in (2, 1, 3, 0):
            for core in range(NC):
                source = pieces.at[o, ((place[o] + step) % SIDE) * NC + (c + core) % NC]
                if step == 0 and core == 0:
                    copy = pltpu.make_async_copy(source, spot(o, 0, 0), own_sem.at[o])
                    copy.start()
                    owned.append(copy)
                else:
                    index = step * NC + core
                    copy = remote(source, spot(o, 0, 0), send3.at[o, index], recv3.at[o, index], target(o, step, core))
                    copy.start()
                    sends.append(copy)
    for o in range(2):
        for step in range(SIDE):
            for core in range(NC):
                if step or core:
                    index = step * NC + core
                    view = spot(o, SIDE - step, NC - core)
                    remote(view, view, send3.at[o, index], recv3.at[o, index], sibling).wait_recv()
    for copy in owned:
        copy.wait()
    return sends + [copy for ring in ring1 + ring2 for copy in ring.started]


def newton_polynomial():
    terms = [0.25 * math.comb(5, i) * 1.25 ** (5 - i) * (-0.25) ** i for i in range(6)]
    terms[0] += 1.25 * 0.25
    return terms


def dot16(a, b):
    return jnp.dot(a, b, preferred_element_type=F32)


def root_steps(stat, square, renew, old, out, n1, n2, n3, u, v, w):
    size = stat.shape[0]
    width = min(size, 256)
    tiles = [pl.ds(low, width) for low in range(0, size, width)]
    inverse = lax.rsqrt(square + EPSILON)
    u1, u2, u3, u4, u5, u6 = newton_polynomial()
    for tile in tiles:
        n1[:, tile] = (stat[:, tile] * inverse).astype(BF16)
    yield
    for tile in tiles:
        n2[:, tile] = dot16(n1[...], n1[:, tile]).astype(BF16)
        yield
    for tile in tiles:
        value = dot16(n1[...], n2[:, tile])
        n3[:, tile] = value.astype(BF16)
        second, first = n2[:, tile].astype(F32), n1[:, tile].astype(F32)
        v[:, tile] = (u4 * first + u5 * second + u6 * value).astype(BF16)
        u[:, tile] = (u1 * first + u2 * second + u3 * value).astype(BF16)
        yield
    for tile in tiles:
        w[:, tile] = (u[:, tile].astype(F32) + dot16(n3[...], v[:, tile])).astype(BF16)
        yield
    for tile in tiles:
        value = w[:, tile]
        n2[:, tile] = (dot16(w[...], value) - 3.125 * value.astype(F32)).astype(BF16)
        yield
    for tile in tiles:
        value = n2[:, tile]
        v[:, tile] = (dot16(n2[...], value) + (2 * 1.5625**2) * value.astype(F32)).astype(BF16)
        n3[:, tile] = (1.5625 * n1[:, tile].astype(F32) - dot16(w[...], n1[:, tile])).astype(BF16)
        yield
    scale = jnp.sqrt(jnp.sqrt(inverse))
    for low, tile in zip(range(0, size, width), tiles):
        value = n3[:, tile]
        last = 1.25 * w[:, tile].astype(F32) + (0.25 * 1.5625**4) * value.astype(F32) + 0.25 * dot16(v[...], value)
        row = lax.broadcasted_iota(jnp.int32, (size, width), 0)
        column = lax.broadcasted_iota(jnp.int32, (size, width), 1)
        eye = jnp.where(row == column + low, jnp.float32(1.25 * 1.5625), jnp.float32(0.0))
        out[:, tile] = jnp.where(renew, (eye - last) * scale, old[:, tile].astype(F32)).astype(BF16)
        yield


def precondition(
    loads, table, groups, grad, old_left, old_right, old_root_left, old_root_right,
    new_left, new_right, root_left, root_right, update, *scratch,
):
    rank, width = grad.shape
    for load in loads:
        load.wait()
    owner = lax.axis_index("dp")
    renew = jnp.int32(0)
    for k in range(table.shape[1]):
        named = jnp.where(table[0, k] == owner, jnp.int32(1), jnp.int32(0))
        renew += named * jnp.where(groups[0, k] == 0, jnp.int32(1), jnp.int32(0))
    renew = renew == 1
    transposed = (((0,), (0,)), ((), ()))
    across = (((1,), (1,)), ((), ()))
    value = grad[...]
    product = lax.dot_general(value, value, across, preferred_element_type=F32)
    fresh = 0.9 * old_left[...] + 0.1 * product
    new_left[...] = fresh
    left_square = jnp.sum(fresh * fresh)
    tile_width = min(width, 256)
    squares = jnp.zeros((1, tile_width), F32)
    for low in range(0, width, tile_width):
        tile = pl.ds(low, tile_width)
        product = lax.dot_general(value, grad[:, tile], transposed, preferred_element_type=F32)
        fresh = 0.9 * old_right[:, tile] + 0.1 * product
        new_right[:, tile] = fresh
        squares += jnp.sum(fresh * fresh, axis=0, keepdims=True)
    right_square = jnp.sum(squares)
    steps = [
        root_steps(new_right, right_square, renew, old_root_right, root_right, *scratch[6:]),
        root_steps(new_left, left_square, renew, old_root_left, root_left, *scratch[:6]),
    ]
    for _ in itertools.zip_longest(*steps):
        pass
    half_product = dot16(root_left[...], grad[...]).astype(BF16)
    direction = dot16(half_product, root_right[...])
    wide = grad[...].astype(F32)
    count = 1.0 / (rank * width)
    ratio = (jnp.sum(wide * wide) * count + EPSILON) / (jnp.sum(direction * direction) * count + EPSILON)
    update[...] = (direction * jnp.sqrt(ratio)).astype(BF16)


def gather(
    table, update, by_block, slots00, slots01, slots10, slots11,
    send1, recv1, send2, recv2, send3, recv3, swap_send, swap_recv, own_sem,
):
    rank, width = update.shape
    half, group = width // NC, rank // (2 * SIDE)
    adapters, per_adapter = by_block.shape[3:5]
    tall = group // 2
    parts = range(2)
    by_slot = ((slots00, slots01), (slots10, slots11))
    x, y, c, _ = coords()
    place = (x, y, c)
    sibling = at(x, y, 1 - c)
    sends = []

    def spot(o, h, step, core):
        return by_slot[o][h].at[place[1 - o], ((place[o] + step) % SIDE) * NC + (c + core) % NC]

    owned = []
    for h in parts:
        for step in (2, 1, 3, 0):
            for o in range(2):
                for core in range(NC):
                    q, lane = (place[o] + step) % SIDE, (c + core) % NC
                    source = update.at[
                        pl.ds(pl.multiple_of((o * SIDE + q) * group + h * tall, tall), tall),
                        pl.ds(pl.multiple_of(lane * half, half), half),
                    ]
                    if step == 0 and core == 0:
                        copy = pltpu.make_async_copy(source, spot(o, h, 0, 0), own_sem.at[o, h])
                        copy.start()
                        owned.append(copy)
                    else:
                        index = (o, h, step * NC + core)
                        device = at(q, y, lane) if o == 0 else at(x, q, lane)
                        copy = remote(source, spot(o, h, 0, 0), send1.at[index], recv1.at[index], device)
                        copy.start()
                        sends.append(copy)

    slot_sets = ((1, pl.ds(0, SIDE)), (3, pl.ds(SIDE, SIDE)))
    ring2 = [
        [RingGather(1 - o, place[1 - o], place, by_slot[o][h], send2.at[o, h], recv2.at[o, h]) for h in parts]
        for o in range(2)
    ]
    for h in parts:
        for o in range(2):
            owned[2 * h + o].wait()
            for step in range(SIDE):
                for core in range(NC):
                    if step or core:
                        index = (o, h, step * NC + core)
                        view = spot(o, h, SIDE - step, NC - core)
                        remote(view, view, send1.at[index], recv1.at[index], sibling).wait_recv()
            for n, (d, some) in enumerate(slot_sets):
                ring2[o][h].first(d, (some,), n)
    for h in parts:
        for o in range(2):
            for n, (d, some) in enumerate(slot_sets):
                ring2[o][h].second(d, (some,), n)

    ring1 = [RingGather(o, place[o], place, by_block.at[o, :, c], send3.at[o], recv3.at[o]) for o in range(2)]

    def view_of(h, some):
        return (some, slice(None), pl.ds(h * tall, tall))

    sets = ((1, pl.ds(0, adapters // 2)), (3, pl.ds(adapters // 2, adapters // 2)))

    def pass_on(o, step, h, n):
        view = by_block.at[(o, (place[o] + step) % SIDE, c) + view_of(h, sets[n][1])]
        index = (o, step, 2 * h + n)
        copy = remote(view, view, swap_send.at[index], swap_recv.at[index], sibling)
        copy.start()
        sends.append(copy)

    for h in parts:
        for o in range(2):
            for n, (d, some) in enumerate(slot_sets):
                ring2[o][h].wait_near(d, (some,), n)
                ring2[o][h].wait_opposite((some,), n)

            def fill(a, carry, o=o, h=h):
                for j in range(per_adapter):
                    s = table[0, a * per_adapter + j]
                    if o == 0:
                        row, item = (s // NC) % NY, (s // (NY * NC)) * NC + s % NC
                    else:
                        row, item = s // (NY * NC), s % (NY * NC)
                    by_block[o, place[o], c, a, j, pl.ds(h * tall, tall)] = by_slot[o][h][row, item]
                return carry

            lax.fori_loop(0, adapters, fill, 0)
            for n, (d, some) in enumerate(sets):
                ring1[o].first(d, view_of(h, some), 2 * h + n)
        for o in range(2):
            for n in range(2):
                pass_on(o, 0, h, n)
    for h in parts:
        for o in range(2):
            for n, (d, some) in enumerate(sets):
                ring1[o].second(d, view_of(h, some), 2 * h + n)
                pass_on(o, SIDE - d, h, n)
        for o in range(2):
            for n, (d, some) in enumerate(sets):
                ring1[o].wait_near(d, view_of(h, some), 2 * h + n)
                pass_on(o, d, h, n)
    for h in parts:
        for o in range(2):
            for n, (d, some) in enumerate(sets):
                ring1[o].wait_opposite(view_of(h, some), 2 * h + n)
                pass_on(o, 2, h, n)
    for o in range(2):
        for step in range(SIDE):
            for h in parts:
                for n in range(2):
                    view = by_block.at[(o, (place[o] + step) % SIDE, 1 - c) + view_of(h, sets[n][1])]
                    index = (o, step, 2 * h + n)
                    remote(view, view, swap_send.at[index], swap_recv.at[index], sibling).wait_recv()
    return sends + [copy for ring in ring1 + ring2[0] + ring2[1] for copy in ring.started]


REDUCE, PRECONDITION = 34, 17


def step_kernel(
    scale, columns, lefts, projs, table, groups, left_stat, right_stat, left_root, right_root,
    new_left, new_right, root_left, root_right, parts, groups_in, load_sem, *scratch,
):
    for_reduce, rest = scratch[:REDUCE], scratch[REDUCE:]
    (old_left, old_right, old_root_left, old_root_right, update), rest = rest[:5], rest[5:]
    for_roots, for_gather = rest[:12], rest[12:]
    table_in, grad = for_reduce[2], for_reduce[15]
    loads = [
        pltpu.make_async_copy(source, dest, load_sem.at[n])
        for n, (source, dest) in enumerate(
            (
                (left_stat.at[0, 0], old_left),
                (right_stat.at[0, 0], old_right),
                (left_root.at[0, 0], old_root_left),
                (right_root.at[0, 0], old_root_right),
                (groups, groups_in),
            )
        )
    ]
    started = reduce(scale, columns, lefts, projs, table, loads, *for_reduce)
    precondition(
        loads, table_in, groups_in, grad, old_left, old_right, old_root_left, old_root_right,
        new_left, new_right, root_left, root_right, update, *for_roots,
    )
    started += gather(table_in, update, parts, *for_gather)
    for copy in started:
        copy.wait_send()


def whole_step(columns, lefts, projs, table, groups, left_stats, right_stats, left_roots, right_roots, scale):
    adapters, tokens, width = columns.shape
    rank = projs.shape[2]
    per_adapter = width // BW
    count = adapters * per_adapter
    half, group, pair = BW // NC, rank // (2 * SIDE), SIDE * NC
    tall = group // 2
    dma = lambda *shape: pltpu.SemaphoreType.DMA(shape)
    vmem = lambda *shape, kind=BF16: pltpu.VMEM(shape, kind)
    for_reduce = [
        vmem(*lefts.shape),
        vmem(*projs.shape),
        pltpu.SMEM(table.shape, jnp.int32),
        vmem(per_adapter, adapters, NC * tokens, half),
        vmem(NZ - 1, rank, tokens),
        vmem(NZ - 1, rank, tokens),
        vmem(adapters, NC, rank, tokens),
        vmem(2, SIDE, 2, count, tall, half),
        vmem(2, 2, count, tall, half),
        vmem(2, 2, 2, count, tall, half),
        vmem(2, count + 1, 2, tall, half),
        vmem(2, SIDE, 2, pair, tall, half),
        vmem(2, 2, pair, tall, half),
        vmem(2, 2, 2, pair, tall, half),
        vmem(2, pair, group, half),
        vmem(rank, BW),
        pltpu.SMEM((NX * NY * NC,), jnp.int32),
        dma(3),
        dma(per_adapter),
        dma(per_adapter),
        dma(per_adapter),
        dma(NZ - 1),
        dma(NZ - 1),
        dma(NZ - 1),
        dma(NZ - 1),
        dma(adapters),
        dma(adapters),
        dma(2, 4 * adapters, 3),
        dma(2, 4 * adapters, 3),
        dma(2, 4, 3),
        dma(2, 4, 3),
        dma(2, pair),
        dma(2, pair),
        dma(2),
    ]
    for_roots = [
        vmem(rank, rank, kind=F32),
        vmem(BW, BW, kind=F32),
        vmem(rank, rank),
        vmem(BW, BW),
        vmem(rank, BW),
    ]
    for_roots += [vmem(rank, rank)] * 6 + [vmem(BW, BW)] * 6
    for_gather = [vmem(SIDE, pair, tall, half)] * 4
    for_gather += [
        dma(2, 2, pair),
        dma(2, 2, pair),
        dma(2, 2, 2, 3),
        dma(2, 2, 2, 3),
        dma(2, 4, 3),
        dma(2, 4, 3),
        dma(2, SIDE, 4),
        dma(2, SIDE, 4),
        dma(2, 2),
    ]
    assert len(for_reduce) == REDUCE and len(for_roots) == PRECONDITION
    hbm, in_vmem = pl.BlockSpec(memory_space=pl.ANY), pl.BlockSpec(memory_space=pltpu.VMEM)
    return pl.pallas_call(
        functools.partial(step_kernel, scale),
        out_shape=(
            pltpu.VMEM((rank, rank), F32),
            pltpu.VMEM((BW, BW), F32),
            pltpu.VMEM((rank, rank), BF16),
            pltpu.VMEM((BW, BW), BF16),
            pltpu.VMEM((2, SIDE, NC, adapters, per_adapter, group, half), BF16),
        ),
        in_specs=[hbm] * 9,
        out_specs=(in_vmem,) * 5,
        scratch_shapes=[pltpu.SMEM(groups.shape, jnp.int32), dma(5)] + for_reduce + for_roots + for_gather,
        compiler_params=pltpu.CompilerParams(
            collective_id=0, has_side_effects=True, vmem_limit_bytes=53477376
        ),
        name="whole_step",
    )(columns, lefts, projs, table, groups, left_stats, right_stats, left_roots, right_roots)


def place_kernel(
    new_left, new_right, root_left, root_right, parts,
    new_left_out, new_right_out, root_left_out, root_right_out, out, sem,
):
    per_adapter, group, half = parts.shape[4:]
    moves = []
    for o in range(2):
        for q in range(SIDE):
            for c in range(NC):
                for j in range(per_adapter):
                    rows, lanes = pl.ds((o * SIDE + q) * group, group), pl.ds(j * BW + c * half, half)
                    moves.append((parts.at[o, q, c, :, j], out.at[:, rows, lanes]))
    moves += [
        (new_left, new_left_out.at[0, 0]),
        (new_right, new_right_out.at[0, 0]),
        (root_left, root_left_out.at[0, 0]),
        (root_right, root_right_out.at[0, 0]),
    ]
    copies = [pltpu.make_async_copy(source, dest, sem.at[n]) for n, (source, dest) in enumerate(moves)]
    for copy in copies:
        copy.start()
    for copy in copies:
        copy.wait()


def placed(new_left, new_right, root_left, root_right, parts):
    _, _, _, adapters, per_adapter, group, _ = parts.shape
    stacked = lambda a: jax.ShapeDtypeStruct((1, 1) + a.shape, a.dtype)
    return pl.pallas_call(
        place_kernel,
        out_shape=(
            stacked(new_left), stacked(new_right), stacked(root_left), stacked(root_right),
            jax.ShapeDtypeStruct((adapters, 2 * SIDE * group, per_adapter * BW), BF16),
        ),
        in_specs=[pl.BlockSpec(memory_space=pltpu.VMEM)] * 5,
        out_specs=(pl.BlockSpec(memory_space=pl.ANY),) * 5,
        scratch_shapes=[pltpu.SemaphoreType.DMA((2 * SIDE * NC * per_adapter + 4,))],
        compiler_params=pltpu.CompilerParams(vmem_limit_bytes=16 * 2**20),
        name="placed",
    )(new_left, new_right, root_left, root_right, parts)


def body(
    columns,
    lefts,
    projs,
    slot_table,
    refresh_group,
    left_stats,
    right_stats,
    left_roots,
    right_roots,
):
    total_tokens = lax.axis_size("dp") * columns.shape[1]
    results = whole_step(
        columns, jnp.swapaxes(lefts, 1, 2), projs, slot_table, refresh_group,
        left_stats, right_stats, left_roots, right_roots, 1.0 / math.sqrt(total_tokens),
    )
    return placed(*results)


def solution(mesh):
    shardings = (
        P(None, "dp", "mp"),
        P(None, "dp", "mp"),
        P(None, "mp", None),
        P("mp", None),
        P("mp", None),
        P("mp", "dp", None, None),
        P("mp", "dp", None, None),
        P("mp", "dp", None, None),
        P("mp", "dp", None, None),
    )
    return jax.shard_map(
        body,
        mesh=mesh,
        in_specs=shardings,
        out_specs=(
            P("mp", "dp", None, None),
            P("mp", "dp", None, None),
            P("mp", "dp", None, None),
            P("mp", "dp", None, None),
            P(None, None, "mp"),
        ),
        check_vma=False,
    )
```

```python
import functools
import itertools
import math

import jax
import jax.numpy as jnp
from jax import lax
from jax.experimental import pallas as pl
from jax.experimental.pallas import tpu as pltpu
from jax.sharding import PartitionSpec as P

BW = 768
EPSILON = 1e-06
NX, NY, NC, NZ = 4, 4, 2, 4
SIDE = 4
ORDER = (0, 1, 3, 2)
MESH = pl.DeviceIdType.MESH
F32, BF16 = jnp.float32, jnp.bfloat16


def coords():
    dp = lax.axis_index("dp")
    return dp // (NY * NC), (dp // NC) % NY, dp % NC, lax.axis_index("mp")


def at(x, y, c):
    return {"dp": (x * NY + y) * NC + c}


def along(axis, step, x, y, c):
    return at((x + step) % NX, y, c) if axis == 0 else at(x, (y + step) % NY, c)


def remote(src, dst, send, recv, device):
    return pltpu.make_async_remote_copy(
        src_ref=src, dst_ref=dst, send_sem=send, recv_sem=recv, device_id=device, device_id_type=MESH
    )


def plane_partners(x, y, c):
    partners = [at(x, y, 1 - c)]
    for step in range(1, SIDE):
        for core in range(NC):
            partners.append(at((x + step) % NX, y, (c + core) % NC))
            partners.append(at(x, (y + step) % NY, (c + core) % NC))
    return partners


def greet(partners):
    barrier = pltpu.get_barrier_semaphore()
    for partner in partners:
        pl.semaphore_signal(barrier, inc=1, device_id=partner, device_id_type=MESH)


def await_partners(partners):
    pl.semaphore_wait(pltpu.get_barrier_semaphore(), len(partners))


class Ring:
    def __init__(self, axis, pos, place, send, recv):
        self.axis, self.pos, self.place, self.send, self.recv = axis, pos, place, send, recv
        self.started = []

    def q(self, step):
        return (self.pos + step) % SIDE

    def put(self, src, dst, step, index):
        descriptor = remote(src, dst, self.send.at[index], self.recv.at[index], along(self.axis, step, *self.place))
        descriptor.start()
        self.started.append(descriptor)

    def wait(self, dst, index):
        device = along(self.axis, 1, *self.place)
        remote(dst, dst, self.send.at[index], self.recv.at[index], device).wait_recv()

    def finish(self):
        for descriptor in self.started:
            descriptor.wait_send()


class RingSum(Ring):
    def __init__(self, axis, pos, place, src, far, near, send, recv):
        super().__init__(axis, pos, place, send, recv)
        self.src, self.far, self.near = src, far, near

    def first(self, sets):
        for d, view, index in sets:
            self.put(self.src.at[(self.q(2),) + view], self.far.at[view], d, (index, 0))
        for d, view, index in sets:
            self.put(self.src.at[(self.q(SIDE - d),) + view], self.near.at[(d // 2,) + view], SIDE - d, (index, 1))

    def wait_far(self, view, index):
        self.wait(self.far.at[view], (index, 0))

    def second(self, d, view, index):
        total = self.src[(self.q(d),) + view].astype(F32) + self.far[view].astype(F32)
        self.src[(self.q(d),) + view] = total.astype(BF16)
        self.put(self.src.at[(self.q(d),) + view], self.near.at[(1 - d // 2,) + view], d, (index, 2))

    def wait_near(self, d, view, index):
        self.wait(self.near.at[(d // 2,) + view], (index, 1))

    def wait_sum(self, d, view, index):
        self.wait(self.near.at[(1 - d // 2,) + view], (index, 2))

    def total(self, view):
        own = self.src[(self.pos,) + view].astype(F32)
        return own + self.near[(0,) + view].astype(F32) + self.near[(1,) + view].astype(F32)


class RingGather(Ring):
    def __init__(self, axis, pos, place, buf, send, recv):
        super().__init__(axis, pos, place, send, recv)
        self.buf = buf

    def at(self, step, view):
        return self.buf.at[(self.q(step),) + view]

    def first(self, sets):
        for d, view, index in sets:
            self.put(self.at(0, view), self.at(0, view), d, (index, 0))
        for d, view, index in sets:
            self.put(self.at(0, view), self.at(0, view), SIDE - d, (index, 1))

    def second(self, d, view, index):
        self.wait(self.at(SIDE - d, view), (index, 0))
        self.put(self.at(SIDE - d, view), self.at(SIDE - d, view), d, (index, 2))

    def wait_near(self, d, view, index):
        self.wait(self.at(d, view), (index, 1))

    def wait_opposite(self, view, index):
        self.wait(self.at(2, view), (index, 2))


def reduce(
    scale, columns, lefts, projs, table, later,
    lefts_in, projs_in, table_in, cols, part, part_in, factors, blocks, far1, near1, summed, slots, far2, near2,
    pieces, grad, block_of,
    in_sem, col_sem, sib_send, sib_recv, part_send, part_recv, fac_send, fac_recv, swap_send, swap_recv,
    send1, recv1, send2, recv2, send3, recv3, own_sem,
):
    adapters, tokens, width = columns.shape
    rank = projs.shape[2]
    per_adapter = width // BW
    half = BW // NC
    group = rank // (2 * SIDE)
    slot_count = NX * NY * NC
    x, y, c, z = coords()
    sibling = at(x, y, 1 - c)
    mine = pl.ds(pl.multiple_of(c * tokens, tokens), tokens)
    theirs = pl.ds(pl.multiple_of((1 - c) * tokens, tokens), tokens)
    partners = plane_partners(x, y, c) + [{"mp": (z + step) % NZ} for step in range(1, NZ)]
    inputs = []
    for source, dest in ((projs, projs_in), (lefts, lefts_in), (table, table_in)):
        copy = pltpu.make_async_copy(source, dest, in_sem.at[len(inputs)])
        copy.start()
        inputs.append(copy)
    greet(partners)
    local, swapped, sends = [], [], []
    for j in range(per_adapter):
        lanes = pl.ds(pl.multiple_of(j * BW + c * half, half), half)
        keep = pltpu.make_async_copy(columns.at[:, :, lanes], cols.at[j, :, mine], col_sem.at[j])
        keep.start()
        local.append(keep)

    def partial(a):
        return lax.dot_general(projs_in[a], lefts_in[a], (((0,), (0,)), ((), ())), preferred_element_type=F32)

    inputs[0].wait()
    inputs[1].wait()
    for step in (2, 1, 3):
        part[step - 1] = partial((z + step) % NZ).astype(BF16)
    own = partial(z)
    await_partners(partners)

    for step in (2, 1, 3):
        copy = remote(
            part.at[step - 1], part_in.at[step - 1], part_send.at[step - 1], part_recv.at[step - 1],
            {"mp": (z + step) % NZ},
        )
        copy.start()
        sends.append(copy)

    for j in range(per_adapter):
        lanes = pl.ds(pl.multiple_of(j * BW + (1 - c) * half, half), half)
        swap = remote(columns.at[:, :, lanes], cols.at[j, :, mine], sib_send.at[j], sib_recv.at[j], sibling)
        swap.start()
        sends.append(swap)
        swapped.append(remote(cols.at[j, :, theirs], cols.at[j, :, theirs], sib_send.at[j], sib_recv.at[j], sibling))

    for copy in later:
        copy.start()
    total = own
    for step in (1, 3, 2):
        remote(
            part_in.at[step - 1], part_in.at[step - 1], part_send.at[step - 1], part_recv.at[step - 1], sibling
        ).wait_recv()
        total += part_in[step - 1].astype(F32)
    factors[z, c] = total.astype(BF16)

    def factor_view(a, part):
        return factors.at[a, c] if part is None else factors.at[a, c, pl.ds(part * (rank // 2), rank // 2)]

    def send_factor(a, part, step, index):
        view = factor_view(a, part)
        copy = remote(view, view, fac_send.at[index], fac_recv.at[index], {"mp": (z + step) % NZ})
        copy.start()
        sends.append(copy)

    def wait_factor(a, part, index):
        view = factor_view(a, part)
        remote(view, view, fac_send.at[index], fac_recv.at[index], sibling).wait_recv()

    send_factor(z, None, 1, 0)
    send_factor(z, None, 3, 2)

    place = (x, y, c)
    ring1 = [
        RingSum(o, place[o], place, blocks.at[o], far1.at[o], near1.at[o], send1.at[o], recv1.at[o]) for o in range(2)
    ]
    parts = range(2)
    tall = group // 2
    items, way = [], (1, 3, 1, 3)
    for t, step in enumerate(ORDER):
        a = (z + step) % NZ
        view = factors.at[a, c]
        if step == 1:
            wait_factor(a, None, 2)
            send_factor(a, 1, 3, 3)
        if step == 3:
            wait_factor(a, None, 0)
            send_factor(a, 0, 1, 1)
        if step == 2:
            wait_factor(a, 0, 1)
            wait_factor(a, 1, 3)
        swap = remote(view, view, swap_send.at[t], swap_recv.at[t], sibling)
        swap.start()
        sends.append(swap)
        other = factors.at[a, 1 - c]
        remote(other, other, swap_send.at[t], swap_recv.at[t], sibling).wait_recv()
        if t == 0:
            for j in range(per_adapter):
                local[j].wait()
                swapped[j].wait_recv()
        factor = jnp.concatenate([factors[a, 0], factors[a, 1]], axis=1)

        def block(j, carry):
            product = lax.dot_general(
                factor, cols[j, a], (((1,), (0,)), ((), ())), preferred_element_type=F32
            ).astype(BF16)
            for o in range(2):
                for q in range(SIDE):
                    for h in parts:
                        low = (o * SIDE + q) * group + h * tall
                        blocks[o, q, h, a * per_adapter + j] = product[low : low + tall]
            return carry

        lax.fori_loop(0, per_adapter, block, 0)
        items.append(pl.ds(a * per_adapter, per_adapter))
        for o in range(2):
            ring1[o].first([(way[t], (slice(None), items[t]), 4 * t)])

    empty = adapters * per_adapter

    def find(s, carry):
        found = jnp.int32(empty)
        for k in range(adapters * per_adapter):
            found = jnp.where(table_in[0, k] == s, jnp.int32(k), found)
        block_of[s] = found
        return carry

    inputs[2].wait()
    lax.fori_loop(0, slot_count, find, 0)

    for o in range(2):
        for h in parts:
            summed[o, empty, h] = jnp.zeros(summed.shape[3:], BF16)
    for h in parts:
        for t in range(adapters):
            for o in range(2):
                if h == 0:
                    ring1[o].wait_far((slice(None), items[t]), 4 * t)
                ring1[o].second(way[t], (h, items[t]), 4 * t + h)

    ring2 = [
        RingSum(1 - o, place[1 - o], place, slots.at[o], far2.at[o], near2.at[o], send2.at[o], recv2.at[o])
        for o in range(2)
    ]
    sets = ((1, pl.ds(0, SIDE)), (3, pl.ds(SIDE, SIDE)))
    for h in parts:
        for t in range(adapters):
            for o in range(2):
                if h == 0:
                    ring1[o].wait_near(way[t], (slice(None), items[t]), 4 * t)
                ring1[o].wait_sum(way[t], (h, items[t]), 4 * t + h)
                summed[o, items[t], h] = ring1[o].total((h, items[t])).astype(BF16)
        for step in (2, 1, 3, 0):
            for o in range(2):
                dest = ring2[o].q(step)
                for j in range(SIDE * NC):
                    s = (j // NC) * (NY * NC) + dest * NC + j % NC if o == 0 else dest * (NY * NC) + j
                    slots[o, dest, h, j] = summed[o, block_of[s], h]
        for o in range(2):
            ring2[o].first([(d, (h, some), 2 * h + n) for n, (d, some) in enumerate(sets)])
    for h in parts:
        for o in range(2):
            for n, (d, some) in enumerate(sets):
                ring2[o].wait_far((h, some), 2 * h + n)
                ring2[o].second(d, (h, some), 2 * h + n)

    def target(o, step, core):
        return at((x + step) % NX, y, (c + core) % NC) if o == 0 else at(x, (y + step) % NY, (c + core) % NC)

    def spot(o, step, core):
        q, lane = (place[o] + step) % SIDE, (c + core) % NC
        return grad.at[
            pl.ds(pl.multiple_of((o * SIDE + q) * group, group), group), pl.ds(pl.multiple_of(lane * half, half), half)
        ]

    owned = []
    for o in range(2):
        for h in parts:
            for n, (d, some) in enumerate(sets):
                ring2[o].wait_near(d, (h, some), 2 * h + n)
                ring2[o].wait_sum(d, (h, some), 2 * h + n)
            pieces[o, :, pl.ds(h * tall, tall)] = (ring2[o].total((h,)) * scale).astype(BF16)
        for step in (2, 1, 3, 0):
            for core in range(NC):
                source = pieces.at[o, ((place[o] + step) % SIDE) * NC + (c + core) % NC]
                if step == 0 and core == 0:
                    copy = pltpu.make_async_copy(source, spot(o, 0, 0), own_sem.at[o])
                    copy.start()
                    owned.append(copy)
                else:
                    index = step * NC + core
                    copy = remote(source, spot(o, 0, 0), send3.at[o, index], recv3.at[o, index], target(o, step, core))
                    copy.start()
                    sends.append(copy)
    for o in range(2):
        for step in range(SIDE):
            for core in range(NC):
                if step or core:
                    index = step * NC + core
                    view = spot(o, SIDE - step, NC - core)
                    remote(view, view, send3.at[o, index], recv3.at[o, index], sibling).wait_recv()
    for copy in owned:
        copy.wait()
    return sends + [copy for ring in ring1 + ring2 for copy in ring.started]


def newton_polynomial():
    terms = [0.25 * math.comb(5, i) * 1.25 ** (5 - i) * (-0.25) ** i for i in range(6)]
    terms[0] += 1.25 * 0.25
    return terms


def dot16(a, b):
    return jnp.dot(a, b, preferred_element_type=F32)


def root_steps(stat, square, renew, old, out, n1, n2, n3, u, v, w):
    size = stat.shape[0]
    width = min(size, 256)
    tiles = [pl.ds(low, width) for low in range(0, size, width)]
    inverse = lax.rsqrt(square + EPSILON)
    u1, u2, u3, u4, u5, u6 = newton_polynomial()
    for tile in tiles:
        n1[:, tile] = (stat[:, tile] * inverse).astype(BF16)
    yield
    for tile in tiles:
        n2[:, tile] = dot16(n1[...], n1[:, tile]).astype(BF16)
        yield
    for tile in tiles:
        value = dot16(n1[...], n2[:, tile])
        n3[:, tile] = value.astype(BF16)
        second, first = n2[:, tile].astype(F32), n1[:, tile].astype(F32)
        v[:, tile] = (u4 * first + u5 * second + u6 * value).astype(BF16)
        u[:, tile] = (u1 * first + u2 * second + u3 * value).astype(BF16)
        yield
    for tile in tiles:
        w[:, tile] = (u[:, tile].astype(F32) + dot16(n3[...], v[:, tile])).astype(BF16)
        yield
    for tile in tiles:
        value = w[:, tile]
        n2[:, tile] = (dot16(w[...], value) - 3.125 * value.astype(F32)).astype(BF16)
        yield
    for tile in tiles:
        value = n2[:, tile]
        v[:, tile] = (dot16(n2[...], value) + (2 * 1.5625**2) * value.astype(F32)).astype(BF16)
        n3[:, tile] = (1.5625 * n1[:, tile].astype(F32) - dot16(w[...], n1[:, tile])).astype(BF16)
        yield
    scale = jnp.sqrt(jnp.sqrt(inverse))
    for low, tile in zip(range(0, size, width), tiles):
        value = n3[:, tile]
        last = 1.25 * w[:, tile].astype(F32) + (0.25 * 1.5625**4) * value.astype(F32) + 0.25 * dot16(v[...], value)
        row = lax.broadcasted_iota(jnp.int32, (size, width), 0)
        column = lax.broadcasted_iota(jnp.int32, (size, width), 1)
        eye = jnp.where(row == column + low, jnp.float32(1.25 * 1.5625), jnp.float32(0.0))
        out[:, tile] = jnp.where(renew, (eye - last) * scale, old[:, tile].astype(F32)).astype(BF16)
        yield


def precondition(
    loads, table, groups, grad, old_left, old_right, old_root_left, old_root_right,
    new_left, new_right, root_left, root_right, update, *scratch,
):
    rank, width = grad.shape
    for load in loads:
        load.wait()
    owner = lax.axis_index("dp")
    renew = jnp.int32(0)
    for k in range(table.shape[1]):
        named = jnp.where(table[0, k] == owner, jnp.int32(1), jnp.int32(0))
        renew += named * jnp.where(groups[0, k] == 0, jnp.int32(1), jnp.int32(0))
    renew = renew == 1
    transposed = (((0,), (0,)), ((), ()))
    across = (((1,), (1,)), ((), ()))
    value = grad[...]
    product = lax.dot_general(value, value, across, preferred_element_type=F32)
    fresh = 0.9 * old_left[...] + 0.1 * product
    new_left[...] = fresh
    left_square = jnp.sum(fresh * fresh)
    tile_width = min(width, 256)
    squares = jnp.zeros((1, tile_width), F32)
    for low in range(0, width, tile_width):
        tile = pl.ds(low, tile_width)
        product = lax.dot_general(value, grad[:, tile], transposed, preferred_element_type=F32)
        fresh = 0.9 * old_right[:, tile] + 0.1 * product
        new_right[:, tile] = fresh
        squares += jnp.sum(fresh * fresh, axis=0, keepdims=True)
    right_square = jnp.sum(squares)
    steps = [
        root_steps(new_right, right_square, renew, old_root_right, root_right, *scratch[6:]),
        root_steps(new_left, left_square, renew, old_root_left, root_left, *scratch[:6]),
    ]
    for _ in itertools.zip_longest(*steps):
        pass
    half_product = dot16(root_left[...], grad[...]).astype(BF16)
    direction = dot16(half_product, root_right[...])
    wide = grad[...].astype(F32)
    count = 1.0 / (rank * width)
    ratio = (jnp.sum(wide * wide) * count + EPSILON) / (jnp.sum(direction * direction) * count + EPSILON)
    update[...] = (direction * jnp.sqrt(ratio)).astype(BF16)


def gather(
    table, update, by_block, slots00, slots01, slots10, slots11,
    send1, recv1, send2, recv2, send3, recv3, swap_send, swap_recv, own_sem,
):
    rank, width = update.shape
    half, group = width // NC, rank // (2 * SIDE)
    adapters, per_adapter = by_block.shape[3:5]
    tall = group // 2
    parts = range(2)
    by_slot = ((slots00, slots01), (slots10, slots11))
    x, y, c, _ = coords()
    place = (x, y, c)
    sibling = at(x, y, 1 - c)
    sends = []

    def spot(o, h, step, core):
        return by_slot[o][h].at[place[1 - o], ((place[o] + step) % SIDE) * NC + (c + core) % NC]

    owned = []
    for h in parts:
        for step in (2, 1, 3, 0):
            for o in range(2):
                for core in range(NC):
                    q, lane = (place[o] + step) % SIDE, (c + core) % NC
                    source = update.at[
                        pl.ds(pl.multiple_of((o * SIDE + q) * group + h * tall, tall), tall),
                        pl.ds(pl.multiple_of(lane * half, half), half),
                    ]
                    if step == 0 and core == 0:
                        copy = pltpu.make_async_copy(source, spot(o, h, 0, 0), own_sem.at[o, h])
                        copy.start()
                        owned.append(copy)
                    else:
                        index = (o, h, step * NC + core)
                        device = at(q, y, lane) if o == 0 else at(x, q, lane)
                        copy = remote(source, spot(o, h, 0, 0), send1.at[index], recv1.at[index], device)
                        copy.start()
                        sends.append(copy)

    slot_sets = ((1, pl.ds(0, SIDE)), (3, pl.ds(SIDE, SIDE)))
    ring2 = [
        [RingGather(1 - o, place[1 - o], place, by_slot[o][h], send2.at[o, h], recv2.at[o, h]) for h in parts]
        for o in range(2)
    ]
    for h in parts:
        for o in range(2):
            owned[2 * h + o].wait()
            for step in range(SIDE):
                for core in range(NC):
                    if step or core:
                        index = (o, h, step * NC + core)
                        view = spot(o, h, SIDE - step, NC - core)
                        remote(view, view, send1.at[index], recv1.at[index], sibling).wait_recv()
            ring2[o][h].first([(d, (some,), n) for n, (d, some) in enumerate(slot_sets)])
    for h in parts:
        for o in range(2):
            for n, (d, some) in enumerate(slot_sets):
                ring2[o][h].second(d, (some,), n)

    ring1 = [RingGather(o, place[o], place, by_block.at[o, :, c], send3.at[o], recv3.at[o]) for o in range(2)]

    def view_of(h, some):
        return (some, slice(None), pl.ds(h * tall, tall))

    sets = ((1, pl.ds(0, adapters // 2)), (3, pl.ds(adapters // 2, adapters // 2)))

    def pass_on(o, step, h, n):
        view = by_block.at[(o, (place[o] + step) % SIDE, c) + view_of(h, sets[n][1])]
        index = (o, step, 2 * h + n)
        copy = remote(view, view, swap_send.at[index], swap_recv.at[index], sibling)
        copy.start()
        sends.append(copy)

    for h in parts:
        for o in range(2):
            for n, (d, some) in enumerate(slot_sets):
                ring2[o][h].wait_near(d, (some,), n)
                ring2[o][h].wait_opposite((some,), n)
            for a in range(adapters):
                for j in range(per_adapter):
                    s = table[0, a * per_adapter + j]
                    if o == 0:
                        row, item = (s // NC) % NY, (s // (NY * NC)) * NC + s % NC
                    else:
                        row, item = s // (NY * NC), s % (NY * NC)
                    by_block[o, place[o], c, a, j, pl.ds(h * tall, tall)] = by_slot[o][h][row, item]
            ring1[o].first([(d, view_of(h, some), 2 * h + n) for n, (d, some) in enumerate(sets)])
        for o in range(2):
            for n in range(2):
                pass_on(o, 0, h, n)
    for h in parts:
        for o in range(2):
            for n, (d, some) in enumerate(sets):
                ring1[o].second(d, view_of(h, some), 2 * h + n)
                pass_on(o, SIDE - d, h, n)
        for o in range(2):
            for n, (d, some) in enumerate(sets):
                ring1[o].wait_near(d, view_of(h, some), 2 * h + n)
                pass_on(o, d, h, n)
    for h in parts:
        for o in range(2):
            for n, (d, some) in enumerate(sets):
                ring1[o].wait_opposite(view_of(h, some), 2 * h + n)
                pass_on(o, 2, h, n)
    for o in range(2):
        for step in range(SIDE):
            for h in parts:
                for n in range(2):
                    view = by_block.at[(o, (place[o] + step) % SIDE, 1 - c) + view_of(h, sets[n][1])]
                    index = (o, step, 2 * h + n)
                    remote(view, view, swap_send.at[index], swap_recv.at[index], sibling).wait_recv()
    return sends + [copy for ring in ring1 + ring2[0] + ring2[1] for copy in ring.started]


REDUCE, PRECONDITION = 34, 17


def step_kernel(
    scale, columns, lefts, projs, table, groups, left_stat, right_stat, left_root, right_root,
    new_left, new_right, root_left, root_right, parts, groups_in, load_sem, *scratch,
):
    for_reduce, rest = scratch[:REDUCE], scratch[REDUCE:]
    (old_left, old_right, old_root_left, old_root_right, update), rest = rest[:5], rest[5:]
    for_roots, for_gather = rest[:12], rest[12:]
    table_in, grad = for_reduce[2], for_reduce[15]
    loads = [
        pltpu.make_async_copy(source, dest, load_sem.at[n])
        for n, (source, dest) in enumerate(
            (
                (left_stat.at[0, 0], old_left),
                (right_stat.at[0, 0], old_right),
                (left_root.at[0, 0], old_root_left),
                (right_root.at[0, 0], old_root_right),
                (groups, groups_in),
            )
        )
    ]
    started = reduce(scale, columns, lefts, projs, table, loads, *for_reduce)
    precondition(
        loads, table_in, groups_in, grad, old_left, old_right, old_root_left, old_root_right,
        new_left, new_right, root_left, root_right, update, *for_roots,
    )
    started += gather(table_in, update, parts, *for_gather)
    for copy in started:
        copy.wait_send()


def whole_step(columns, lefts, projs, table, groups, left_stats, right_stats, left_roots, right_roots, scale):
    adapters, tokens, width = columns.shape
    rank = projs.shape[2]
    per_adapter = width // BW
    count = adapters * per_adapter
    half, group, pair = BW // NC, rank // (2 * SIDE), SIDE * NC
    tall = group // 2
    dma = lambda *shape: pltpu.SemaphoreType.DMA(shape)
    vmem = lambda *shape, kind=BF16: pltpu.VMEM(shape, kind)
    for_reduce = [
        vmem(*lefts.shape),
        vmem(*projs.shape),
        pltpu.SMEM(table.shape, jnp.int32),
        vmem(per_adapter, adapters, NC * tokens, half),
        vmem(NZ - 1, rank, tokens),
        vmem(NZ - 1, rank, tokens),
        vmem(adapters, NC, rank, tokens),
        vmem(2, SIDE, 2, count, tall, half),
        vmem(2, 2, count, tall, half),
        vmem(2, 2, 2, count, tall, half),
        vmem(2, count + 1, 2, tall, half),
        vmem(2, SIDE, 2, pair, tall, half),
        vmem(2, 2, pair, tall, half),
        vmem(2, 2, 2, pair, tall, half),
        vmem(2, pair, group, half),
        vmem(rank, BW),
        pltpu.SMEM((NX * NY * NC,), jnp.int32),
        dma(3),
        dma(per_adapter),
        dma(per_adapter),
        dma(per_adapter),
        dma(NZ - 1),
        dma(NZ - 1),
        dma(NZ),
        dma(NZ),
        dma(adapters),
        dma(adapters),
        dma(2, 4 * adapters, 3),
        dma(2, 4 * adapters, 3),
        dma(2, 4, 3),
        dma(2, 4, 3),
        dma(2, pair),
        dma(2, pair),
        dma(2),
    ]
    for_roots = [
        vmem(rank, rank, kind=F32),
        vmem(BW, BW, kind=F32),
        vmem(rank, rank),
        vmem(BW, BW),
        vmem(rank, BW),
    ]
    for_roots += [vmem(rank, rank)] * 6 + [vmem(BW, BW)] * 6
    for_gather = [vmem(SIDE, pair, tall, half)] * 4
    for_gather += [
        dma(2, 2, pair),
        dma(2, 2, pair),
        dma(2, 2, 2, 3),
        dma(2, 2, 2, 3),
        dma(2, 4, 3),
        dma(2, 4, 3),
        dma(2, SIDE, 4),
        dma(2, SIDE, 4),
        dma(2, 2),
    ]
    assert len(for_reduce) == REDUCE and len(for_roots) == PRECONDITION
    hbm, in_vmem = pl.BlockSpec(memory_space=pl.ANY), pl.BlockSpec(memory_space=pltpu.VMEM)
    return pl.pallas_call(
        functools.partial(step_kernel, scale),
        out_shape=(
            pltpu.VMEM((rank, rank), F32),
            pltpu.VMEM((BW, BW), F32),
            pltpu.VMEM((rank, rank), BF16),
            pltpu.VMEM((BW, BW), BF16),
            pltpu.VMEM((2, SIDE, NC, adapters, per_adapter, group, half), BF16),
        ),
        in_specs=[hbm] * 9,
        out_specs=(in_vmem,) * 5,
        scratch_shapes=[pltpu.SMEM(groups.shape, jnp.int32), dma(5)] + for_reduce + for_roots + for_gather,
        compiler_params=pltpu.CompilerParams(
            collective_id=0, has_side_effects=True, vmem_limit_bytes=53477376
        ),
        name="whole_step",
    )(columns, lefts, projs, table, groups, left_stats, right_stats, left_roots, right_roots)


def place_kernel(
    new_left, new_right, root_left, root_right, parts,
    new_left_out, new_right_out, root_left_out, root_right_out, out, sem,
):
    per_adapter, group, half = parts.shape[4:]
    moves = []
    for o in range(2):
        for q in range(SIDE):
            for c in range(NC):
                for j in range(per_adapter):
                    rows, lanes = pl.ds((o * SIDE + q) * group, group), pl.ds(j * BW + c * half, half)
                    moves.append((parts.at[o, q, c, :, j], out.at[:, rows, lanes]))
    moves += [
        (new_left, new_left_out.at[0, 0]),
        (new_right, new_right_out.at[0, 0]),
        (root_left, root_left_out.at[0, 0]),
        (root_right, root_right_out.at[0, 0]),
    ]
    copies = [pltpu.make_async_copy(source, dest, sem.at[n]) for n, (source, dest) in enumerate(moves)]
    for copy in copies:
        copy.start()
    for copy in copies:
        copy.wait()


def placed(new_left, new_right, root_left, root_right, parts):
    _, _, _, adapters, per_adapter, group, _ = parts.shape
    stacked = lambda a: jax.ShapeDtypeStruct((1, 1) + a.shape, a.dtype)
    return pl.pallas_call(
        place_kernel,
        out_shape=(
            stacked(new_left), stacked(new_right), stacked(root_left), stacked(root_right),
            jax.ShapeDtypeStruct((adapters, 2 * SIDE * group, per_adapter * BW), BF16),
        ),
        in_specs=[pl.BlockSpec(memory_space=pltpu.VMEM)] * 5,
        out_specs=(pl.BlockSpec(memory_space=pl.ANY),) * 5,
        scratch_shapes=[pltpu.SemaphoreType.DMA((2 * SIDE * NC * per_adapter + 4,))],
        compiler_params=pltpu.CompilerParams(vmem_limit_bytes=16 * 2**20),
        name="placed",
    )(new_left, new_right, root_left, root_right, parts)


def body(
    columns,
    lefts,
    projs,
    slot_table,
    refresh_group,
    left_stats,
    right_stats,
    left_roots,
    right_roots,
):
    total_tokens = lax.axis_size("dp") * columns.shape[1]
    results = whole_step(
        columns, jnp.swapaxes(lefts, 1, 2), projs, slot_table, refresh_group,
        left_stats, right_stats, left_roots, right_roots, 1.0 / math.sqrt(total_tokens),
    )
    return placed(*results)


def solution(mesh):
    shardings = (
        P(None, "dp", "mp"),
        P(None, "dp", "mp"),
        P(None, "mp", None),
        P("mp", None),
        P("mp", None),
        P("mp", "dp", None, None),
        P("mp", "dp", None, None),
        P("mp", "dp", None, None),
        P("mp", "dp", None, None),
    )
    return jax.shard_map(
        body,
        mesh=mesh,
        in_specs=shardings,
        out_specs=(
            P("mp", "dp", None, None),
            P("mp", "dp", None, None),
            P("mp", "dp", None, None),
            P("mp", "dp", None, None),
            P(None, None, "mp"),
        ),
        check_vma=False,
    )
```

```python
import functools
import itertools
import math

import jax
import jax.numpy as jnp
from jax import lax
from jax.experimental import pallas as pl
from jax.experimental.pallas import tpu as pltpu
from jax.sharding import PartitionSpec as P

BW = 768
EPSILON = 1e-06
NX, NY, NC, NZ = 4, 4, 2, 4
SIDE = 4
ORDER = (0, 1, 3, 2)
MESH = pl.DeviceIdType.MESH
F32, BF16 = jnp.float32, jnp.bfloat16


def coords():
    dp = lax.axis_index("dp")
    return dp // (NY * NC), (dp // NC) % NY, dp % NC, lax.axis_index("mp")


def at(x, y, c):
    return {"dp": (x * NY + y) * NC + c}


def along(axis, step, x, y, c):
    return at((x + step) % NX, y, c) if axis == 0 else at(x, (y + step) % NY, c)


def remote(src, dst, send, recv, device):
    return pltpu.make_async_remote_copy(
        src_ref=src, dst_ref=dst, send_sem=send, recv_sem=recv, device_id=device, device_id_type=MESH
    )


def plane_partners(x, y, c):
    partners = [at(x, y, 1 - c)]
    for step in range(1, SIDE):
        for core in range(NC):
            partners.append(at((x + step) % NX, y, (c + core) % NC))
            partners.append(at(x, (y + step) % NY, (c + core) % NC))
    return partners


def greet(partners):
    barrier = pltpu.get_barrier_semaphore()
    for partner in partners:
        pl.semaphore_signal(barrier, inc=1, device_id=partner, device_id_type=MESH)


def await_partners(partners):
    pl.semaphore_wait(pltpu.get_barrier_semaphore(), len(partners))


class Ring:
    def __init__(self, axis, pos, place, send, recv):
        self.axis, self.pos, self.place, self.send, self.recv = axis, pos, place, send, recv
        self.started = []

    def q(self, step):
        return (self.pos + step) % SIDE

    def put(self, src, dst, step, index):
        descriptor = remote(src, dst, self.send.at[index], self.recv.at[index], along(self.axis, step, *self.place))
        descriptor.start()
        self.started.append(descriptor)

    def wait(self, dst, index):
        device = along(self.axis, 1, *self.place)
        remote(dst, dst, self.send.at[index], self.recv.at[index], device).wait_recv()

    def finish(self):
        for descriptor in self.started:
            descriptor.wait_send()


class RingSum(Ring):
    def __init__(self, axis, pos, place, src, far, near, send, recv):
        super().__init__(axis, pos, place, send, recv)
        self.src, self.far, self.near = src, far, near

    def first(self, sets):
        for d, view, index in sets:
            self.put(self.src.at[(self.q(2),) + view], self.far.at[view], d, (index, 0))
        for d, view, index in sets:
            self.put(self.src.at[(self.q(SIDE - d),) + view], self.near.at[(d // 2,) + view], SIDE - d, (index, 1))

    def wait_far(self, view, index):
        self.wait(self.far.at[view], (index, 0))

    def second(self, d, view, index):
        total = self.src[(self.q(d),) + view].astype(F32) + self.far[view].astype(F32)
        self.src[(self.q(d),) + view] = total.astype(BF16)
        self.put(self.src.at[(self.q(d),) + view], self.near.at[(1 - d // 2,) + view], d, (index, 2))

    def wait_near(self, d, view, index):
        self.wait(self.near.at[(d // 2,) + view], (index, 1))

    def wait_sum(self, d, view, index):
        self.wait(self.near.at[(1 - d // 2,) + view], (index, 2))

    def total(self, view):
        own = self.src[(self.pos,) + view].astype(F32)
        return own + self.near[(0,) + view].astype(F32) + self.near[(1,) + view].astype(F32)


class RingGather(Ring):
    def __init__(self, axis, pos, place, buf, send, recv):
        super().__init__(axis, pos, place, send, recv)
        self.buf = buf

    def at(self, step, view):
        return self.buf.at[(self.q(step),) + view]

    def first(self, sets):
        for d, view, index in sets:
            self.put(self.at(0, view), self.at(0, view), d, (index, 0))
        for d, view, index in sets:
            self.put(self.at(0, view), self.at(0, view), SIDE - d, (index, 1))

    def second(self, d, view, index):
        self.wait(self.at(SIDE - d, view), (index, 0))
        self.put(self.at(SIDE - d, view), self.at(SIDE - d, view), d, (index, 2))

    def wait_near(self, d, view, index):
        self.wait(self.at(d, view), (index, 1))

    def wait_opposite(self, view, index):
        self.wait(self.at(2, view), (index, 2))


def reduce(
    scale, columns, lefts, projs, table, later,
    lefts_in, projs_in, table_in, cols, part, part_in, factors, blocks, far1, near1, summed, slots, far2, near2,
    pieces, grad, block_of,
    in_sem, col_sem, sib_send, sib_recv, part_send, part_recv, fac_send, fac_recv, swap_send, swap_recv,
    send1, recv1, send2, recv2, send3, recv3, own_sem,
):
    adapters, tokens, width = columns.shape
    rank = projs.shape[2]
    per_adapter = width // BW
    half = BW // NC
    group = rank // (2 * SIDE)
    slot_count = NX * NY * NC
    x, y, c, z = coords()
    sibling = at(x, y, 1 - c)
    mine = pl.ds(pl.multiple_of(c * tokens, tokens), tokens)
    theirs = pl.ds(pl.multiple_of((1 - c) * tokens, tokens), tokens)
    partners = plane_partners(x, y, c) + [{"mp": (z + step) % NZ} for step in range(1, NZ)]
    inputs = []
    for source, dest in ((projs, projs_in), (lefts, lefts_in), (table, table_in)):
        copy = pltpu.make_async_copy(source, dest, in_sem.at[len(inputs)])
        copy.start()
        inputs.append(copy)
    greet(partners)
    local, swapped, sends = [], [], []
    for j in range(per_adapter):
        lanes = pl.ds(pl.multiple_of(j * BW + c * half, half), half)
        keep = pltpu.make_async_copy(columns.at[:, :, lanes], cols.at[j, :, mine], col_sem.at[j])
        keep.start()
        local.append(keep)

    def partial(a):
        return lax.dot_general(projs_in[a], lefts_in[a], (((0,), (0,)), ((), ())), preferred_element_type=F32)

    inputs[0].wait()
    inputs[1].wait()
    for step in (2, 1, 3):
        part[step - 1] = partial((z + step) % NZ).astype(BF16)
        if step == 2:
            await_partners(partners)
        copy = remote(
            part.at[step - 1], part_in.at[step - 1], part_send.at[step - 1], part_recv.at[step - 1],
            {"mp": (z + step) % NZ},
        )
        copy.start()
        sends.append(copy)

    for j in range(per_adapter):
        lanes = pl.ds(pl.multiple_of(j * BW + (1 - c) * half, half), half)
        swap = remote(columns.at[:, :, lanes], cols.at[j, :, mine], sib_send.at[j], sib_recv.at[j], sibling)
        swap.start()
        sends.append(swap)
        swapped.append(remote(cols.at[j, :, theirs], cols.at[j, :, theirs], sib_send.at[j], sib_recv.at[j], sibling))

    total = partial(z)
    for step in (1, 3, 2):
        remote(
            part_in.at[step - 1], part_in.at[step - 1], part_send.at[step - 1], part_recv.at[step - 1], sibling
        ).wait_recv()
        total += part_in[step - 1].astype(F32)
    factors[z, c] = total.astype(BF16)

    def factor_view(a, part):
        return factors.at[a, c] if part is None else factors.at[a, c, pl.ds(part * (rank // 2), rank // 2)]

    def send_factor(a, part, step, index):
        view = factor_view(a, part)
        copy = remote(view, view, fac_send.at[index], fac_recv.at[index], {"mp": (z + step) % NZ})
        copy.start()
        sends.append(copy)

    def wait_factor(a, part, index):
        view = factor_view(a, part)
        remote(view, view, fac_send.at[index], fac_recv.at[index], sibling).wait_recv()

    send_factor(z, None, 1, 0)
    send_factor(z, None, 3, 2)

    place = (x, y, c)
    ring1 = [
        RingSum(o, place[o], place, blocks.at[o], far1.at[o], near1.at[o], send1.at[o], recv1.at[o]) for o in range(2)
    ]
    parts = range(2)
    tall = group // 2
    items, way = [], (1, 3, 1, 3)
    for t, step in enumerate(ORDER):
        a = (z + step) % NZ
        view = factors.at[a, c]
        if step == 1:
            wait_factor(a, None, 2)
            send_factor(a, 1, 3, 3)
        if step == 3:
            wait_factor(a, None, 0)
            send_factor(a, 0, 1, 1)
        if step == 2:
            wait_factor(a, 0, 1)
            wait_factor(a, 1, 3)
        swap = remote(view, view, swap_send.at[t], swap_recv.at[t], sibling)
        swap.start()
        sends.append(swap)
        other = factors.at[a, 1 - c]
        remote(other, other, swap_send.at[t], swap_recv.at[t], sibling).wait_recv()
        if t == 0:
            for j in range(per_adapter):
                local[j].wait()
                swapped[j].wait_recv()
        factor = jnp.concatenate([factors[a, 0], factors[a, 1]], axis=1)

        def block(j, carry):
            product = lax.dot_general(
                factor, cols[j, a], (((1,), (0,)), ((), ())), preferred_element_type=F32
            ).astype(BF16)
            for o in range(2):
                for q in range(SIDE):
                    for h in parts:
                        low = (o * SIDE + q) * group + h * tall
                        blocks[o, q, h, a * per_adapter + j] = product[low : low + tall]
            return carry

        lax.fori_loop(0, per_adapter, block, 0)
        items.append(pl.ds(a * per_adapter, per_adapter))
        for o in range(2):
            ring1[o].first([(way[t], (slice(None), items[t]), 4 * t)])

    for copy in later:
        copy.start()

    empty = adapters * per_adapter

    def find(s, carry):
        found = jnp.int32(empty)
        for k in range(adapters * per_adapter):
            found = jnp.where(table_in[0, k] == s, jnp.int32(k), found)
        block_of[s] = found
        return carry

    inputs[2].wait()
    lax.fori_loop(0, slot_count, find, 0)

    for o in range(2):
        for h in parts:
            summed[o, empty, h] = jnp.zeros(summed.shape[3:], BF16)
    for h in parts:
        for t in range(adapters):
            for o in range(2):
                if h == 0:
                    ring1[o].wait_far((slice(None), items[t]), 4 * t)
                ring1[o].second(way[t], (h, items[t]), 4 * t + h)

    ring2 = [
        RingSum(1 - o, place[1 - o], place, slots.at[o], far2.at[o], near2.at[o], send2.at[o], recv2.at[o])
        for o in range(2)
    ]
    sets = ((1, pl.ds(0, SIDE)), (3, pl.ds(SIDE, SIDE)))
    for h in parts:
        for t in range(adapters):
            for o in range(2):
                if h == 0:
                    ring1[o].wait_near(way[t], (slice(None), items[t]), 4 * t)
                ring1[o].wait_sum(way[t], (h, items[t]), 4 * t + h)
                summed[o, items[t], h] = ring1[o].total((h, items[t])).astype(BF16)
        for step in (2, 1, 3, 0):
            for o in range(2):
                dest = ring2[o].q(step)
                for j in range(SIDE * NC):
                    s = (j // NC) * (NY * NC) + dest * NC + j % NC if o == 0 else dest * (NY * NC) + j
                    slots[o, dest, h, j] = summed[o, block_of[s], h]
        for o in range(2):
            ring2[o].first([(d, (h, some), 2 * h + n) for n, (d, some) in enumerate(sets)])
    for h in parts:
        for o in range(2):
            for n, (d, some) in enumerate(sets):
                ring2[o].wait_far((h, some), 2 * h + n)
                ring2[o].second(d, (h, some), 2 * h + n)

    def target(o, step, core):
        return at((x + step) % NX, y, (c + core) % NC) if o == 0 else at(x, (y + step) % NY, (c + core) % NC)

    def spot(o, step, core):
        q, lane = (place[o] + step) % SIDE, (c + core) % NC
        return grad.at[
            pl.ds(pl.multiple_of((o * SIDE + q) * group, group), group), pl.ds(pl.multiple_of(lane * half, half), half)
        ]

    owned = []
    for o in range(2):
        for h in parts:
            for n, (d, some) in enumerate(sets):
                ring2[o].wait_near(d, (h, some), 2 * h + n)
                ring2[o].wait_sum(d, (h, some), 2 * h + n)
            pieces[o, :, pl.ds(h * tall, tall)] = (ring2[o].total((h,)) * scale).astype(BF16)
        for step in (2, 1, 3, 0):
            for core in range(NC):
                source = pieces.at[o, ((place[o] + step) % SIDE) * NC + (c + core) % NC]
                if step == 0 and core == 0:
                    copy = pltpu.make_async_copy(source, spot(o, 0, 0), own_sem.at[o])
                    copy.start()
                    owned.append(copy)
                else:
                    index = step * NC + core
                    copy = remote(source, spot(o, 0, 0), send3.at[o, index], recv3.at[o, index], target(o, step, core))
                    copy.start()
                    sends.append(copy)
    for o in range(2):
        for step in range(SIDE):
            for core in range(NC):
                if step or core:
                    index = step * NC + core
                    view = spot(o, SIDE - step, NC - core)
                    remote(view, view, send3.at[o, index], recv3.at[o, index], sibling).wait_recv()
    for copy in owned:
        copy.wait()
    return sends + [copy for ring in ring1 + ring2 for copy in ring.started]


def newton_polynomial():
    terms = [0.25 * math.comb(5, i) * 1.25 ** (5 - i) * (-0.25) ** i for i in range(6)]
    terms[0] += 1.25 * 0.25
    return terms


def dot16(a, b):
    return jnp.dot(a, b, preferred_element_type=F32)


def root_steps(stat, square, renew, old, out, n1, n2, n3, u, v, w):
    size = stat.shape[0]
    width = min(size, 256)
    tiles = [pl.ds(low, width) for low in range(0, size, width)]
    inverse = lax.rsqrt(square + EPSILON)
    u1, u2, u3, u4, u5, u6 = newton_polynomial()
    for tile in tiles:
        n1[:, tile] = (stat[:, tile] * inverse).astype(BF16)
    yield
    for tile in tiles:
        n2[:, tile] = dot16(n1[...], n1[:, tile]).astype(BF16)
        yield
    for tile in tiles:
        value = dot16(n1[...], n2[:, tile])
        n3[:, tile] = value.astype(BF16)
        second, first = n2[:, tile].astype(F32), n1[:, tile].astype(F32)
        v[:, tile] = (u4 * first + u5 * second + u6 * value).astype(BF16)
        u[:, tile] = (u1 * first + u2 * second + u3 * value).astype(BF16)
        yield
    for tile in tiles:
        w[:, tile] = (u[:, tile].astype(F32) + dot16(n3[...], v[:, tile])).astype(BF16)
        yield
    for tile in tiles:
        value = w[:, tile]
        n2[:, tile] = (dot16(w[...], value) - 3.125 * value.astype(F32)).astype(BF16)
        yield
    for tile in tiles:
        value = n2[:, tile]
        v[:, tile] = (dot16(n2[...], value) + (2 * 1.5625**2) * value.astype(F32)).astype(BF16)
        n3[:, tile] = (1.5625 * n1[:, tile].astype(F32) - dot16(w[...], n1[:, tile])).astype(BF16)
        yield
    scale = jnp.sqrt(jnp.sqrt(inverse))
    for low, tile in zip(range(0, size, width), tiles):
        value = n3[:, tile]
        last = 1.25 * w[:, tile].astype(F32) + (0.25 * 1.5625**4) * value.astype(F32) + 0.25 * dot16(v[...], value)
        row = lax.broadcasted_iota(jnp.int32, (size, width), 0)
        column = lax.broadcasted_iota(jnp.int32, (size, width), 1)
        eye = jnp.where(row == column + low, jnp.float32(1.25 * 1.5625), jnp.float32(0.0))
        out[:, tile] = jnp.where(renew, (eye - last) * scale, old[:, tile].astype(F32)).astype(BF16)
        yield


def precondition(
    loads, table, groups, grad, old_left, old_right, old_root_left, old_root_right,
    new_left, new_right, root_left, root_right, update, *scratch,
):
    rank, width = grad.shape
    for load in loads:
        load.wait()
    owner = lax.axis_index("dp")
    renew = jnp.int32(0)
    for k in range(table.shape[1]):
        named = jnp.where(table[0, k] == owner, jnp.int32(1), jnp.int32(0))
        renew += named * jnp.where(groups[0, k] == 0, jnp.int32(1), jnp.int32(0))
    renew = renew == 1
    transposed = (((0,), (0,)), ((), ()))
    across = (((1,), (1,)), ((), ()))
    value = grad[...]
    product = lax.dot_general(value, value, across, preferred_element_type=F32)
    fresh = 0.9 * old_left[...] + 0.1 * product
    new_left[...] = fresh
    left_square = jnp.sum(fresh * fresh)
    tile_width = min(width, 256)
    squares = jnp.zeros((1, tile_width), F32)
    for low in range(0, width, tile_width):
        tile = pl.ds(low, tile_width)
        product = lax.dot_general(value, grad[:, tile], transposed, preferred_element_type=F32)
        fresh = 0.9 * old_right[:, tile] + 0.1 * product
        new_right[:, tile] = fresh
        squares += jnp.sum(fresh * fresh, axis=0, keepdims=True)
    right_square = jnp.sum(squares)
    steps = [
        root_steps(new_right, right_square, renew, old_root_right, root_right, *scratch[6:]),
        root_steps(new_left, left_square, renew, old_root_left, root_left, *scratch[:6]),
    ]
    for _ in itertools.zip_longest(*steps):
        pass
    half_product = dot16(root_left[...], grad[...]).astype(BF16)
    direction = dot16(half_product, root_right[...])
    wide = grad[...].astype(F32)
    count = 1.0 / (rank * width)
    ratio = (jnp.sum(wide * wide) * count + EPSILON) / (jnp.sum(direction * direction) * count + EPSILON)
    update[...] = (direction * jnp.sqrt(ratio)).astype(BF16)


def gather(
    table, update, by_block, slots00, slots01, slots10, slots11,
    send1, recv1, send2, recv2, send3, recv3, swap_send, swap_recv, own_sem,
):
    rank, width = update.shape
    half, group = width // NC, rank // (2 * SIDE)
    adapters, per_adapter = by_block.shape[3:5]
    tall = group // 2
    parts = range(2)
    by_slot = ((slots00, slots01), (slots10, slots11))
    x, y, c, _ = coords()
    place = (x, y, c)
    sibling = at(x, y, 1 - c)
    sends = []

    def spot(o, h, step, core):
        return by_slot[o][h].at[place[1 - o], ((place[o] + step) % SIDE) * NC + (c + core) % NC]

    owned = []
    for h in parts:
        for step in (2, 1, 3, 0):
            for o in range(2):
                for core in range(NC):
                    q, lane = (place[o] + step) % SIDE, (c + core) % NC
                    source = update.at[
                        pl.ds(pl.multiple_of((o * SIDE + q) * group + h * tall, tall), tall),
                        pl.ds(pl.multiple_of(lane * half, half), half),
                    ]
                    if step == 0 and core == 0:
                        copy = pltpu.make_async_copy(source, spot(o, h, 0, 0), own_sem.at[o, h])
                        copy.start()
                        owned.append(copy)
                    else:
                        index = (o, h, step * NC + core)
                        device = at(q, y, lane) if o == 0 else at(x, q, lane)
                        copy = remote(source, spot(o, h, 0, 0), send1.at[index], recv1.at[index], device)
                        copy.start()
                        sends.append(copy)

    slot_sets = ((1, pl.ds(0, SIDE)), (3, pl.ds(SIDE, SIDE)))
    ring2 = [
        [RingGather(1 - o, place[1 - o], place, by_slot[o][h], send2.at[o, h], recv2.at[o, h]) for h in parts]
        for o in range(2)
    ]
    for h in parts:
        for o in range(2):
            owned[2 * h + o].wait()
            for step in range(SIDE):
                for core in range(NC):
                    if step or core:
                        index = (o, h, step * NC + core)
                        view = spot(o, h, SIDE - step, NC - core)
                        remote(view, view, send1.at[index], recv1.at[index], sibling).wait_recv()
            ring2[o][h].first([(d, (some,), n) for n, (d, some) in enumerate(slot_sets)])
    for h in parts:
        for o in range(2):
            for n, (d, some) in enumerate(slot_sets):
                ring2[o][h].second(d, (some,), n)

    ring1 = [RingGather(o, place[o], place, by_block.at[o, :, c], send3.at[o], recv3.at[o]) for o in range(2)]

    def view_of(h, some):
        return (some, slice(None), pl.ds(h * tall, tall))

    sets = [(1 + 2 * (a % 2), pl.ds(a, 1)) for a in range(adapters)]

    def pass_on(o, step, h, n):
        view = by_block.at[(o, (place[o] + step) % SIDE, c) + view_of(h, sets[n][1])]
        index = (o, step, adapters * h + n)
        copy = remote(view, view, swap_send.at[index], swap_recv.at[index], sibling)
        copy.start()
        sends.append(copy)

    for h in parts:
        for o in range(2):
            for n, (d, some) in enumerate(slot_sets):
                ring2[o][h].wait_near(d, (some,), n)
                ring2[o][h].wait_opposite((some,), n)
            for a in range(adapters):
                for j in range(per_adapter):
                    s = table[0, a * per_adapter + j]
                    if o == 0:
                        row, item = (s // NC) % NY, (s // (NY * NC)) * NC + s % NC
                    else:
                        row, item = s // (NY * NC), s % (NY * NC)
                    by_block[o, place[o], c, a, j, pl.ds(h * tall, tall)] = by_slot[o][h][row, item]
            ring1[o].first([(d, view_of(h, some), adapters * h + n) for n, (d, some) in enumerate(sets)])
        for o in range(2):
            for n in range(adapters):
                pass_on(o, 0, h, n)
    for h in parts:
        for o in range(2):
            for n, (d, some) in enumerate(sets):
                ring1[o].second(d, view_of(h, some), adapters * h + n)
                pass_on(o, SIDE - d, h, n)
        for o in range(2):
            for n, (d, some) in enumerate(sets):
                ring1[o].wait_near(d, view_of(h, some), adapters * h + n)
                pass_on(o, d, h, n)
    for h in parts:
        for o in range(2):
            for n, (d, some) in enumerate(sets):
                ring1[o].wait_opposite(view_of(h, some), adapters * h + n)
                pass_on(o, 2, h, n)
    for o in range(2):
        for step in range(SIDE):
            for h in parts:
                for n in range(adapters):
                    view = by_block.at[(o, (place[o] + step) % SIDE, 1 - c) + view_of(h, sets[n][1])]
                    index = (o, step, adapters * h + n)
                    remote(view, view, swap_send.at[index], swap_recv.at[index], sibling).wait_recv()
    return sends + [copy for ring in ring1 + ring2[0] + ring2[1] for copy in ring.started]


REDUCE, PRECONDITION = 34, 17


def step_kernel(
    scale, columns, lefts, projs, table, groups, left_stat, right_stat, left_root, right_root,
    new_left, new_right, root_left, root_right, parts, groups_in, load_sem, *scratch,
):
    for_reduce, rest = scratch[:REDUCE], scratch[REDUCE:]
    (old_left, old_right, old_root_left, old_root_right, update), rest = rest[:5], rest[5:]
    for_roots, for_gather = rest[:12], rest[12:]
    table_in, grad = for_reduce[2], for_reduce[15]
    moves = [(groups, groups_in)]
    for source, dest in (
        (left_stat, old_left), (right_stat, old_right), (left_root, old_root_left), (right_root, old_root_right)
    ):
        size = dest.shape[0] // 2
        moves += [(source.at[0, 0, pl.ds(low, size)], dest.at[pl.ds(low, size)]) for low in (0, size)]
    loads = [pltpu.make_async_copy(source, dest, load_sem.at[n]) for n, (source, dest) in enumerate(moves)]
    started = reduce(scale, columns, lefts, projs, table, loads, *for_reduce)
    precondition(
        loads, table_in, groups_in, grad, old_left, old_right, old_root_left, old_root_right,
        new_left, new_right, root_left, root_right, update, *for_roots,
    )
    started += gather(table_in, update, parts, *for_gather)
    for copy in started:
        copy.wait_send()


def whole_step(columns, lefts, projs, table, groups, left_stats, right_stats, left_roots, right_roots, scale):
    adapters, tokens, width = columns.shape
    rank = projs.shape[2]
    per_adapter = width // BW
    count = adapters * per_adapter
    half, group, pair = BW // NC, rank // (2 * SIDE), SIDE * NC
    tall = group // 2
    dma = lambda *shape: pltpu.SemaphoreType.DMA(shape)
    vmem = lambda *shape, kind=BF16: pltpu.VMEM(shape, kind)
    for_reduce = [
        vmem(*lefts.shape),
        vmem(*projs.shape),
        pltpu.SMEM(table.shape, jnp.int32),
        vmem(per_adapter, adapters, NC * tokens, half),
        vmem(NZ - 1, rank, tokens),
        vmem(NZ - 1, rank, tokens),
        vmem(adapters, NC, rank, tokens),
        vmem(2, SIDE, 2, count, tall, half),
        vmem(2, 2, count, tall, half),
        vmem(2, 2, 2, count, tall, half),
        vmem(2, count + 1, 2, tall, half),
        vmem(2, SIDE, 2, pair, tall, half),
        vmem(2, 2, pair, tall, half),
        vmem(2, 2, 2, pair, tall, half),
        vmem(2, pair, group, half),
        vmem(rank, BW),
        pltpu.SMEM((NX * NY * NC,), jnp.int32),
        dma(3),
        dma(per_adapter),
        dma(per_adapter),
        dma(per_adapter),
        dma(NZ - 1),
        dma(NZ - 1),
        dma(NZ),
        dma(NZ),
        dma(adapters),
        dma(adapters),
        dma(2, 4 * adapters, 3),
        dma(2, 4 * adapters, 3),
        dma(2, 4, 3),
        dma(2, 4, 3),
        dma(2, pair),
        dma(2, pair),
        dma(2),
    ]
    for_roots = [
        vmem(rank, rank, kind=F32),
        vmem(BW, BW, kind=F32),
        vmem(rank, rank),
        vmem(BW, BW),
        vmem(rank, BW),
    ]
    for_roots += [vmem(rank, rank)] * 6 + [vmem(BW, BW)] * 6
    for_gather = [vmem(SIDE, pair, tall, half)] * 4
    for_gather += [
        dma(2, 2, pair),
        dma(2, 2, pair),
        dma(2, 2, 2, 3),
        dma(2, 2, 2, 3),
        dma(2, 2 * adapters, 3),
        dma(2, 2 * adapters, 3),
        dma(2, SIDE, 2 * adapters),
        dma(2, SIDE, 2 * adapters),
        dma(2, 2),
    ]
    assert len(for_reduce) == REDUCE and len(for_roots) == PRECONDITION
    hbm, in_vmem = pl.BlockSpec(memory_space=pl.ANY), pl.BlockSpec(memory_space=pltpu.VMEM)
    return pl.pallas_call(
        functools.partial(step_kernel, scale),
        out_shape=(
            pltpu.VMEM((rank, rank), F32),
            pltpu.VMEM((BW, BW), F32),
            pltpu.VMEM((rank, rank), BF16),
            pltpu.VMEM((BW, BW), BF16),
            pltpu.VMEM((2, SIDE, NC, adapters, per_adapter, group, half), BF16),
        ),
        in_specs=[hbm] * 9,
        out_specs=(in_vmem,) * 5,
        scratch_shapes=[pltpu.SMEM(groups.shape, jnp.int32), dma(9)] + for_reduce + for_roots + for_gather,
        compiler_params=pltpu.CompilerParams(
            collective_id=0, has_side_effects=True, vmem_limit_bytes=53477376
        ),
        name="whole_step",
    )(columns, lefts, projs, table, groups, left_stats, right_stats, left_roots, right_roots)


def place_kernel(
    new_left, new_right, root_left, root_right, parts,
    new_left_out, new_right_out, root_left_out, root_right_out, out, sem,
):
    per_adapter, group, half = parts.shape[4:]
    moves = []
    for o in range(2):
        for q in range(SIDE):
            for c in range(NC):
                for j in range(per_adapter):
                    rows, lanes = pl.ds((o * SIDE + q) * group, group), pl.ds(j * BW + c * half, half)
                    moves.append((parts.at[o, q, c, :, j], out.at[:, rows, lanes]))
    moves += [
        (new_left, new_left_out.at[0, 0]),
        (new_right, new_right_out.at[0, 0]),
        (root_left, root_left_out.at[0, 0]),
        (root_right, root_right_out.at[0, 0]),
    ]
    copies = [pltpu.make_async_copy(source, dest, sem.at[n]) for n, (source, dest) in enumerate(moves)]
    for copy in copies:
        copy.start()
    for copy in copies:
        copy.wait()


def placed(new_left, new_right, root_left, root_right, parts):
    _, _, _, adapters, per_adapter, group, _ = parts.shape
    stacked = lambda a: jax.ShapeDtypeStruct((1, 1) + a.shape, a.dtype)
    return pl.pallas_call(
        place_kernel,
        out_shape=(
            stacked(new_left), stacked(new_right), stacked(root_left), stacked(root_right),
            jax.ShapeDtypeStruct((adapters, 2 * SIDE * group, per_adapter * BW), BF16),
        ),
        in_specs=[pl.BlockSpec(memory_space=pltpu.VMEM)] * 5,
        out_specs=(pl.BlockSpec(memory_space=pl.ANY),) * 5,
        scratch_shapes=[pltpu.SemaphoreType.DMA((2 * SIDE * NC * per_adapter + 4,))],
        compiler_params=pltpu.CompilerParams(vmem_limit_bytes=16 * 2**20),
        name="placed",
    )(new_left, new_right, root_left, root_right, parts)


def body(
    columns,
    lefts,
    projs,
    slot_table,
    refresh_group,
    left_stats,
    right_stats,
    left_roots,
    right_roots,
):
    total_tokens = lax.axis_size("dp") * columns.shape[1]
    results = whole_step(
        columns, jnp.swapaxes(lefts, 1, 2), projs, slot_table, refresh_group,
        left_stats, right_stats, left_roots, right_roots, 1.0 / math.sqrt(total_tokens),
    )
    return placed(*results)


def solution(mesh):
    shardings = (
        P(None, "dp", "mp"),
        P(None, "dp", "mp"),
        P(None, "mp", None),
        P("mp", None),
        P("mp", None),
        P("mp", "dp", None, None),
        P("mp", "dp", None, None),
        P("mp", "dp", None, None),
        P("mp", "dp", None, None),
    )
    return jax.shard_map(
        body,
        mesh=mesh,
        in_specs=shardings,
        out_specs=(
            P("mp", "dp", None, None),
            P("mp", "dp", None, None),
            P("mp", "dp", None, None),
            P("mp", "dp", None, None),
            P(None, None, "mp"),
        ),
        check_vma=False,
    )
```

```python
import functools
import itertools
import math

import jax
import jax.numpy as jnp
from jax import lax
from jax.experimental import pallas as pl
from jax.experimental.pallas import tpu as pltpu
from jax.sharding import PartitionSpec as P

BW = 768
EPSILON = 1e-06
NX, NY, NC, NZ = 4, 4, 2, 4
SIDE = 4
ORDER = (0, 1, 3, 2)
MESH = pl.DeviceIdType.MESH
F32, BF16 = jnp.float32, jnp.bfloat16


def coords():
    dp = lax.axis_index("dp")
    return dp // (NY * NC), (dp // NC) % NY, dp % NC, lax.axis_index("mp")


def at(x, y, c):
    return {"dp": (x * NY + y) * NC + c}


def along(axis, step, x, y, c):
    return at((x + step) % NX, y, c) if axis == 0 else at(x, (y + step) % NY, c)


def remote(src, dst, send, recv, device):
    return pltpu.make_async_remote_copy(
        src_ref=src, dst_ref=dst, send_sem=send, recv_sem=recv, device_id=device, device_id_type=MESH
    )


def plane_partners(x, y, c):
    partners = [at(x, y, 1 - c)]
    for step in range(1, SIDE):
        for core in range(NC):
            partners.append(at((x + step) % NX, y, (c + core) % NC))
            partners.append(at(x, (y + step) % NY, (c + core) % NC))
    return partners


def greet(partners):
    barrier = pltpu.get_barrier_semaphore()
    for partner in partners:
        pl.semaphore_signal(barrier, inc=1, device_id=partner, device_id_type=MESH)


def await_partners(partners):
    pl.semaphore_wait(pltpu.get_barrier_semaphore(), len(partners))


class Ring:
    def __init__(self, axis, pos, place, send, recv):
        self.axis, self.pos, self.place, self.send, self.recv = axis, pos, place, send, recv
        self.started = []

    def q(self, step):
        return (self.pos + step) % SIDE

    def put(self, src, dst, step, index):
        descriptor = remote(src, dst, self.send.at[index], self.recv.at[index], along(self.axis, step, *self.place))
        descriptor.start()
        self.started.append(descriptor)

    def wait(self, dst, index):
        device = along(self.axis, 1, *self.place)
        remote(dst, dst, self.send.at[index], self.recv.at[index], device).wait_recv()

    def finish(self):
        for descriptor in self.started:
            descriptor.wait_send()


class RingSum(Ring):
    def __init__(self, axis, pos, place, src, far, near, send, recv):
        super().__init__(axis, pos, place, send, recv)
        self.src, self.far, self.near = src, far, near

    def first(self, sets):
        self.send_far(sets)
        self.send_near(sets)

    def send_far(self, sets):
        for d, view, index in sets:
            self.put(self.src.at[(self.q(2),) + view], self.far.at[view], d, (index, 0))

    def send_near(self, sets):
        for d, view, index in sets:
            self.put(self.src.at[(self.q(SIDE - d),) + view], self.near.at[(d // 2,) + view], SIDE - d, (index, 1))

    def wait_far(self, view, index):
        self.wait(self.far.at[view], (index, 0))

    def second(self, d, view, index):
        total = self.src[(self.q(d),) + view].astype(F32) + self.far[view].astype(F32)
        self.src[(self.q(d),) + view] = total.astype(BF16)
        self.put(self.src.at[(self.q(d),) + view], self.near.at[(1 - d // 2,) + view], d, (index, 2))

    def wait_near(self, d, view, index):
        self.wait(self.near.at[(d // 2,) + view], (index, 1))

    def wait_sum(self, d, view, index):
        self.wait(self.near.at[(1 - d // 2,) + view], (index, 2))

    def total(self, view):
        own = self.src[(self.pos,) + view].astype(F32)
        return own + self.near[(0,) + view].astype(F32) + self.near[(1,) + view].astype(F32)


class RingGather(Ring):
    def __init__(self, axis, pos, place, buf, send, recv):
        super().__init__(axis, pos, place, send, recv)
        self.buf = buf

    def at(self, step, view):
        return self.buf.at[(self.q(step),) + view]

    def first(self, sets):
        for d, view, index in sets:
            self.put(self.at(0, view), self.at(0, view), d, (index, 0))
        for d, view, index in sets:
            self.put(self.at(0, view), self.at(0, view), SIDE - d, (index, 1))

    def second(self, d, view, index):
        self.wait(self.at(SIDE - d, view), (index, 0))
        self.put(self.at(SIDE - d, view), self.at(SIDE - d, view), d, (index, 2))

    def wait_near(self, d, view, index):
        self.wait(self.at(d, view), (index, 1))

    def wait_opposite(self, view, index):
        self.wait(self.at(2, view), (index, 2))


def reduce(
    scale, columns, lefts, projs, table, later,
    lefts_in, projs_in, table_in, cols, part, part_in, factors, blocks, far1, near1, summed, slots, far2, near2,
    pieces, grad, block_of,
    in_sem, col_sem, sib_send, sib_recv, part_send, part_recv, fac_send, fac_recv, swap_send, swap_recv,
    send1, recv1, send2, recv2, send3, recv3, own_sem,
):
    adapters, tokens, width = columns.shape
    rank = projs.shape[2]
    per_adapter = width // BW
    half = BW // NC
    group = rank // (2 * SIDE)
    slot_count = NX * NY * NC
    x, y, c, z = coords()
    sibling = at(x, y, 1 - c)
    mine = pl.ds(pl.multiple_of(c * tokens, tokens), tokens)
    theirs = pl.ds(pl.multiple_of((1 - c) * tokens, tokens), tokens)
    partners = plane_partners(x, y, c) + [{"mp": (z + step) % NZ} for step in range(1, NZ)]
    inputs = []
    for source, dest in ((projs, projs_in), (lefts, lefts_in), (table, table_in)):
        copy = pltpu.make_async_copy(source, dest, in_sem.at[len(inputs)])
        copy.start()
        inputs.append(copy)
    greet(partners)
    local, swapped, sends = [], [], []
    for j in range(per_adapter):
        lanes = pl.ds(pl.multiple_of(j * BW + c * half, half), half)
        keep = pltpu.make_async_copy(columns.at[:, :, lanes], cols.at[j, :, mine], col_sem.at[j])
        keep.start()
        local.append(keep)

    def partial(a):
        return lax.dot_general(projs_in[a], lefts_in[a], (((0,), (0,)), ((), ())), preferred_element_type=F32)

    inputs[0].wait()
    inputs[1].wait()
    for step in (2, 1, 3):
        part[step - 1] = partial((z + step) % NZ).astype(BF16)
        if step == 2:
            await_partners(partners)
        copy = remote(
            part.at[step - 1], part_in.at[step - 1], part_send.at[step - 1], part_recv.at[step - 1],
            {"mp": (z + step) % NZ},
        )
        copy.start()
        sends.append(copy)

    for j in range(per_adapter):
        lanes = pl.ds(pl.multiple_of(j * BW + (1 - c) * half, half), half)
        swap = remote(columns.at[:, :, lanes], cols.at[j, :, mine], sib_send.at[j], sib_recv.at[j], sibling)
        swap.start()
        sends.append(swap)
        swapped.append(remote(cols.at[j, :, theirs], cols.at[j, :, theirs], sib_send.at[j], sib_recv.at[j], sibling))

    total = partial(z)
    for step in (1, 3, 2):
        remote(
            part_in.at[step - 1], part_in.at[step - 1], part_send.at[step - 1], part_recv.at[step - 1], sibling
        ).wait_recv()
        total += part_in[step - 1].astype(F32)
    factors[z, c] = total.astype(BF16)

    def factor_view(a, part):
        return factors.at[a, c] if part is None else factors.at[a, c, pl.ds(part * (rank // 2), rank // 2)]

    def send_factor(a, part, step, index):
        view = factor_view(a, part)
        copy = remote(view, view, fac_send.at[index], fac_recv.at[index], {"mp": (z + step) % NZ})
        copy.start()
        sends.append(copy)

    def wait_factor(a, part, index):
        view = factor_view(a, part)
        remote(view, view, fac_send.at[index], fac_recv.at[index], sibling).wait_recv()

    send_factor(z, None, 1, 0)
    send_factor(z, None, 3, 2)

    place = (x, y, c)
    ring1 = [
        RingSum(o, place[o], place, blocks.at[o], far1.at[o], near1.at[o], send1.at[o], recv1.at[o]) for o in range(2)
    ]
    whole = slice(None)
    tall = group // 2
    items, way = [], (1, 3, 1, 3)
    for t, step in enumerate(ORDER):
        a = (z + step) % NZ
        view = factors.at[a, c]
        if step == 1:
            wait_factor(a, None, 2)
            send_factor(a, 1, 3, 3)
        if step == 3:
            wait_factor(a, None, 0)
            send_factor(a, 0, 1, 1)
        if step == 2:
            wait_factor(a, 0, 1)
            wait_factor(a, 1, 3)
        swap = remote(view, view, swap_send.at[t], swap_recv.at[t], sibling)
        swap.start()
        sends.append(swap)
        other = factors.at[a, 1 - c]
        remote(other, other, swap_send.at[t], swap_recv.at[t], sibling).wait_recv()
        if t == 0:
            for j in range(per_adapter):
                local[j].wait()
                swapped[j].wait_recv()
        factor = jnp.concatenate([factors[a, 0], factors[a, 1]], axis=1)

        def block(j, carry):
            product = lax.dot_general(
                factor, cols[j, a], (((1,), (0,)), ((), ())), preferred_element_type=F32
            ).astype(BF16)
            for o in range(2):
                for q in range(SIDE):
                    for h in range(2):
                        low = (o * SIDE + q) * group + h * tall
                        blocks[o, q, h, a * per_adapter + j] = product[low : low + tall]
            return carry

        lax.fori_loop(0, per_adapter, block, 0)
        items.append(pl.ds(a * per_adapter, per_adapter))
        for o in range(2):
            ring1[o].first([(way[t], (whole, items[t]), t)])

    for copy in later:
        copy.start()

    empty = adapters * per_adapter

    def find(s, carry):
        found = jnp.int32(empty)
        for k in range(adapters * per_adapter):
            found = jnp.where(table_in[0, k] == s, jnp.int32(k), found)
        block_of[s] = found
        return carry

    inputs[2].wait()
    lax.fori_loop(0, slot_count, find, 0)

    for o in range(2):
        summed[o, whole, empty] = jnp.zeros((2, tall, half), BF16)
    for t in range(adapters):
        for o in range(2):
            ring1[o].wait_far((whole, items[t]), t)
            ring1[o].second(way[t], (whole, items[t]), t)
    for t in range(adapters):
        for o in range(2):
            ring1[o].wait_near(way[t], (whole, items[t]), t)
            ring1[o].wait_sum(way[t], (whole, items[t]), t)
            summed[o, whole, items[t]] = ring1[o].total((whole, items[t])).astype(BF16)

    ring2 = [
        RingSum(1 - o, place[1 - o], place, slots.at[o], far2.at[o], near2.at[o], send2.at[o], recv2.at[o])
        for o in range(2)
    ]
    sets = [(d, (whole, pl.ds(n * SIDE, SIDE)), n) for n, d in enumerate((1, 3))]
    for step in (2, 1, 3, 0):
        for o in range(2):
            dest = ring2[o].q(step)
            for j in range(SIDE * NC):
                s = (j // NC) * (NY * NC) + dest * NC + j % NC if o == 0 else dest * (NY * NC) + j
                slots[o, dest, whole, j] = summed[o, whole, block_of[s]]
            if step == 2:
                ring2[o].send_far(sets)
    for o in range(2):
        ring2[o].send_near(sets)
    for o in range(2):
        for d, view, n in sets:
            ring2[o].wait_far(view, n)
            ring2[o].second(d, view, n)

    def target(o, step, core):
        return at((x + step) % NX, y, (c + core) % NC) if o == 0 else at(x, (y + step) % NY, (c + core) % NC)

    def spot(o, step, core):
        q, lane = (place[o] + step) % SIDE, (c + core) % NC
        return grad.at[
            pl.ds(pl.multiple_of((o * SIDE + q) * group, group), group), pl.ds(pl.multiple_of(lane * half, half), half)
        ]

    owned = []
    for o in range(2):
        for d, view, n in sets:
            ring2[o].wait_near(d, view, n)
            ring2[o].wait_sum(d, view, n)
        total = ring2[o].total((whole,)) * scale
        for h in range(2):
            pieces[o, :, pl.ds(h * tall, tall)] = total[h].astype(BF16)
        for step in (2, 1, 3, 0):
            for core in range(NC):
                source = pieces.at[o, ((place[o] + step) % SIDE) * NC + (c + core) % NC]
                if step == 0 and core == 0:
                    copy = pltpu.make_async_copy(source, spot(o, 0, 0), own_sem.at[o])
                    copy.start()
                    owned.append(copy)
                else:
                    index = step * NC + core
                    copy = remote(source, spot(o, 0, 0), send3.at[o, index], recv3.at[o, index], target(o, step, core))
                    copy.start()
                    sends.append(copy)
    for o in range(2):
        for step in range(SIDE):
            for core in range(NC):
                if step or core:
                    index = step * NC + core
                    view = spot(o, SIDE - step, NC - core)
                    remote(view, view, send3.at[o, index], recv3.at[o, index], sibling).wait_recv()
    for copy in owned:
        copy.wait()
    return sends + [copy for ring in ring1 + ring2 for copy in ring.started]


def newton_polynomial():
    terms = [0.25 * math.comb(5, i) * 1.25 ** (5 - i) * (-0.25) ** i for i in range(6)]
    terms[0] += 1.25 * 0.25
    return terms


def dot16(a, b):
    return jnp.dot(a, b, preferred_element_type=F32)


def root_steps(stat, square, renew, old, out, n1, n2, n3, u, v, w):
    size = stat.shape[0]
    width = min(size, 256)
    tiles = [pl.ds(low, width) for low in range(0, size, width)]
    inverse = lax.rsqrt(square + EPSILON)
    u1, u2, u3, u4, u5, u6 = newton_polynomial()
    for tile in tiles:
        n1[:, tile] = (stat[:, tile] * inverse).astype(BF16)
    yield
    for tile in tiles:
        n2[:, tile] = dot16(n1[...], n1[:, tile]).astype(BF16)
        yield
    for tile in tiles:
        value = dot16(n1[...], n2[:, tile])
        n3[:, tile] = value.astype(BF16)
        second, first = n2[:, tile].astype(F32), n1[:, tile].astype(F32)
        v[:, tile] = (u4 * first + u5 * second + u6 * value).astype(BF16)
        u[:, tile] = (u1 * first + u2 * second + u3 * value).astype(BF16)
        yield
    for tile in tiles:
        w[:, tile] = (u[:, tile].astype(F32) + dot16(n3[...], v[:, tile])).astype(BF16)
        yield
    for tile in tiles:
        value = w[:, tile]
        n2[:, tile] = (dot16(w[...], value) - 3.125 * value.astype(F32)).astype(BF16)
        yield
    for tile in tiles:
        value = n2[:, tile]
        v[:, tile] = (dot16(n2[...], value) + (2 * 1.5625**2) * value.astype(F32)).astype(BF16)
        n3[:, tile] = (1.5625 * n1[:, tile].astype(F32) - dot16(w[...], n1[:, tile])).astype(BF16)
        yield
    scale = jnp.sqrt(jnp.sqrt(inverse))
    for low, tile in zip(range(0, size, width), tiles):
        value = n3[:, tile]
        last = 1.25 * w[:, tile].astype(F32) + (0.25 * 1.5625**4) * value.astype(F32) + 0.25 * dot16(v[...], value)
        row = lax.broadcasted_iota(jnp.int32, (size, width), 0)
        column = lax.broadcasted_iota(jnp.int32, (size, width), 1)
        eye = jnp.where(row == column + low, jnp.float32(1.25 * 1.5625), jnp.float32(0.0))
        out[:, tile] = jnp.where(renew, (eye - last) * scale, old[:, tile].astype(F32)).astype(BF16)
        yield


def precondition(
    loads, table, groups, grad, old_left, old_right, old_root_left, old_root_right,
    new_left, new_right, root_left, root_right, update, *scratch,
):
    rank, width = grad.shape
    for load in loads:
        load.wait()
    owner = lax.axis_index("dp")
    renew = jnp.int32(0)
    for k in range(table.shape[1]):
        named = jnp.where(table[0, k] == owner, jnp.int32(1), jnp.int32(0))
        renew += named * jnp.where(groups[0, k] == 0, jnp.int32(1), jnp.int32(0))
    renew = renew == 1
    transposed = (((0,), (0,)), ((), ()))
    across = (((1,), (1,)), ((), ()))
    value = grad[...]
    product = lax.dot_general(value, value, across, preferred_element_type=F32)
    fresh = 0.9 * old_left[...] + 0.1 * product
    new_left[...] = fresh
    left_square = jnp.sum(fresh * fresh)
    tile_width = min(width, 256)
    squares = jnp.zeros((1, tile_width), F32)
    for low in range(0, width, tile_width):
        tile = pl.ds(low, tile_width)
        product = lax.dot_general(value, grad[:, tile], transposed, preferred_element_type=F32)
        fresh = 0.9 * old_right[:, tile] + 0.1 * product
        new_right[:, tile] = fresh
        squares += jnp.sum(fresh * fresh, axis=0, keepdims=True)
    right_square = jnp.sum(squares)
    steps = [
        root_steps(new_right, right_square, renew, old_root_right, root_right, *scratch[6:]),
        root_steps(new_left, left_square, renew, old_root_left, root_left, *scratch[:6]),
    ]
    for _ in itertools.zip_longest(*steps):
        pass
    half_product = dot16(root_left[...], grad[...]).astype(BF16)
    direction = dot16(half_product, root_right[...])
    wide = grad[...].astype(F32)
    count = 1.0 / (rank * width)
    ratio = (jnp.sum(wide * wide) * count + EPSILON) / (jnp.sum(direction * direction) * count + EPSILON)
    update[...] = (direction * jnp.sqrt(ratio)).astype(BF16)


def gather(
    table, update, by_block, slots0, slots1,
    send1, recv1, send2, recv2, send3, recv3, swap_send, swap_recv, own_sem,
):
    rank, width = update.shape
    half, group = width // NC, rank // (2 * SIDE)
    adapters, per_adapter = by_block.shape[3:5]
    by_slot = (slots0, slots1)
    x, y, c, _ = coords()
    place = (x, y, c)
    sibling = at(x, y, 1 - c)
    sends = []

    def spot(o, step, core):
        return by_slot[o].at[place[1 - o], ((place[o] + step) % SIDE) * NC + (c + core) % NC]

    owned = []
    for step in (2, 1, 3, 0):
        for o in range(2):
            for core in range(NC):
                q, lane = (place[o] + step) % SIDE, (c + core) % NC
                source = update.at[
                    pl.ds(pl.multiple_of((o * SIDE + q) * group, group), group),
                    pl.ds(pl.multiple_of(lane * half, half), half),
                ]
                if step == 0 and core == 0:
                    copy = pltpu.make_async_copy(source, spot(o, 0, 0), own_sem.at[o])
                    copy.start()
                    owned.append(copy)
                else:
                    index = (o, step * NC + core)
                    device = at(q, y, lane) if o == 0 else at(x, q, lane)
                    copy = remote(source, spot(o, 0, 0), send1.at[index], recv1.at[index], device)
                    copy.start()
                    sends.append(copy)

    slot_sets = [(d, (pl.ds(n * SIDE, SIDE),), n) for n, d in enumerate((1, 3))]
    ring2 = [RingGather(1 - o, place[1 - o], place, by_slot[o], send2.at[o], recv2.at[o]) for o in range(2)]
    for o in range(2):
        owned[o].wait()
        for step in range(SIDE):
            for core in range(NC):
                if step or core:
                    index = (o, step * NC + core)
                    view = spot(o, SIDE - step, NC - core)
                    remote(view, view, send1.at[index], recv1.at[index], sibling).wait_recv()
        ring2[o].first(slot_sets)
    for o in range(2):
        for d, view, n in slot_sets:
            ring2[o].second(d, view, n)

    ring1 = [RingGather(o, place[o], place, by_block.at[o, :, c], send3.at[o], recv3.at[o]) for o in range(2)]
    sets = [(1 + 2 * (a % 2), (pl.ds(a, 1),), a) for a in range(adapters)]

    def pass_on(o, step, a):
        view = by_block.at[o, (place[o] + step) % SIDE, c, pl.ds(a, 1)]
        copy = remote(view, view, swap_send.at[o, step, a], swap_recv.at[o, step, a], sibling)
        copy.start()
        sends.append(copy)

    for o in range(2):
        for d, view, n in slot_sets:
            ring2[o].wait_near(d, view, n)
            ring2[o].wait_opposite(view, n)
    for pair in range(0, adapters, 2):
        for o in range(2):
            for a in (pair, pair + 1):
                for j in range(per_adapter):
                    s = table[0, a * per_adapter + j]
                    if o == 0:
                        row, item = (s // NC) % NY, (s // (NY * NC)) * NC + s % NC
                    else:
                        row, item = s // (NY * NC), s % (NY * NC)
                    by_block[o, place[o], c, a, j] = by_slot[o][row, item]
            ring1[o].first(sets[pair : pair + 2])
    for o in range(2):
        for a in range(adapters):
            pass_on(o, 0, a)
    for d, view, a in sets:
        for o in range(2):
            ring1[o].second(d, view, a)
            pass_on(o, SIDE - d, a)
        for o in range(2):
            ring1[o].wait_near(d, view, a)
            pass_on(o, d, a)
    for _, view, a in sets:
        for o in range(2):
            ring1[o].wait_opposite(view, a)
            pass_on(o, 2, a)
    for o in range(2):
        for step in range(SIDE):
            for a in range(adapters):
                view = by_block.at[o, (place[o] + step) % SIDE, 1 - c, pl.ds(a, 1)]
                remote(view, view, swap_send.at[o, step, a], swap_recv.at[o, step, a], sibling).wait_recv()
    return sends + [copy for ring in ring1 + ring2 for copy in ring.started]


REDUCE, PRECONDITION = 34, 17


def step_kernel(
    scale, columns, lefts, projs, table, groups, left_stat, right_stat, left_root, right_root,
    new_left, new_right, root_left, root_right, parts, groups_in, load_sem, *scratch,
):
    for_reduce, rest = scratch[:REDUCE], scratch[REDUCE:]
    (old_left, old_right, old_root_left, old_root_right, update), rest = rest[:5], rest[5:]
    for_roots, for_gather = rest[:12], rest[12:]
    table_in, grad = for_reduce[2], for_reduce[15]
    moves = [(groups, groups_in)]
    for source, dest in (
        (left_stat, old_left), (right_stat, old_right), (left_root, old_root_left), (right_root, old_root_right)
    ):
        size = dest.shape[0] // 2
        moves += [(source.at[0, 0, pl.ds(low, size)], dest.at[pl.ds(low, size)]) for low in (0, size)]
    loads = [pltpu.make_async_copy(source, dest, load_sem.at[n]) for n, (source, dest) in enumerate(moves)]
    started = reduce(scale, columns, lefts, projs, table, loads, *for_reduce)
    precondition(
        loads, table_in, groups_in, grad, old_left, old_right, old_root_left, old_root_right,
        new_left, new_right, root_left, root_right, update, *for_roots,
    )
    started += gather(table_in, update, parts, *for_gather)
    for copy in started:
        copy.wait_send()


def whole_step(columns, lefts, projs, table, groups, left_stats, right_stats, left_roots, right_roots, scale):
    adapters, tokens, width = columns.shape
    rank = projs.shape[2]
    per_adapter = width // BW
    count = adapters * per_adapter
    half, group, pair = BW // NC, rank // (2 * SIDE), SIDE * NC
    tall = group // 2
    dma = lambda *shape: pltpu.SemaphoreType.DMA(shape)
    vmem = lambda *shape, kind=BF16: pltpu.VMEM(shape, kind)
    for_reduce = [
        vmem(*lefts.shape),
        vmem(*projs.shape),
        pltpu.SMEM(table.shape, jnp.int32),
        vmem(per_adapter, adapters, NC * tokens, half),
        vmem(NZ - 1, rank, tokens),
        vmem(NZ - 1, rank, tokens),
        vmem(adapters, NC, rank, tokens),
        vmem(2, SIDE, 2, count, tall, half),
        vmem(2, 2, count, tall, half),
        vmem(2, 2, 2, count, tall, half),
        vmem(2, 2, count + 1, tall, half),
        vmem(2, SIDE, 2, pair, tall, half),
        vmem(2, 2, pair, tall, half),
        vmem(2, 2, 2, pair, tall, half),
        vmem(2, pair, group, half),
        vmem(rank, BW),
        pltpu.SMEM((NX * NY * NC,), jnp.int32),
        dma(3),
        dma(per_adapter),
        dma(per_adapter),
        dma(per_adapter),
        dma(NZ - 1),
        dma(NZ - 1),
        dma(NZ),
        dma(NZ),
        dma(adapters),
        dma(adapters),
        dma(2, adapters, 3),
        dma(2, adapters, 3),
        dma(2, 2, 3),
        dma(2, 2, 3),
        dma(2, pair),
        dma(2, pair),
        dma(2),
    ]
    for_roots = [
        vmem(rank, rank, kind=F32),
        vmem(BW, BW, kind=F32),
        vmem(rank, rank),
        vmem(BW, BW),
        vmem(rank, BW),
    ]
    for_roots += [vmem(rank, rank)] * 6 + [vmem(BW, BW)] * 6
    for_gather = [vmem(SIDE, pair, group, half)] * 2
    for_gather += [
        dma(2, pair),
        dma(2, pair),
        dma(2, 2, 3),
        dma(2, 2, 3),
        dma(2, adapters, 3),
        dma(2, adapters, 3),
        dma(2, SIDE, adapters),
        dma(2, SIDE, adapters),
        dma(2),
    ]
    assert len(for_reduce) == REDUCE and len(for_roots) == PRECONDITION
    hbm, in_vmem = pl.BlockSpec(memory_space=pl.ANY), pl.BlockSpec(memory_space=pltpu.VMEM)
    return pl.pallas_call(
        functools.partial(step_kernel, scale),
        out_shape=(
            pltpu.VMEM((rank, rank), F32),
            pltpu.VMEM((BW, BW), F32),
            pltpu.VMEM((rank, rank), BF16),
            pltpu.VMEM((BW, BW), BF16),
            pltpu.VMEM((2, SIDE, NC, adapters, per_adapter, group, half), BF16),
        ),
        in_specs=[hbm] * 9,
        out_specs=(in_vmem,) * 5,
        scratch_shapes=[pltpu.SMEM(groups.shape, jnp.int32), dma(9)] + for_reduce + for_roots + for_gather,
        compiler_params=pltpu.CompilerParams(
            collective_id=0, has_side_effects=True, vmem_limit_bytes=53477376
        ),
        name="whole_step",
    )(columns, lefts, projs, table, groups, left_stats, right_stats, left_roots, right_roots)


def place_kernel(
    new_left, new_right, root_left, root_right, parts,
    new_left_out, new_right_out, root_left_out, root_right_out, out, sem,
):
    per_adapter, group, half = parts.shape[4:]
    moves = []
    for o in range(2):
        for q in range(SIDE):
            for c in range(NC):
                for j in range(per_adapter):
                    rows, lanes = pl.ds((o * SIDE + q) * group, group), pl.ds(j * BW + c * half, half)
                    moves.append((parts.at[o, q, c, :, j], out.at[:, rows, lanes]))
    moves += [
        (new_left, new_left_out.at[0, 0]),
        (new_right, new_right_out.at[0, 0]),
        (root_left, root_left_out.at[0, 0]),
        (root_right, root_right_out.at[0, 0]),
    ]
    copies = [pltpu.make_async_copy(source, dest, sem.at[n]) for n, (source, dest) in enumerate(moves)]
    for copy in copies:
        copy.start()
    for copy in copies:
        copy.wait()


def placed(new_left, new_right, root_left, root_right, parts):
    _, _, _, adapters, per_adapter, group, _ = parts.shape
    stacked = lambda a: jax.ShapeDtypeStruct((1, 1) + a.shape, a.dtype)
    return pl.pallas_call(
        place_kernel,
        out_shape=(
            stacked(new_left), stacked(new_right), stacked(root_left), stacked(root_right),
            jax.ShapeDtypeStruct((adapters, 2 * SIDE * group, per_adapter * BW), BF16),
        ),
        in_specs=[pl.BlockSpec(memory_space=pltpu.VMEM)] * 5,
        out_specs=(pl.BlockSpec(memory_space=pl.ANY),) * 5,
        scratch_shapes=[pltpu.SemaphoreType.DMA((2 * SIDE * NC * per_adapter + 4,))],
        compiler_params=pltpu.CompilerParams(vmem_limit_bytes=16 * 2**20),
        name="placed",
    )(new_left, new_right, root_left, root_right, parts)


def body(
    columns,
    lefts,
    projs,
    slot_table,
    refresh_group,
    left_stats,
    right_stats,
    left_roots,
    right_roots,
):
    total_tokens = lax.axis_size("dp") * columns.shape[1]
    results = whole_step(
        columns, jnp.swapaxes(lefts, 1, 2), projs, slot_table, refresh_group,
        left_stats, right_stats, left_roots, right_roots, 1.0 / math.sqrt(total_tokens),
    )
    return placed(*results)


def solution(mesh):
    shardings = (
        P(None, "dp", "mp"),
        P(None, "dp", "mp"),
        P(None, "mp", None),
        P("mp", None),
        P("mp", None),
        P("mp", "dp", None, None),
        P("mp", "dp", None, None),
        P("mp", "dp", None, None),
        P("mp", "dp", None, None),
    )
    return jax.shard_map(
        body,
        mesh=mesh,
        in_specs=shardings,
        out_specs=(
            P("mp", "dp", None, None),
            P("mp", "dp", None, None),
            P("mp", "dp", None, None),
            P("mp", "dp", None, None),
            P(None, None, "mp"),
        ),
        check_vma=False,
    )
```

```python
import functools
import itertools
import math

import jax
import jax.numpy as jnp
from jax import lax
from jax.experimental import pallas as pl
from jax.experimental.pallas import tpu as pltpu
from jax.sharding import PartitionSpec as P

BW = 768
EPSILON = 1e-06
NX, NY, NC, NZ = 4, 4, 2, 4
SIDE = 4
ORDER = (0, 1, 3, 2)
MESH = pl.DeviceIdType.MESH
F32, BF16 = jnp.float32, jnp.bfloat16


def coords():
    dp = lax.axis_index("dp")
    return dp // (NY * NC), (dp // NC) % NY, dp % NC, lax.axis_index("mp")


def at(x, y, c):
    return {"dp": (x * NY + y) * NC + c}


def along(axis, step, x, y, c):
    return at((x + step) % NX, y, c) if axis == 0 else at(x, (y + step) % NY, c)


def remote(src, dst, send, recv, device):
    return pltpu.make_async_remote_copy(
        src_ref=src, dst_ref=dst, send_sem=send, recv_sem=recv, device_id=device, device_id_type=MESH
    )


def plane_partners(x, y, c):
    partners = [at(x, y, 1 - c)]
    for step in range(1, SIDE):
        for core in range(NC):
            partners.append(at((x + step) % NX, y, (c + core) % NC))
            partners.append(at(x, (y + step) % NY, (c + core) % NC))
    return partners


def greet(partners):
    barrier = pltpu.get_barrier_semaphore()
    for partner in partners:
        pl.semaphore_signal(barrier, inc=1, device_id=partner, device_id_type=MESH)


def await_partners(partners):
    pl.semaphore_wait(pltpu.get_barrier_semaphore(), len(partners))


class Ring:
    def __init__(self, axis, pos, place, send, recv):
        self.axis, self.pos, self.place, self.send, self.recv = axis, pos, place, send, recv
        self.started = []

    def q(self, step):
        return (self.pos + step) % SIDE

    def put(self, src, dst, step, index):
        descriptor = remote(src, dst, self.send.at[index], self.recv.at[index], along(self.axis, step, *self.place))
        descriptor.start()
        self.started.append(descriptor)

    def wait(self, dst, index):
        device = along(self.axis, 1, *self.place)
        remote(dst, dst, self.send.at[index], self.recv.at[index], device).wait_recv()

    def finish(self):
        for descriptor in self.started:
            descriptor.wait_send()


class RingSum(Ring):
    def __init__(self, axis, pos, place, src, far, near, send, recv):
        super().__init__(axis, pos, place, send, recv)
        self.src, self.far, self.near = src, far, near

    def first(self, sets):
        self.send_far(sets)
        self.send_near(sets)

    def send_far(self, sets):
        for d, view, index in sets:
            self.put(self.src.at[(self.q(2),) + view], self.far.at[view], d, (index, 0))

    def send_near(self, sets):
        for d, view, index in sets:
            self.put(self.src.at[(self.q(SIDE - d),) + view], self.near.at[(d // 2,) + view], SIDE - d, (index, 1))

    def wait_far(self, view, index):
        self.wait(self.far.at[view], (index, 0))

    def second(self, d, view, index):
        total = self.src[(self.q(d),) + view].astype(F32) + self.far[view].astype(F32)
        self.src[(self.q(d),) + view] = total.astype(BF16)
        self.put(self.src.at[(self.q(d),) + view], self.near.at[(1 - d // 2,) + view], d, (index, 2))

    def wait_near(self, d, view, index):
        self.wait(self.near.at[(d // 2,) + view], (index, 1))

    def wait_sum(self, d, view, index):
        self.wait(self.near.at[(1 - d // 2,) + view], (index, 2))

    def total(self, view):
        own = self.src[(self.pos,) + view].astype(F32)
        return own + self.near[(0,) + view].astype(F32) + self.near[(1,) + view].astype(F32)


class RingGather(Ring):
    def __init__(self, axis, pos, place, buf, send, recv):
        super().__init__(axis, pos, place, send, recv)
        self.buf = buf

    def at(self, step, view):
        return self.buf.at[(self.q(step),) + view]

    def first(self, sets):
        for d, view, index in sets:
            self.put(self.at(0, view), self.at(0, view), d, (index, 0))
        for d, view, index in sets:
            self.put(self.at(0, view), self.at(0, view), SIDE - d, (index, 1))

    def second(self, d, view, index):
        self.wait(self.at(SIDE - d, view), (index, 0))
        self.put(self.at(SIDE - d, view), self.at(SIDE - d, view), d, (index, 2))

    def wait_near(self, d, view, index):
        self.wait(self.at(d, view), (index, 1))

    def wait_opposite(self, view, index):
        self.wait(self.at(2, view), (index, 2))


def reduce(
    scale, columns, lefts, projs, table, later,
    lefts_in, projs_in, table_in, cols, part, part_in, factors, blocks, far1, near1, summed, slots, far2, near2,
    pieces, grad, block_of,
    in_sem, col_sem, sib_send, sib_recv, part_send, part_recv, fac_send, fac_recv, swap_send, swap_recv,
    send1, recv1, send2, recv2, send3, recv3, own_sem,
):
    adapters, tokens, width = columns.shape
    rank = projs.shape[2]
    per_adapter = width // BW
    half = BW // NC
    group = rank // (2 * SIDE)
    slot_count = NX * NY * NC
    x, y, c, z = coords()
    sibling = at(x, y, 1 - c)
    mine = pl.ds(pl.multiple_of(c * tokens, tokens), tokens)
    theirs = pl.ds(pl.multiple_of((1 - c) * tokens, tokens), tokens)
    partners = plane_partners(x, y, c) + [{"mp": (z + step) % NZ} for step in range(1, NZ)]
    inputs = []
    for n, step in enumerate((2, 1, 3, 0)):
        a = (z + step) % NZ
        inputs.append(pltpu.make_async_copy(projs.at[a], projs_in.at[a], in_sem.at[2 * n]))
        inputs.append(pltpu.make_async_copy(lefts.at[a], lefts_in.at[a], in_sem.at[2 * n + 1]))
    inputs.append(pltpu.make_async_copy(table, table_in, in_sem.at[2 * NZ]))
    for copy in inputs[:2]:
        copy.start()
    greet(partners)
    for copy in inputs[2:]:
        copy.start()
    local, swapped, sends = [], [], []
    for j in range(per_adapter):
        lanes = pl.ds(pl.multiple_of(j * BW + c * half, half), half)
        keep = pltpu.make_async_copy(columns.at[:, :, lanes], cols.at[j, :, mine], col_sem.at[j])
        keep.start()
        local.append(keep)

    def partial(a):
        return lax.dot_general(projs_in[a], lefts_in[a], (((0,), (0,)), ((), ())), preferred_element_type=F32)

    for n, step in enumerate((2, 1, 3)):
        inputs[2 * n].wait()
        inputs[2 * n + 1].wait()
        part[step - 1] = partial((z + step) % NZ).astype(BF16)
        if step == 2:
            await_partners(partners)
        copy = remote(
            part.at[step - 1], part_in.at[step - 1], part_send.at[step - 1], part_recv.at[step - 1],
            {"mp": (z + step) % NZ},
        )
        copy.start()
        sends.append(copy)

    for j in range(per_adapter):
        lanes = pl.ds(pl.multiple_of(j * BW + (1 - c) * half, half), half)
        swap = remote(columns.at[:, :, lanes], cols.at[j, :, mine], sib_send.at[j], sib_recv.at[j], sibling)
        swap.start()
        sends.append(swap)
        swapped.append(remote(cols.at[j, :, theirs], cols.at[j, :, theirs], sib_send.at[j], sib_recv.at[j], sibling))

    inputs[6].wait()
    inputs[7].wait()
    total = partial(z)
    for step in (1, 3, 2):
        remote(
            part_in.at[step - 1], part_in.at[step - 1], part_send.at[step - 1], part_recv.at[step - 1], sibling
        ).wait_recv()
        total += part_in[step - 1].astype(F32)
    factors[z, c] = total.astype(BF16)

    def factor_view(a, part):
        return factors.at[a, c] if part is None else factors.at[a, c, pl.ds(part * (rank // 2), rank // 2)]

    def send_factor(a, part, step, index):
        view = factor_view(a, part)
        copy = remote(view, view, fac_send.at[index], fac_recv.at[index], {"mp": (z + step) % NZ})
        copy.start()
        sends.append(copy)

    def wait_factor(a, part, index):
        view = factor_view(a, part)
        remote(view, view, fac_send.at[index], fac_recv.at[index], sibling).wait_recv()

    send_factor(z, None, 1, 0)
    send_factor(z, None, 3, 2)

    place = (x, y, c)
    ring1 = [
        RingSum(o, place[o], place, blocks.at[o], far1.at[o], near1.at[o], send1.at[o], recv1.at[o]) for o in range(2)
    ]
    whole = slice(None)
    tall = group // 2
    items, way = [], (1, 3, 1, 3)
    for t, step in enumerate(ORDER):
        a = (z + step) % NZ
        view = factors.at[a, c]
        if step == 1:
            wait_factor(a, None, 2)
            send_factor(a, 1, 3, 3)
        if step == 3:
            wait_factor(a, None, 0)
            send_factor(a, 0, 1, 1)
        if step == 2:
            wait_factor(a, 0, 1)
            wait_factor(a, 1, 3)
        swap = remote(view, view, swap_send.at[t], swap_recv.at[t], sibling)
        swap.start()
        sends.append(swap)
        other = factors.at[a, 1 - c]
        remote(other, other, swap_send.at[t], swap_recv.at[t], sibling).wait_recv()
        if t == 0:
            for j in range(per_adapter):
                local[j].wait()
                swapped[j].wait_recv()
        factor = jnp.concatenate([factors[a, 0], factors[a, 1]], axis=1)

        def block(j, carry):
            product = lax.dot_general(
                factor, cols[j, a], (((1,), (0,)), ((), ())), preferred_element_type=F32
            ).astype(BF16)
            for o in range(2):
                for q in range(SIDE):
                    for h in range(2):
                        low = (o * SIDE + q) * group + h * tall
                        blocks[o, q, h, a * per_adapter + j] = product[low : low + tall]
            return carry

        lax.fori_loop(0, per_adapter, block, 0)
        items.append(pl.ds(a * per_adapter, per_adapter))
        for o in range(2):
            ring1[o].first([(way[t], (whole, items[t]), t)])

    for copy in later:
        copy.start()

    empty = adapters * per_adapter

    def find(s, carry):
        found = jnp.int32(empty)
        for k in range(adapters * per_adapter):
            found = jnp.where(table_in[0, k] == s, jnp.int32(k), found)
        block_of[s] = found
        return carry

    inputs[8].wait()
    lax.fori_loop(0, slot_count, find, 0)

    for o in range(2):
        summed[o, whole, empty] = jnp.zeros((2, tall, half), BF16)
    for t in range(adapters):
        for o in range(2):
            ring1[o].wait_far((whole, items[t]), t)
            ring1[o].second(way[t], (whole, items[t]), t)
    for t in range(adapters):
        for o in range(2):
            ring1[o].wait_near(way[t], (whole, items[t]), t)
            ring1[o].wait_sum(way[t], (whole, items[t]), t)
            summed[o, whole, items[t]] = ring1[o].total((whole, items[t])).astype(BF16)

    ring2 = [
        RingSum(1 - o, place[1 - o], place, slots.at[o], far2.at[o], near2.at[o], send2.at[o], recv2.at[o])
        for o in range(2)
    ]
    sets = [(d, (whole, pl.ds(n * SIDE, SIDE)), n) for n, d in enumerate((1, 3))]
    for step in (2, 1, 3, 0):
        for o in range(2):
            dest = ring2[o].q(step)
            for j in range(SIDE * NC):
                s = (j // NC) * (NY * NC) + dest * NC + j % NC if o == 0 else dest * (NY * NC) + j
                slots[o, dest, whole, j] = summed[o, whole, block_of[s]]
            if step == 2:
                ring2[o].send_far(sets)
    for o in range(2):
        ring2[o].send_near(sets)
    for o in range(2):
        for d, view, n in sets:
            ring2[o].wait_far(view, n)
            ring2[o].second(d, view, n)

    def target(o, step, core):
        return at((x + step) % NX, y, (c + core) % NC) if o == 0 else at(x, (y + step) % NY, (c + core) % NC)

    def spot(o, step, core):
        q, lane = (place[o] + step) % SIDE, (c + core) % NC
        return grad.at[
            pl.ds(pl.multiple_of((o * SIDE + q) * group, group), group), pl.ds(pl.multiple_of(lane * half, half), half)
        ]

    owned = []
    for o in range(2):
        for d, view, n in sets:
            ring2[o].wait_near(d, view, n)
            ring2[o].wait_sum(d, view, n)
        total = ring2[o].total((whole,)) * scale
        for h in range(2):
            pieces[o, :, pl.ds(h * tall, tall)] = total[h].astype(BF16)
        for step in (2, 1, 3, 0):
            for core in range(NC):
                source = pieces.at[o, ((place[o] + step) % SIDE) * NC + (c + core) % NC]
                if step == 0 and core == 0:
                    copy = pltpu.make_async_copy(source, spot(o, 0, 0), own_sem.at[o])
                    copy.start()
                    owned.append(copy)
                else:
                    index = step * NC + core
                    copy = remote(source, spot(o, 0, 0), send3.at[o, index], recv3.at[o, index], target(o, step, core))
                    copy.start()
                    sends.append(copy)
    for o in range(2):
        for step in range(SIDE):
            for core in range(NC):
                if step or core:
                    index = step * NC + core
                    view = spot(o, SIDE - step, NC - core)
                    remote(view, view, send3.at[o, index], recv3.at[o, index], sibling).wait_recv()
    for copy in owned:
        copy.wait()
    return sends + [copy for ring in ring1 + ring2 for copy in ring.started]


def newton_polynomial():
    terms = [0.25 * math.comb(5, i) * 1.25 ** (5 - i) * (-0.25) ** i for i in range(6)]
    terms[0] += 1.25 * 0.25
    return terms


def dot16(a, b):
    return jnp.dot(a, b, preferred_element_type=F32)


def root_steps(stat, square, renew, old, out, n1, n2, n3, u, v, w):
    size = stat.shape[0]
    width = min(size, 256)
    tiles = [pl.ds(low, width) for low in range(0, size, width)]
    inverse = lax.rsqrt(square + EPSILON)
    u1, u2, u3, u4, u5, u6 = newton_polynomial()
    for tile in tiles:
        n1[:, tile] = (stat[:, tile] * inverse).astype(BF16)
    yield
    for tile in tiles:
        n2[:, tile] = dot16(n1[...], n1[:, tile]).astype(BF16)
        yield
    for tile in tiles:
        value = dot16(n1[...], n2[:, tile])
        n3[:, tile] = value.astype(BF16)
        second, first = n2[:, tile].astype(F32), n1[:, tile].astype(F32)
        v[:, tile] = (u4 * first + u5 * second + u6 * value).astype(BF16)
        u[:, tile] = (u1 * first + u2 * second + u3 * value).astype(BF16)
        yield
    for tile in tiles:
        w[:, tile] = (u[:, tile].astype(F32) + dot16(n3[...], v[:, tile])).astype(BF16)
        yield
    for tile in tiles:
        value = w[:, tile]
        n2[:, tile] = (dot16(w[...], value) - 3.125 * value.astype(F32)).astype(BF16)
        yield
    for tile in tiles:
        value = n2[:, tile]
        v[:, tile] = (dot16(n2[...], value) + (2 * 1.5625**2) * value.astype(F32)).astype(BF16)
        n3[:, tile] = (1.5625 * n1[:, tile].astype(F32) - dot16(w[...], n1[:, tile])).astype(BF16)
        yield
    scale = jnp.sqrt(jnp.sqrt(inverse))
    for low, tile in zip(range(0, size, width), tiles):
        value = n3[:, tile]
        last = 1.25 * w[:, tile].astype(F32) + (0.25 * 1.5625**4) * value.astype(F32) + 0.25 * dot16(v[...], value)
        row = lax.broadcasted_iota(jnp.int32, (size, width), 0)
        column = lax.broadcasted_iota(jnp.int32, (size, width), 1)
        eye = jnp.where(row == column + low, jnp.float32(1.25 * 1.5625), jnp.float32(0.0))
        out[:, tile] = jnp.where(renew, (eye - last) * scale, old[:, tile].astype(F32)).astype(BF16)
        yield


def precondition(
    loads, table, groups, grad, old_left, old_right, old_root_left, old_root_right,
    new_left, new_right, root_left, root_right, update, *scratch,
):
    rank, width = grad.shape
    for load in loads:
        load.wait()
    owner = lax.axis_index("dp")
    renew = jnp.int32(0)
    for k in range(table.shape[1]):
        named = jnp.where(table[0, k] == owner, jnp.int32(1), jnp.int32(0))
        renew += named * jnp.where(groups[0, k] == 0, jnp.int32(1), jnp.int32(0))
    renew = renew == 1
    across = (((1,), (1,)), ((), ()))
    value = grad[...]
    turned = value.T
    product = lax.dot_general(value, value, across, preferred_element_type=F32)
    fresh = 0.9 * old_left[...] + 0.1 * product
    new_left[...] = fresh
    left_square = jnp.sum(fresh * fresh)
    tile_width = min(width, 256)
    squares = jnp.zeros((1, tile_width), F32)
    for low in range(0, width, tile_width):
        tile = pl.ds(low, tile_width)
        product = dot16(turned, grad[:, tile])
        fresh = 0.9 * old_right[:, tile] + 0.1 * product
        new_right[:, tile] = fresh
        squares += jnp.sum(fresh * fresh, axis=0, keepdims=True)
    right_square = jnp.sum(squares)
    steps = [
        root_steps(new_right, right_square, renew, old_root_right, root_right, *scratch[6:]),
        root_steps(new_left, left_square, renew, old_root_left, root_left, *scratch[:6]),
    ]
    for _ in itertools.zip_longest(*steps):
        pass
    half_product = dot16(root_left[...], grad[...]).astype(BF16)
    direction = dot16(half_product, root_right[...])
    wide = grad[...].astype(F32)
    count = 1.0 / (rank * width)
    ratio = (jnp.sum(wide * wide) * count + EPSILON) / (jnp.sum(direction * direction) * count + EPSILON)
    update[...] = (direction * jnp.sqrt(ratio)).astype(BF16)


def gather(
    table, update, by_block, slots0, slots1,
    send1, recv1, send2, recv2, send3, recv3, swap_send, swap_recv, own_sem,
):
    rank, width = update.shape
    half, group = width // NC, rank // (2 * SIDE)
    adapters, per_adapter = by_block.shape[3:5]
    by_slot = (slots0, slots1)
    x, y, c, _ = coords()
    place = (x, y, c)
    sibling = at(x, y, 1 - c)
    sends = []

    def spot(o, step, core):
        return by_slot[o].at[place[1 - o], ((place[o] + step) % SIDE) * NC + (c + core) % NC]

    owned = []
    for step in (2, 1, 3, 0):
        for o in range(2):
            for core in range(NC):
                q, lane = (place[o] + step) % SIDE, (c + core) % NC
                source = update.at[
                    pl.ds(pl.multiple_of((o * SIDE + q) * group, group), group),
                    pl.ds(pl.multiple_of(lane * half, half), half),
                ]
                if step == 0 and core == 0:
                    copy = pltpu.make_async_copy(source, spot(o, 0, 0), own_sem.at[o])
                    copy.start()
                    owned.append(copy)
                else:
                    index = (o, step * NC + core)
                    device = at(q, y, lane) if o == 0 else at(x, q, lane)
                    copy = remote(source, spot(o, 0, 0), send1.at[index], recv1.at[index], device)
                    copy.start()
                    sends.append(copy)

    slot_sets = [(d, (pl.ds(n * SIDE, SIDE),), n) for n, d in enumerate((1, 3))]
    ring2 = [RingGather(1 - o, place[1 - o], place, by_slot[o], send2.at[o], recv2.at[o]) for o in range(2)]
    for o in range(2):
        owned[o].wait()
        for step in range(SIDE):
            for core in range(NC):
                if step or core:
                    index = (o, step * NC + core)
                    view = spot(o, SIDE - step, NC - core)
                    remote(view, view, send1.at[index], recv1.at[index], sibling).wait_recv()
        ring2[o].first(slot_sets)
    for o in range(2):
        for d, view, n in slot_sets:
            ring2[o].second(d, view, n)

    ring1 = [RingGather(o, place[o], place, by_block.at[o, :, c], send3.at[o], recv3.at[o]) for o in range(2)]
    sets = [(1 + 2 * (a % 2), (pl.ds(a, 1),), a) for a in range(adapters)]

    def pass_on(o, step, a):
        view = by_block.at[o, (place[o] + step) % SIDE, c, pl.ds(a, 1)]
        copy = remote(view, view, swap_send.at[o, step, a], swap_recv.at[o, step, a], sibling)
        copy.start()
        sends.append(copy)

    for o in range(2):
        for d, view, n in slot_sets:
            ring2[o].wait_near(d, view, n)
            ring2[o].wait_opposite(view, n)
    for pair in range(0, adapters, 2):
        for o in range(2):
            for a in (pair, pair + 1):
                for j in range(per_adapter):
                    s = table[0, a * per_adapter + j]
                    if o == 0:
                        row, item = (s // NC) % NY, (s // (NY * NC)) * NC + s % NC
                    else:
                        row, item = s // (NY * NC), s % (NY * NC)
                    by_block[o, place[o], c, a, j] = by_slot[o][row, item]
            ring1[o].first(sets[pair : pair + 2])
    for o in range(2):
        for a in range(adapters):
            pass_on(o, 0, a)
    for d, view, a in sets:
        for o in range(2):
            ring1[o].second(d, view, a)
            pass_on(o, SIDE - d, a)
        for o in range(2):
            ring1[o].wait_near(d, view, a)
            pass_on(o, d, a)
    for _, view, a in sets:
        for o in range(2):
            ring1[o].wait_opposite(view, a)
            pass_on(o, 2, a)
    for o in range(2):
        for step in range(SIDE):
            for a in range(adapters):
                view = by_block.at[o, (place[o] + step) % SIDE, 1 - c, pl.ds(a, 1)]
                remote(view, view, swap_send.at[o, step, a], swap_recv.at[o, step, a], sibling).wait_recv()
    return sends + [copy for ring in ring1 + ring2 for copy in ring.started]


REDUCE, PRECONDITION = 34, 17


def step_kernel(
    scale, columns, lefts, projs, table, groups, left_stat, right_stat, left_root, right_root,
    new_left, new_right, root_left, root_right, parts, groups_in, load_sem, *scratch,
):
    for_reduce, rest = scratch[:REDUCE], scratch[REDUCE:]
    (old_left, old_right, old_root_left, old_root_right, update), rest = rest[:5], rest[5:]
    for_roots, for_gather = rest[:12], rest[12:]
    table_in, grad = for_reduce[2], for_reduce[15]
    moves = [(groups, groups_in)]
    for source, dest in (
        (left_stat, old_left), (right_stat, old_right), (left_root, old_root_left), (right_root, old_root_right)
    ):
        size = dest.shape[0] // 2
        moves += [(source.at[0, 0, pl.ds(low, size)], dest.at[pl.ds(low, size)]) for low in (0, size)]
    loads = [pltpu.make_async_copy(source, dest, load_sem.at[n]) for n, (source, dest) in enumerate(moves)]
    started = reduce(scale, columns, lefts, projs, table, loads, *for_reduce)
    precondition(
        loads, table_in, groups_in, grad, old_left, old_right, old_root_left, old_root_right,
        new_left, new_right, root_left, root_right, update, *for_roots,
    )
    started += gather(table_in, update, parts, *for_gather)
    for copy in started:
        copy.wait_send()


def whole_step(columns, lefts, projs, table, groups, left_stats, right_stats, left_roots, right_roots, scale):
    adapters, tokens, width = columns.shape
    rank = projs.shape[2]
    per_adapter = width // BW
    count = adapters * per_adapter
    half, group, pair = BW // NC, rank // (2 * SIDE), SIDE * NC
    tall = group // 2
    dma = lambda *shape: pltpu.SemaphoreType.DMA(shape)
    vmem = lambda *shape, kind=BF16: pltpu.VMEM(shape, kind)
    for_reduce = [
        vmem(*lefts.shape),
        vmem(*projs.shape),
        pltpu.SMEM(table.shape, jnp.int32),
        vmem(per_adapter, adapters, NC * tokens, half),
        vmem(NZ - 1, rank, tokens),
        vmem(NZ - 1, rank, tokens),
        vmem(adapters, NC, rank, tokens),
        vmem(2, SIDE, 2, count, tall, half),
        vmem(2, 2, count, tall, half),
        vmem(2, 2, 2, count, tall, half),
        vmem(2, 2, count + 1, tall, half),
        vmem(2, SIDE, 2, pair, tall, half),
        vmem(2, 2, pair, tall, half),
        vmem(2, 2, 2, pair, tall, half),
        vmem(2, pair, group, half),
        vmem(rank, BW),
        pltpu.SMEM((NX * NY * NC,), jnp.int32),
        dma(2 * NZ + 1),
        dma(per_adapter),
        dma(per_adapter),
        dma(per_adapter),
        dma(NZ - 1),
        dma(NZ - 1),
        dma(NZ),
        dma(NZ),
        dma(adapters),
        dma(adapters),
        dma(2, adapters, 3),
        dma(2, adapters, 3),
        dma(2, 2, 3),
        dma(2, 2, 3),
        dma(2, pair),
        dma(2, pair),
        dma(2),
    ]
    for_roots = [
        vmem(rank, rank, kind=F32),
        vmem(BW, BW, kind=F32),
        vmem(rank, rank),
        vmem(BW, BW),
        vmem(rank, BW),
    ]
    for_roots += [vmem(rank, rank)] * 6 + [vmem(BW, BW)] * 6
    for_gather = [vmem(SIDE, pair, group, half)] * 2
    for_gather += [
        dma(2, pair),
        dma(2, pair),
        dma(2, 2, 3),
        dma(2, 2, 3),
        dma(2, adapters, 3),
        dma(2, adapters, 3),
        dma(2, SIDE, adapters),
        dma(2, SIDE, adapters),
        dma(2),
    ]
    assert len(for_reduce) == REDUCE and len(for_roots) == PRECONDITION
    hbm, in_vmem = pl.BlockSpec(memory_space=pl.ANY), pl.BlockSpec(memory_space=pltpu.VMEM)
    return pl.pallas_call(
        functools.partial(step_kernel, scale),
        out_shape=(
            pltpu.VMEM((rank, rank), F32),
            pltpu.VMEM((BW, BW), F32),
            pltpu.VMEM((rank, rank), BF16),
            pltpu.VMEM((BW, BW), BF16),
            pltpu.VMEM((2, SIDE, NC, adapters, per_adapter, group, half), BF16),
        ),
        in_specs=[hbm] * 9,
        out_specs=(in_vmem,) * 5,
        scratch_shapes=[pltpu.SMEM(groups.shape, jnp.int32), dma(9)] + for_reduce + for_roots + for_gather,
        compiler_params=pltpu.CompilerParams(
            collective_id=0, has_side_effects=True, vmem_limit_bytes=53477376
        ),
        name="whole_step",
    )(columns, lefts, projs, table, groups, left_stats, right_stats, left_roots, right_roots)


def place_kernel(
    new_left, new_right, root_left, root_right, parts,
    new_left_out, new_right_out, root_left_out, root_right_out, out, sem,
):
    per_adapter, group, half = parts.shape[4:]
    moves = []
    for o in range(2):
        for q in range(SIDE):
            for c in range(NC):
                for j in range(per_adapter):
                    rows, lanes = pl.ds((o * SIDE + q) * group, group), pl.ds(j * BW + c * half, half)
                    moves.append((parts.at[o, q, c, :, j], out.at[:, rows, lanes]))
    moves += [
        (new_left, new_left_out.at[0, 0]),
        (new_right, new_right_out.at[0, 0]),
        (root_left, root_left_out.at[0, 0]),
        (root_right, root_right_out.at[0, 0]),
    ]
    copies = [pltpu.make_async_copy(source, dest, sem.at[n]) for n, (source, dest) in enumerate(moves)]
    for copy in copies:
        copy.start()
    for copy in copies:
        copy.wait()


def placed(new_left, new_right, root_left, root_right, parts):
    _, _, _, adapters, per_adapter, group, _ = parts.shape
    stacked = lambda a: jax.ShapeDtypeStruct((1, 1) + a.shape, a.dtype)
    return pl.pallas_call(
        place_kernel,
        out_shape=(
            stacked(new_left), stacked(new_right), stacked(root_left), stacked(root_right),
            jax.ShapeDtypeStruct((adapters, 2 * SIDE * group, per_adapter * BW), BF16),
        ),
        in_specs=[pl.BlockSpec(memory_space=pltpu.VMEM)] * 5,
        out_specs=(pl.BlockSpec(memory_space=pl.ANY),) * 5,
        scratch_shapes=[pltpu.SemaphoreType.DMA((2 * SIDE * NC * per_adapter + 4,))],
        compiler_params=pltpu.CompilerParams(vmem_limit_bytes=16 * 2**20),
        name="placed",
    )(new_left, new_right, root_left, root_right, parts)


def body(
    columns,
    lefts,
    projs,
    slot_table,
    refresh_group,
    left_stats,
    right_stats,
    left_roots,
    right_roots,
):
    total_tokens = lax.axis_size("dp") * columns.shape[1]
    results = whole_step(
        columns, jnp.swapaxes(lefts, 1, 2), projs, slot_table, refresh_group,
        left_stats, right_stats, left_roots, right_roots, 1.0 / math.sqrt(total_tokens),
    )
    return placed(*results)


def solution(mesh):
    shardings = (
        P(None, "dp", "mp"),
        P(None, "dp", "mp"),
        P(None, "mp", None),
        P("mp", None),
        P("mp", None),
        P("mp", "dp", None, None),
        P("mp", "dp", None, None),
        P("mp", "dp", None, None),
        P("mp", "dp", None, None),
    )
    return jax.shard_map(
        body,
        mesh=mesh,
        in_specs=shardings,
        out_specs=(
            P("mp", "dp", None, None),
            P("mp", "dp", None, None),
            P("mp", "dp", None, None),
            P("mp", "dp", None, None),
            P(None, None, "mp"),
        ),
        check_vma=False,
    )
```
